32 devices in a mesh: dp: 4 (over z), pipe: 2 (over core), tensor: 4 (over y, x).
Axes of the slice: x: 2, y: 2, z: 4, core: 2. Of those that a mesh axis runs over, the one named last changes fastest.
Arguments:
- tokens: bfloat16 [4, 2, 1280, 768], P('dp', None, 'tensor'), may hold values from -6 to 6
- lengths: int32 [4, 2, 3], P('dp'), may hold values from 1 to 1024, 1280 in all within a row
- qkv_weight: bfloat16 [2, 768, 3, 768], P('pipe', 'dp', None, 'tensor'), may hold values from -0.21875 to 0.21875
- out_weight: bfloat16 [2, 768, 768], P('pipe', 'tensor', 'dp'), may hold values from -0.875 to 0.875
- gate_up_weight: bfloat16 [2, 768, 2, 1152], P('pipe', 'dp', None, 'tensor'), may hold values from -0.21875 to 0.21875
- down_weight: bfloat16 [2, 1152, 768], P('pipe', 'tensor', 'dp'), may hold values from -0.25 to 0.25
- gains: float32 [2, 1536], P('pipe'), may hold values from 0.5 to 1.5
- out_cotangent: bfloat16 [4, 2, 1280, 768], P('dp', None, 'tensor'), may hold values from -6 to 6
Outputs:
- activations: bfloat16 [2, 4, 2, 1280, 768], P('pipe', 'dp', None, 'tensor')
- input_grads: float32 [2, 4, 2, 1280, 768], P('pipe', 'dp', None, 'tensor')
- qkv_grad: float32 [2, 768, 3, 768], P('pipe', 'dp', None, 'tensor')
- out_grad: float32 [2, 768, 768], P('pipe', 'tensor', 'dp')
- gate_up_grad: float32 [2, 768, 2, 1152], P('pipe', 'dp', None, 'tensor')
- down_grad: float32 [2, 1152, 768], P('pipe', 'tensor', 'dp')
- gain_grad: float32 [2, 1536], P('pipe', ('dp', 'tensor'))
The draws below stay inside these ranges and needn't reach their ends.
Inputs may be any that keep to these rules, and one draw needn't show every extreme that they name: `lengths`: each micro-batch holds 3 whole sequences that fill its 1280 tokens in order; the longest has 1024 tokens.
All inputs are finite; a program needn't handle non-finite values.
Results may differ from the reference program's by a relative error of at most 0.029.
Values may be sent and summed in bfloat16 or wider, within the bound.
No kernel may reach another device: no remote copies, remote signals or barrier semaphores. Data moves between devices by JAX's collectives and lax.ppermute only.
A program may use at most 192 MiB of HBM per device.

```python
import math
import jax
import jax.numpy as jnp
import numpy as np
from jax import lax

D = 768
HEAD_DIM = 64
FF = 1152
WINDOW = 128
MB_TOKENS = 1280
LONGEST = 1024
SEQS = 3
MICRO = 2
N_DP = 4


def steps_of(key, shape, cuts, smallest, largest):
    level, own = 1.0, jax.random.fold_in(key, 6)
    for position, shards_of in cuts:
        draws = jnp.exp(jax.random.uniform(jax.random.fold_in(own, position), (shards_of,), jnp.float32, smallest / len(cuts), largest / len(cuts)))
        level = level * jnp.repeat(draws, shape[position] // shards_of).reshape([-1 if axis == position else 1 for axis in range(len(shape))])
    return level


def split_up(number_of, total, most, slope):
    loads = [(1 << 20) // math.isqrt(standing ** slope) + 1 for standing in range(2, number_of + 1)]
    rest, counts = total - most - (number_of - 1), [1] * (number_of - 1)
    while rest > 0:
        movable = [i for i in range(number_of - 1) if counts[i] < most]
        mass, left = sum([loads[i] for i in movable]), rest
        for i in movable:
            addition = min(most - counts[i], max(1, left * loads[i] // mass), rest)
            counts[i] = counts[i] + addition
            rest = rest - addition
    return np.array([most] + counts)


def ragged_sizes(rng, count, total, bound, slope):
    if count == 2:
        one = jax.random.randint(rng, (), max(1, total - bound), min(bound, total - 1) + 1)
        return jnp.stack([one, total - one])
    sizes = jnp.asarray(split_up(count, total, bound, slope), jnp.int32)
    pairs = (count - 1) // 2
    source_of, taker = sizes[1:1 + 2 * pairs:2], sizes[2:2 + 2 * pairs:2]
    room = jnp.minimum(source_of - 1, bound - taker)
    shifted = jax.random.randint(jax.random.fold_in(rng, 1), (pairs,), 0, 1 << 20) % (room + 1)
    sizes = sizes.at[1:1 + 2 * pairs:2].set(source_of - shifted).at[2:2 + 2 * pairs:2].set(taker + shifted)
    return sizes[jax.random.permutation(jax.random.fold_in(rng, 2), count)]


def scatter_about(own_key, dims, scale, limit, shards=(), held_as=jnp.bfloat16):
    drawn = scale * jax.random.normal(own_key, dims, jnp.float32)
    if shards:
        drawn = drawn * steps_of(own_key, dims, shards, -0.22, 0.18)
    return jnp.clip(drawn, -limit, limit).astype(held_as)


def setup_inputs(seed: int = 0) -> dict:
    key_list = jax.random.split(jax.random.key(seed), 9)
    return {
        "tokens": scatter_about(key_list[0], (N_DP, MICRO, MB_TOKENS, D), 1.0, 6.0, ((0, 4), (2, 4))),
        "lengths": jax.vmap(lambda own: ragged_sizes(own, SEQS, MB_TOKENS, LONGEST, 2))(jax.random.split(key_list[1], N_DP * MICRO)).reshape((N_DP, MICRO, SEQS)).astype(jnp.int32),
        "qkv_weight": scatter_about(key_list[2], (2, D, 3, D), D ** -0.5, 0.21875, ((0, 2), (1, 4), (3, 4))),
        "out_weight": scatter_about(key_list[3], (2, D, D), (D // 16) ** -0.5, 0.875, ((0, 2), (1, 4), (2, 4))),
        "gate_up_weight": scatter_about(key_list[4], (2, D, 2, FF), D ** -0.5, 0.21875, ((0, 2), (1, 4), (3, 4))),
        "down_weight": scatter_about(key_list[5], (2, FF, D), (FF // 2) ** -0.5, 0.25, ((0, 2), (1, 4), (2, 4))),
        "gains": jnp.clip(1.0 + 0.1 * jax.random.normal(key_list[6], (2, 2 * D), jnp.float32), 0.5, 1.5),
        "out_cotangent": scatter_about(key_list[7], (N_DP, MICRO, MB_TOKENS, D), 1.0, 6.0, ((0, 4), (2, 4))),
    }


HIGHEST_PREC = lax.Precision.HIGHEST

@jax.custom_vjp
def low(v):
    return lax.optimization_barrier(v.astype(jnp.bfloat16)).astype(jnp.float32)

@jax.custom_vjp
def low_back(v):
    return v

def low_keep(v):
    return (low(v), None)

def low_pass(kept, grad):
    return (grad,)

def back_keep(v):
    return (v, None)

def back_low(kept, grad):
    return (low(grad),)
low.defvjp(low_keep, low_pass)
low_back.defvjp(back_keep, back_low)

def norm_gain(stream, gain_row):
    average = lax.optimization_barrier(jnp.mean(stream, axis=-1, keepdims=True))
    centred = stream - average
    spread = lax.optimization_barrier(jnp.mean(centred * centred, axis=-1, keepdims=True))
    return centred * lax.rsqrt(spread + 1e-05) * gain_row

def frequencies(theta_base, half_dim):
    return theta_base ** (-(jnp.arange(half_dim, dtype=jnp.float32) * 2.0) / (2.0 * half_dim))

def layout(seq_lengths, full_rows):
    seq_ends = jnp.cumsum(seq_lengths).astype(jnp.int32)
    seq_starts = seq_ends - seq_lengths
    positions = jnp.arange(full_rows, dtype=jnp.int32)
    seq_of = lax.optimization_barrier(jnp.sum((positions[:, None] >= seq_ends[None, :]).astype(jnp.int32), axis=1))
    matches = jnp.arange(seq_lengths.shape[0], dtype=jnp.int32)[None, :] == seq_of[:, None]
    first_row = lax.optimization_barrier(jnp.sum(jnp.where(matches, seq_starts[None, :], 0), axis=1))
    return (seq_of, positions - first_row)

def angles(offset, inv_freq):
    turns = offset.astype(jnp.float32)[:, None] * inv_freq[None, :]
    turns = jnp.concatenate([turns, turns], axis=1)
    return (jnp.cos(turns), jnp.sin(turns))

def rotate(values_in, cosines, sines):
    half_dim = values_in.shape[-1] // 2
    turned = jnp.concatenate([-values_in[..., half_dim:], values_in[..., :half_dim]], axis=-1)
    return values_in * cosines[:, None, :] + turned * sines[:, None, :]

def allowed(seq_of, row_start, block_size, is_local):
    positions = jnp.arange(seq_of.shape[0], dtype=jnp.int32)
    row_ids = row_start + jnp.arange(block_size, dtype=jnp.int32)
    row_seq = lax.dynamic_slice_in_dim(seq_of, row_start, block_size, 0)
    same_seq = row_seq[:, None] == seq_of[None, :]
    near_rows = jnp.abs(row_ids[:, None] - positions[None, :]) <= WINDOW // 2
    return same_seq & (near_rows | jnp.logical_not(is_local))

def block_plan(full_rows):
    blocks = max(1, full_rows // 512)
    return (full_rows // blocks, blocks)

def attention(queries, keys, values, seq_of, is_local):
    full_rows, heads, head_dim = queries.shape
    block_size, blocks = block_plan(full_rows)
    score_scale = head_dim ** (-0.5)
    query_heads = jnp.moveaxis(queries, 1, 0).reshape(heads * blocks, block_size, head_dim)
    key_heads = jnp.moveaxis(keys, 1, 0)
    value_heads = jnp.moveaxis(values, 1, 0)
    head_ids = jnp.repeat(jnp.arange(heads, dtype=jnp.int32), blocks)
    block_ids = jnp.tile(jnp.arange(blocks, dtype=jnp.int32), heads)

    def one_block(operands):
        query_rows, head_id, block_id = operands
        key_rows = lax.dynamic_index_in_dim(key_heads, head_id, 0, keepdims=False)
        value_rows = lax.dynamic_index_in_dim(value_heads, head_id, 0, keepdims=False)
        scores = low_back(score_scale * jnp.dot(query_rows, key_rows.T, precision=HIGHEST_PREC))
        mask_rows = allowed(seq_of, block_id * block_size, block_size, is_local)
        scores = jnp.where(mask_rows, scores, -1e+30)
        probabilities = low(jax.nn.softmax(scores, axis=-1))
        return jnp.dot(probabilities, value_rows, precision=HIGHEST_PREC)
    mixed = lax.map(jax.checkpoint(one_block), (query_heads, head_ids, block_ids))
    mixed = jnp.moveaxis(mixed.reshape(heads, full_rows, head_dim), 0, 1)
    return mixed.reshape(full_rows, heads * head_dim)

def layer(stream, w_qkv, w_out, w_pair, w_down, gain_row, seq_of, cosines, sines, is_local):
    full_rows, model_width = stream.shape
    heads = model_width // HEAD_DIM
    normed_attn = low(norm_gain(stream, gain_row[:model_width]))
    projected = low_back(jnp.einsum('sd,dkf->skf', normed_attn, w_qkv, precision=HIGHEST_PREC))
    queries = low(rotate(projected[:, 0].reshape(full_rows, heads, HEAD_DIM), cosines, sines))
    keys = low(rotate(projected[:, 1].reshape(full_rows, heads, HEAD_DIM), cosines, sines))
    values = low(projected[:, 2].reshape(full_rows, heads, HEAD_DIM))
    mixed = low(low_back(attention(queries, keys, values, seq_of, is_local)))
    resid_mid = stream + low_back(jnp.dot(mixed, w_out, precision=HIGHEST_PREC))
    normed_mlp = low(norm_gain(resid_mid, gain_row[model_width:]))
    gate_up = low_back(jnp.einsum('sd,dkf->skf', normed_mlp, w_pair, precision=HIGHEST_PREC))
    geglu_out = low(jax.nn.gelu(gate_up[:, 0], approximate=False) * gate_up[:, 1])
    return resid_mid + low_back(jnp.dot(geglu_out, w_down, precision=HIGHEST_PREC))

def reference(tokens, lengths, qkv_weight, out_weight, gate_up_weight, down_weight, gains, out_cotangent):
    params = tuple((weight.astype(jnp.float32) for weight in (qkv_weight, out_weight, gate_up_weight, down_weight, gains)))
    micro_total = tokens.shape[0] * tokens.shape[1]
    flat_tokens = tokens.reshape(micro_total, tokens.shape[2], tokens.shape[3])
    flat_lengths = lengths.reshape(micro_total, lengths.shape[2])
    flat_cots = out_cotangent.reshape(micro_total, tokens.shape[2], tokens.shape[3])
    half_dim = HEAD_DIM // 2

    def one_batch(running, operands):
        batch_tokens, seq_lengths, batch_cot = operands
        full_rows = batch_tokens.shape[0]
        seq_of, offset = layout(seq_lengths, full_rows)
        cos_local, sin_local = angles(offset, frequencies(10000.0, half_dim))
        cos_global, sin_global = angles(offset, frequencies(160000.0, half_dim))

        def whole_block(stream, delta, w_qkv, w_out, w_pair, w_down, gain_rows):
            first_out = low(layer(stream, w_qkv[0], w_out[0], w_pair[0], w_down[0], gain_rows[0], seq_of, cos_local, sin_local, True))
            second_out = layer(low_back(first_out + delta), w_qkv[1], w_out[1], w_pair[1], w_down[1], gain_rows[1], seq_of, cos_global, sin_global, False)
            return (second_out, first_out)
        stream = batch_tokens.astype(jnp.float32)
        second_out, pullback, first_out = jax.vjp(whole_block, stream, jnp.zeros_like(stream), *params, has_aux=True)
        grads = pullback(batch_cot.astype(jnp.float32))
        running = tuple((so_far + addend for so_far, addend in zip(running, grads[2:])))
        return (running, (first_out.astype(jnp.bfloat16), second_out.astype(jnp.bfloat16), grads[0], grads[1]))
    initial = tuple((jnp.zeros_like(weight) for weight in params))
    totals, (first_all, second_all, grad_first_in, grad_second_in) = lax.scan(one_batch, initial, (flat_tokens, flat_lengths, flat_cots))
    activations = jnp.stack([first_all.reshape(tokens.shape), second_all.reshape(tokens.shape)])
    input_grads = jnp.stack([grad_first_in.reshape(tokens.shape), grad_second_in.reshape(tokens.shape)])
    return (activations, input_grads, totals[0], totals[1], totals[2], totals[3], totals[4])
```

```python
import functools

import jax
import jax.numpy as jnp
from jax import lax
from jax.experimental import pallas as pl
from jax.experimental.pallas import tpu as pltpu
from jax.sharding import PartitionSpec as P

HEAD_DIM = 64
WINDOW = 128
EPS = 1e-05
BLOCK = 256
BF16 = jnp.bfloat16
F32 = jnp.float32
VMEM_BYTES = 48 * 1024 * 1024


def swap_cores(block):
    return lax.ppermute(block, "pipe", [(0, 1), (1, 0)])


def to_mate(block, bit):
    size = lax.axis_size("tensor")
    return lax.ppermute(block, "tensor", [(i, i ^ bit) for i in range(size)])


def put(buffer, block, index):
    return lax.dynamic_update_slice_in_dim(buffer, block[None], index, 0)


def take(buffer, index):
    return lax.dynamic_index_in_dim(buffer, index, 0, keepdims=False)


def gather_tensor(block):
    me = lax.axis_index("tensor")
    half = block.shape[0] // 2
    one = to_mate(block, 1)
    two = to_mate(block, 2)
    far_head = to_mate(two[:half], 1)
    far_tail = to_mate(one[half:], 2)
    out = jnp.zeros((4,) + block.shape, block.dtype)
    out = put(out, block, me)
    out = put(out, one, me ^ 1)
    out = put(out, two, me ^ 2)
    return put(out, jnp.concatenate([far_head, far_tail], 0), me ^ 3)


def scatter_tensor(blocks):
    me = lax.axis_index("tensor")
    half = blocks.shape[1] // 2
    low = blocks.dtype
    far = take(blocks, me ^ 3)
    head = to_mate(far[:half], 1)
    tail = to_mate(far[half:], 2)
    one = take(blocks, me ^ 1).astype(F32)
    two = take(blocks, me ^ 2).astype(F32)
    one = jnp.concatenate([one[:half], one[half:] + tail.astype(F32)], 0).astype(low)
    two = jnp.concatenate([two[:half] + head.astype(F32), two[half:]], 0).astype(low)
    from_one = to_mate(one, 1)
    from_two = to_mate(two, 2)
    return take(blocks, me).astype(F32) + from_one.astype(F32) + from_two.astype(F32)


def swap_tensor(blocks):
    me = lax.axis_index("tensor")
    out = jnp.zeros_like(blocks)
    out = put(out, take(blocks, me), me)
    for bit in (1, 2, 3):
        out = put(out, to_mate(take(blocks, me ^ bit), bit), me ^ bit)
    return out


def gather_dp(block):
    size = lax.axis_size("dp")
    if size > 4:
        return lax.all_gather(block, "dp", axis=0)
    me = lax.axis_index("dp")
    out = put(jnp.zeros((size,) + block.shape, block.dtype), block, me)
    for step in range(1, size):
        route = [(i, (i + step) % size) for i in range(size)]
        out = put(out, lax.ppermute(block, "dp", route), (me - step) % size)
    return out


def scatter_dp(blocks, low):
    size = lax.axis_size("dp")
    if size > 4:
        return lax.psum_scatter(
            blocks.astype(low), "dp", scatter_dimension=0, tiled=False
        ).astype(F32)
    me = lax.axis_index("dp")
    total = take(blocks, me)
    for step in range(1, size):
        route = [(i, (i + step) % size) for i in range(size)]
        sent = take(blocks, (me + step) % size).astype(low)
        total = total + lax.ppermute(sent, "dp", route).astype(F32)
    return total


def join_halves(mine, other, axis):
    core = lax.axis_index("pipe")
    out = jnp.stack([mine, other], axis)
    return jnp.where(core == 0, out, jnp.stack([other, mine], axis))


def layer_halves(shard):
    core = lax.axis_index("pipe")
    rows = shard.shape[0] // 2
    mine = lax.dynamic_slice_in_dim(shard, core * rows, rows, 0)
    other = lax.dynamic_slice_in_dim(shard, (1 - core) * rows, rows, 0)
    got = swap_cores(other)
    first = jnp.where(core == 0, mine, got)
    second = jnp.where(core == 0, got, mine)
    return first, second


def whole_dp(half):
    gathered = gather_dp(half)
    both = join_halves(gathered, swap_cores(gathered), 1)
    return both.reshape(-1, half.shape[-1])


def whole_all(half):
    gathered = gather_tensor(gather_dp(half))
    both = join_halves(gathered, swap_cores(gathered), 2)
    return both.reshape(4, -1, half.shape[-1])


def half_sums(grad):
    core = lax.axis_index("pipe")
    n = lax.axis_size("dp")
    lead = grad.shape[:-2]
    rows = grad.shape[-2] // (2 * n)
    split = grad.reshape(lead + (n, 2, rows, grad.shape[-1]))
    axis = len(lead) + 1
    mine = lax.dynamic_index_in_dim(split, core, axis, keepdims=False)
    other = lax.dynamic_index_in_dim(split, 1 - core, axis, keepdims=False)
    return mine.astype(F32) + swap_cores(other).astype(F32)


def reduce_dp(grad):
    return scatter_dp(half_sums(grad), BF16)


def reduce_all(grad):
    return scatter_dp(scatter_tensor(half_sums(grad).astype(BF16)), BF16)


def own_layer(first, second):
    core = lax.axis_index("pipe")
    mine = jnp.where(core == 0, first, second)
    other = swap_cores(jnp.where(core == 0, second, first))
    return join_halves(mine, other, 0).reshape(-1, first.shape[-1])


def norm_parts(stream):
    average = jnp.mean(stream, axis=-1, keepdims=True)
    centred = stream - average
    spread = jnp.mean(centred * centred, axis=-1, keepdims=True)
    scale = lax.rsqrt(spread + EPS)
    return centred * scale, scale


def norm_back(grad, unit, scale, gain):
    scaled = grad * gain
    mean_one = jnp.mean(scaled, axis=-1, keepdims=True)
    mean_two = jnp.mean(scaled * unit, axis=-1, keepdims=True)
    return scale * (scaled - mean_one - unit * mean_two)


def dot(left, right, dims):
    return lax.dot_general(left, right, (dims, ((), ())), preferred_element_type=F32)


NN = ((1,), (0,))
NT = ((1,), (1,))
TN = ((0,), (0,))


def window_start(block_id, rows, span):
    if span == rows:
        return 0
    start = jnp.clip(block_id * BLOCK - WINDOW // 2, 0, rows - span)
    return pl.multiple_of(start, WINDOW // 2)


def key_mask(start, span, first, last):
    keys = start + lax.broadcasted_iota(jnp.int32, (span, BLOCK), 0)
    return (keys >= first) & (keys < last)


def attend_kernel(
    span, proj_ref, cos_ref, sin_ref, first_ref, last_ref,
    mixed_ref, queries_ref, keys_ref, values_ref, mass_ref, key_rows, value_rows,
):
    width, rows = queries_ref.shape
    heads = width // HEAD_DIM
    half = HEAD_DIM // 2
    cosines, sines = cos_ref[...], sin_ref[...]
    for head in range(heads):
        low = head * HEAD_DIM
        for part, ref in ((0, queries_ref), (1, keys_ref)):
            upper = proj_ref[part * width + low : part * width + low + half, :]
            lower = proj_ref[part * width + low + half : part * width + low + HEAD_DIM, :]
            turned = jnp.concatenate(
                [upper * cosines - lower * sines, lower * cosines + upper * sines], 0
            )
            ref[low : low + HEAD_DIM, :] = turned.astype(BF16)
            if part == 1:
                key_rows[head] = turned.T.astype(BF16)
        value = proj_ref[2 * width + low : 2 * width + low + HEAD_DIM, :]
        values_ref[low : low + HEAD_DIM, :] = value.astype(BF16)
        value_rows[head] = value.T.astype(BF16)
    mass_ref[...] = jnp.zeros_like(mass_ref)

    def block(block_id, carry):
        start = window_start(block_id, rows, span)
        columns = pl.ds(pl.multiple_of(block_id * BLOCK, BLOCK), BLOCK)
        mask = key_mask(start, span, first_ref[:, columns], last_ref[:, columns])
        outs = []
        for head in range(heads):
            low = head * HEAD_DIM
            query = queries_ref[low : low + HEAD_DIM, columns] * BF16(HEAD_DIM**-0.5)
            scores = dot(key_rows[head, pl.ds(start, span), :], query, NN)
            scores = jnp.where(mask, scores, -1e30)
            top = jnp.max(scores, axis=0, keepdims=True)
            expos = jnp.exp(scores - top)
            total = jnp.sum(expos, axis=0, keepdims=True)
            probs = (expos * (1.0 / total)).astype(BF16)
            if span == rows:
                value = values_ref[low : low + HEAD_DIM, :]
            else:
                value = value_rows[head, pl.ds(start, span), :].T
            outs.append(dot(value, probs, NN))
            mass_ref[head : head + 1, columns] = top + jnp.log(total)
        mixed_ref[columns, :] = jnp.concatenate(outs, 0).T.astype(BF16)
        return carry

    lax.fori_loop(0, rows // BLOCK, block, 0)


def attend(projected, cosines, sines, first, last, is_local):
    width3, rows = projected.shape
    width = width3 // 3
    heads = width // HEAD_DIM
    span = min(rows, BLOCK + WINDOW) if is_local else rows
    shape = jax.ShapeDtypeStruct((width, rows), BF16)
    return pl.pallas_call(
        functools.partial(attend_kernel, span),
        out_shape=(
            jax.ShapeDtypeStruct((rows, width), BF16), shape, shape, shape,
            jax.ShapeDtypeStruct((8, rows), F32),
        ),
        scratch_shapes=[
            pltpu.VMEM((heads, rows, HEAD_DIM), BF16),
            pltpu.VMEM((heads, rows, HEAD_DIM), BF16),
        ],
        compiler_params=pltpu.CompilerParams(vmem_limit_bytes=VMEM_BYTES),
        name="attend_local" if is_local else "attend_global",
    )(projected, cosines, sines, first, last)


def attend_back_kernel(
    span, queries_ref, keys_ref, values_ref, mass_ref, grad_ref,
    cos_ref, sin_ref, first_ref, last_ref, out_ref,
    query_rows, key_rows, value_rows, grad_cols, grad_rows, sum_q, sum_k, sum_v,
):
    width, rows = queries_ref.shape
    heads = width // HEAD_DIM
    half = HEAD_DIM // 2
    scale = HEAD_DIM**-0.5
    grad_cols[...] = grad_ref[...].astype(F32).T.astype(BF16)
    for head in range(heads):
        cut = slice(head * HEAD_DIM, (head + 1) * HEAD_DIM)
        query_rows[head] = (queries_ref[cut, :].astype(F32) * scale).T.astype(BF16)
        key_rows[head] = keys_ref[cut, :].astype(F32).T.astype(BF16)
        value_rows[head] = values_ref[cut, :].astype(F32).T.astype(BF16)
        grad_rows[head] = grad_ref[:, cut]
    sum_k[...] = jnp.zeros_like(sum_k)
    sum_v[...] = jnp.zeros_like(sum_v)

    def block(block_id, carry):
        start = window_start(block_id, rows, span)
        window = pl.ds(start, span)
        columns = pl.ds(pl.multiple_of(block_id * BLOCK, BLOCK), BLOCK)
        mask = key_mask(start, span, first_ref[:, columns], last_ref[:, columns])
        for head in range(heads):
            cut = slice(head * HEAD_DIM, (head + 1) * HEAD_DIM)
            query = queries_ref[cut, columns] * BF16(scale)
            key = key_rows[head, window, :]
            scores = dot(key, query, NN) - mass_ref[head : head + 1, columns]
            probs = jnp.exp(jnp.where(mask, scores, -1e30))
            grad_probs = dot(value_rows[head, window, :], grad_cols[cut, columns], NN)
            weighted = probs * grad_probs
            inner = jnp.sum(weighted, axis=0, keepdims=True)
            grad_scores = (weighted - probs * inner).astype(BF16)
            sum_v[head, window, :] += dot(probs.astype(BF16), grad_rows[head, columns, :], NN)
            sum_k[head, window, :] += dot(grad_scores, query_rows[head, columns, :], NN)
            key_cols = keys_ref[cut, :] if span == rows else key.T
            sum_q[cut, columns] = dot(key_cols, grad_scores, NN)
        return carry

    lax.fori_loop(0, rows // BLOCK, block, 0)
    cosines, sines = cos_ref[...], sin_ref[...]
    for head in range(heads):
        low = head * HEAD_DIM
        turned_q = sum_q[low : low + HEAD_DIM, :] * scale
        for part, turned in ((0, turned_q), (1, sum_k[head].T)):
            upper, lower = turned[:half], turned[half:]
            raw = jnp.concatenate(
                [upper * cosines + lower * sines, lower * cosines - upper * sines], 0
            )
            out_ref[part * width + low : part * width + low + HEAD_DIM, :] = raw.astype(BF16)
        out_ref[2 * width + low : 2 * width + low + HEAD_DIM, :] = sum_v[head].T.astype(BF16)


def attend_back(queries, keys, values, mass, grad, cosines, sines, first, last, is_local):
    width, rows = queries.shape
    heads = width // HEAD_DIM
    span = min(rows, BLOCK + WINDOW) if is_local else rows
    low_rows = pltpu.VMEM((heads, rows, HEAD_DIM), BF16)
    sums = pltpu.VMEM((heads, rows, HEAD_DIM), F32)
    return pl.pallas_call(
        functools.partial(attend_back_kernel, span),
        out_shape=jax.ShapeDtypeStruct((3 * width, rows), BF16),
        scratch_shapes=[
            low_rows, low_rows, low_rows, pltpu.VMEM((width, rows), BF16), low_rows,
            pltpu.VMEM((width, rows), F32), sums, sums,
        ],
        compiler_params=pltpu.CompilerParams(vmem_limit_bytes=VMEM_BYTES),
        name="attend_back_local" if is_local else "attend_back_global",
    )(queries, keys, values, mass, grad, cosines, sines, first, last)


def erf_parts(gate):
    cumulative = 0.5 * (1.0 + lax.erf(gate * 0.7071067811865476))
    density = 0.3989422804014327 * jnp.exp(-0.5 * gate * gate)
    return cumulative, density


def token_kernel(
    pair, mixed_ref, in_ref, mats_ref, down_ref, gain_ref, next_ref,
    mid_ref, out_ref, normed_ref, sums,
):
    parts, _, width = mixed_ref.shape
    units = pair // 2
    sums[...] = in_ref[...].astype(F32)

    def project(part, carry):
        sums[...] += dot(mixed_ref[part], mats_ref[part, :, pair : pair + width], NT)
        return carry

    lax.fori_loop(0, parts, project, 0)
    mid = sums[...]
    mid_ref[...] = mid
    normed = (norm_parts(mid)[0] * gain_ref[...]).astype(BF16)

    def feed(part, carry):
        gate_up = dot(normed, mats_ref[part, :, :pair], NN)
        gate = gate_up[:, :units]
        hidden = (gate * erf_parts(gate)[0] * gate_up[:, units:]).astype(BF16)
        sums[...] += dot(hidden, down_ref[part], NT)
        return carry

    lax.fori_loop(0, parts, feed, 0)
    low = sums[...].astype(BF16)
    out_ref[...] = low
    normed_ref[...] = (norm_parts(low.astype(F32))[0] * next_ref[...]).astype(BF16)


def token_forward(mixed, layer_in, mats, down, gain, next_gain):
    pair = mats.shape[2] - mixed.shape[2]
    shape = layer_in.shape
    return pl.pallas_call(
        functools.partial(token_kernel, pair),
        out_shape=(
            jax.ShapeDtypeStruct(shape, F32),
            jax.ShapeDtypeStruct(shape, BF16),
            jax.ShapeDtypeStruct(shape, BF16),
        ),
        scratch_shapes=[pltpu.VMEM(shape, F32)],
        compiler_params=pltpu.CompilerParams(vmem_limit_bytes=VMEM_BYTES),
        name="token_forward",
    )(mixed, layer_in, mats, down, gain, next_gain)


def token_back_kernel(
    pair, grad_ref, mid_ref, mixed_ref, mats_ref, down_ref, gain_ref,
    mats_grad_ref, down_grad_ref, mixed_grad_ref, grad_mid_ref, gain_grad_ref, sums,
):
    parts, _, width = mixed_ref.shape
    units = pair // 2
    grad = grad_ref[...].astype(F32)
    grad_low = grad.astype(BF16)
    grad_flip = grad.T.astype(BF16)
    unit, scale = norm_parts(mid_ref[...])
    gained = unit * gain_ref[...]
    normed = gained.astype(BF16)
    normed_flip = gained.T.astype(BF16)
    sums[...] = jnp.zeros_like(sums)

    def feed(part, carry):
        gate_up = dot(normed, mats_ref[part, :, :pair], NN)
        gate, up = gate_up[:, :units], gate_up[:, units:]
        cumulative, density = erf_parts(gate)
        gelu = gate * cumulative
        hidden = (gelu * up).astype(BF16)
        grad_hidden = dot(grad_low, down_ref[part], NN)
        grad_gate = grad_hidden * up * (cumulative + gate * density)
        grad_up = grad_hidden * gelu
        grad_pair = jnp.concatenate([grad_gate, grad_up], 1).astype(BF16)
        down_grad_ref[part] = dot(grad_flip, hidden, NN).astype(BF16)
        mats_grad_ref[part, :, :pair] = dot(normed_flip, grad_pair, NN).astype(BF16)
        sums[...] += dot(grad_pair, mats_ref[part, :, :pair], NT)
        return carry

    lax.fori_loop(0, parts, feed, 0)
    grad_normed = sums[...]
    gain_grad_ref[...] = jnp.sum(grad_normed * unit, axis=0, keepdims=True)
    grad_mid = grad + norm_back(grad_normed, unit, scale, gain_ref[...])
    grad_mid_ref[...] = grad_mid
    mid_low = grad_mid.astype(BF16)
    mid_flip = grad_mid.T.astype(BF16)

    def project(part, carry):
        weight = mats_ref[part, :, pair : pair + width]
        mixed_grad_ref[part] = dot(mid_low, weight, NN).astype(BF16)
        mats_grad_ref[part, :, pair : pair + width] = dot(
            mid_flip, mixed_ref[part], NN
        ).astype(BF16)
        return carry

    lax.fori_loop(0, parts, project, 0)


def token_back(grad, mid, mixed, mats, down, gain):
    pair = mats.shape[2] - mixed.shape[2]
    return pl.pallas_call(
        functools.partial(token_back_kernel, pair),
        out_shape=(
            jax.ShapeDtypeStruct(mats.shape, BF16),
            jax.ShapeDtypeStruct(down.shape, BF16),
            jax.ShapeDtypeStruct(mixed.shape, BF16),
            jax.ShapeDtypeStruct(mid.shape, F32),
            jax.ShapeDtypeStruct((1, mid.shape[1]), F32),
        ),
        scratch_shapes=[pltpu.VMEM(mid.shape, F32)],
        compiler_params=pltpu.CompilerParams(vmem_limit_bytes=VMEM_BYTES),
        name="token_back",
    )(grad, mid, mixed, mats, down, gain)


def frequencies(theta_base, half_dim):
    return theta_base ** (-(jnp.arange(half_dim, dtype=F32) * 2.0) / (2.0 * half_dim))


def sequences(seq_lengths, rows):
    seq_ends = jnp.cumsum(seq_lengths)
    positions = jnp.arange(rows, dtype=jnp.int32)
    seq_of = jnp.sum((positions[:, None] >= seq_ends[None, :]).astype(jnp.int32), axis=1)
    matches = jnp.arange(seq_lengths.shape[0], dtype=jnp.int32)[None, :] == seq_of[:, None]
    last = jnp.sum(jnp.where(matches, seq_ends[None, :], 0), axis=1)
    first = jnp.sum(jnp.where(matches, (seq_ends - seq_lengths)[None, :], 0), axis=1)
    return first[None], last[None], positions[None]


def body(
    tokens, lengths, qkv_weight, out_weight, gate_up_weight, down_weight, gains, out_cotangent
):
    core = lax.axis_index("pipe")
    model = tokens.shape[-1]
    local_rows = tokens.shape[2]
    rows = 4 * local_rows
    shard_rows = qkv_weight.shape[1]
    width = qkv_weight.shape[3]
    pair = 2 * gate_up_weight.shape[3]

    stream = take(tokens[0], core)
    cotangent = take(out_cotangent[0], core)
    first, last, positions = sequences(take(lengths[0], core), rows)
    bounds = (
        (jnp.maximum(first, positions - WINDOW // 2), jnp.minimum(last, positions + WINDOW // 2 + 1)),
        (first, last),
    )
    tables = []
    for base in (10000.0, 160000.0):
        turns = frequencies(base, HEAD_DIM // 2)[:, None] * (positions - first).astype(F32)
        tables.append((jnp.cos(turns), jnp.sin(turns)))

    other_gains = swap_cores(gains[0])
    gain_rows = (
        jnp.where(core == 0, gains[0], other_gains)[None],
        jnp.where(core == 0, other_gains, gains[0])[None],
    )

    qkv_halves = layer_halves(qkv_weight[0].reshape(shard_rows, 3 * width))
    mats_halves = layer_halves(
        jnp.concatenate([gate_up_weight[0].reshape(shard_rows, pair), out_weight[0].T], 1)
    )
    down_halves = layer_halves(down_weight[0].T)

    normed = (norm_parts(stream.astype(F32))[0] * gain_rows[0][:, :model]).astype(BF16)
    layer_in = stream
    saved = []
    for layer in (0, 1):
        qkv = whole_dp(qkv_halves[layer])
        normed_full = gather_tensor(normed).reshape(rows, model)
        mats = whole_all(mats_halves[layer])
        down = whole_all(down_halves[layer])
        projected = dot(qkv, normed_full, ((0,), (1,)))
        mixed, queries, keys, values, mass = attend(
            projected, *tables[layer], *bounds[layer], layer == 0
        )
        mixed = swap_tensor(mixed.reshape(4, local_rows, width))
        mid, layer_out, normed = token_forward(
            mixed, layer_in, mats, down, gain_rows[layer][:, model:], gain_rows[1][:, :model]
        )
        saved.append((layer_in, qkv, mats, down, normed_full, queries, keys, values, mass, mixed, mid))
        layer_in = layer_out
        if layer == 0:
            first_out = layer_out
    second_out = layer_in

    grad = cotangent
    reduced = [None, None]
    gain_grads = [None, None]
    input_grads = [None, None]
    for layer in (1, 0):
        stream, qkv, mats, down, normed_full, queries, keys, values, mass, mixed, mid = saved[layer]
        mats_grad, down_grad, mixed_grad, grad_mid, gain_mlp = token_back(
            grad, mid, mixed, mats, down, gain_rows[layer][:, model:]
        )
        grad_full = swap_tensor(mixed_grad).reshape(rows, width)
        grad_projected = attend_back(
            queries, keys, values, mass, grad_full, *tables[layer], *bounds[layer], layer == 0
        )
        qkv_grad = dot(normed_full, grad_projected, ((0,), (1,))).astype(BF16)
        partial_in = dot(grad_projected, qkv, ((0,), (1,))).astype(BF16)
        grad_normed = scatter_tensor(partial_in.reshape(4, local_rows, model))
        unit, scale = norm_parts(stream.astype(F32))
        gain_attn = jnp.sum(grad_normed * unit, axis=0, keepdims=True)
        grad_in = grad_mid + norm_back(grad_normed, unit, scale, gain_rows[layer][:, :model])
        gain_grads[layer] = jnp.concatenate([gain_attn, gain_mlp], 1)
        reduced[layer] = (reduce_all(mats_grad), reduce_all(down_grad), reduce_dp(qkv_grad))
        if layer == 1:
            grad = grad_in.astype(BF16)
            grad_in = grad.astype(F32)
        input_grads[layer] = grad_in

    mats_grad, down_grad, qkv_grad = (own_layer(one, two) for one, two in zip(*reduced))
    n = lax.axis_size("dp")
    gain_mine = jnp.where(core == 0, gain_grads[0], gain_grads[1])
    gain_other = swap_cores(jnp.where(core == 0, gain_grads[1], gain_grads[0]))
    gain_blocks = (gain_mine + gain_other).reshape(n, 4, -1)
    gain_blocks = jnp.moveaxis(gain_blocks, 1, 0)
    gain_part = scatter_dp(jnp.sum(swap_tensor(gain_blocks), axis=0), F32)

    activations = join_halves(
        jnp.where(core == 0, first_out, second_out),
        swap_cores(jnp.where(core == 0, second_out, first_out)),
        0,
    )
    grads_in = join_halves(
        jnp.where(core == 0, input_grads[0], input_grads[1]),
        swap_cores(jnp.where(core == 0, input_grads[1], input_grads[0])),
        0,
    )
    return (
        activations[None, None],
        grads_in[None, None],
        qkv_grad.reshape(qkv_weight.shape),
        mats_grad[:, pair:].T[None],
        mats_grad[:, :pair].reshape(gate_up_weight.shape),
        down_grad.T[None],
        gain_part[None],
    )


def solution(mesh):
    return jax.shard_map(
        body,
        mesh=mesh,
        in_specs=(
            P("dp", None, "tensor", None),
            P("dp", None, None),
            P("pipe", "dp", None, "tensor"),
            P("pipe", "tensor", "dp"),
            P("pipe", "dp", None, "tensor"),
            P("pipe", "tensor", "dp"),
            P("pipe", None),
            P("dp", None, "tensor", None),
        ),
        out_specs=(
            P("pipe", "dp", None, "tensor", None),
            P("pipe", "dp", None, "tensor", None),
            P("pipe", "dp", None, "tensor"),
            P("pipe", "tensor", "dp"),
            P("pipe", "dp", None, "tensor"),
            P("pipe", "tensor", "dp"),
            P("pipe", ("dp", "tensor")),
        ),
        check_vma=False,
    )
```

```python
import functools

import jax
import jax.numpy as jnp
from jax import lax
from jax.experimental import pallas as pl
from jax.experimental.pallas import tpu as pltpu
from jax.sharding import PartitionSpec as P

HEAD_DIM = 64
WINDOW = 128
EPS = 1e-05
BLOCK = 256
BF16 = jnp.bfloat16
F32 = jnp.float32
VMEM_BYTES = 48 * 1024 * 1024


def swap_cores(block):
    return lax.ppermute(block, "pipe", [(0, 1), (1, 0)])


def to_mate(block, bit):
    size = lax.axis_size("tensor")
    return lax.ppermute(block, "tensor", [(i, i ^ bit) for i in range(size)])


def put(buffer, block, index):
    return lax.dynamic_update_slice_in_dim(buffer, block[None], index, 0)


def take(buffer, index):
    return lax.dynamic_index_in_dim(buffer, index, 0, keepdims=False)


def spread_tensor(block):
    half = block.shape[0] // 2
    one = to_mate(block, 1)
    two = to_mate(block, 2)
    return block, one, two, to_mate(two[:half], 1), to_mate(one[half:], 2)


def scatter_tensor(own, one, two, far):
    half = far.shape[0] // 2
    low = far.dtype
    head = to_mate(far[:half], 1)
    tail = to_mate(far[half:], 2)
    one = jnp.concatenate([one[:half], (one[half:].astype(F32) + tail.astype(F32)).astype(low)], 0)
    two = jnp.concatenate([(two[:half].astype(F32) + head.astype(F32)).astype(low), two[half:]], 0)
    from_one = to_mate(one, 1)
    from_two = to_mate(two, 2)
    return own.astype(F32) + from_one.astype(F32) + from_two.astype(F32)


def swap_tensor(blocks):
    return (blocks[0],) + tuple(to_mate(blocks[bit], bit) for bit in (1, 2, 3))


def after(block, *earlier):
    return lax.optimization_barrier((block,) + earlier)[0]


def few_dp():
    return lax.axis_size("dp") <= 4


def ring(step):
    size = lax.axis_size("dp")
    return [(i, (i + step) % size) for i in range(size)]


def gather_dp(block):
    if not few_dp():
        return lax.all_gather(block, "dp", axis=0)
    moved = [lax.ppermute(block, "dp", ring(step)) for step in range(1, lax.axis_size("dp"))]
    return jnp.stack([block] + moved)


def scatter_dp(blocks, low):
    if not few_dp():
        return lax.psum_scatter(
            blocks.astype(low), "dp", scatter_dimension=0, tiled=False
        ).astype(F32)
    total = blocks[0]
    for step in range(1, lax.axis_size("dp")):
        total = total + lax.ppermute(blocks[step].astype(low), "dp", ring(-step)).astype(F32)
    return total


def join_halves(mine, other, axis):
    core = lax.axis_index("pipe")
    out = jnp.stack([mine, other], axis)
    return jnp.where(core == 0, out, jnp.stack([other, mine], axis))


def layer_halves(shard):
    core = lax.axis_index("pipe")
    rows = shard.shape[0] // 2
    mine = lax.dynamic_slice_in_dim(shard, core * rows, rows, 0)
    other = lax.dynamic_slice_in_dim(shard, (1 - core) * rows, rows, 0)
    got = swap_cores(other)
    first = jnp.where(core == 0, mine, got)
    second = jnp.where(core == 0, got, mine)
    return first, second


def placement():
    me = lax.axis_index("tensor")
    if not few_dp():
        return jnp.stack([me, 0, 0]).astype(jnp.int32)
    n = lax.axis_size("dp")
    slots = [(lax.axis_index("dp") - step) % n for step in range(n)]
    return jnp.stack([me, lax.axis_index("pipe")] + slots).astype(jnp.int32)


def halves(gathered):
    other = swap_cores(gathered)
    if few_dp():
        return gathered, other
    both = join_halves(gathered, other, gathered.ndim - 2)
    both = both.reshape(gathered.shape[:-3] + (2, -1, gathered.shape[-1]))
    return both[..., :1, :, :], both[..., 1:, :, :]


def half_sums(mine, other):
    if few_dp():
        return mine, swap_cores(other)
    core = lax.axis_index("pipe")
    n = lax.axis_size("dp")
    full = jnp.concatenate([mine, other], -3)
    full = full.reshape(full.shape[:-3] + (n, 2, -1, full.shape[-1]))
    axis = full.ndim - 3
    kept = lax.dynamic_index_in_dim(full, core, axis, keepdims=False)
    return kept, swap_cores(lax.dynamic_index_in_dim(full, 1 - core, axis, keepdims=False))


def add_low(left, right):
    return (left.astype(F32) + right.astype(F32)).astype(BF16)


def own_layer(first, second):
    core = lax.axis_index("pipe")
    mine = jnp.where(core == 0, first, second)
    other = swap_cores(jnp.where(core == 0, second, first))
    return join_halves(mine, other, 0).reshape(-1, first.shape[-1])


def norm_parts(stream):
    average = jnp.mean(stream, axis=-1, keepdims=True)
    centred = stream - average
    spread = jnp.mean(centred * centred, axis=-1, keepdims=True)
    scale = lax.rsqrt(spread + EPS)
    return centred * scale, scale


def norm_back(grad, unit, scale, gain):
    scaled = grad * gain
    mean_one = jnp.mean(scaled, axis=-1, keepdims=True)
    mean_two = jnp.mean(scaled * unit, axis=-1, keepdims=True)
    return scale * (scaled - mean_one - unit * mean_two)


def dot(left, right, dims):
    return lax.dot_general(left, right, (dims, ((), ())), preferred_element_type=F32)


NN = ((1,), (0,))
NT = ((1,), (1,))
TN = ((0,), (0,))


def cost(micros):
    return pl.CostEstimate(
        flops=int(micros * 1.15e9), bytes_accessed=int(micros * 3.6e6), transcendentals=0
    )


def run_all(copies):
    for copy in copies:
        copy.start()
    for copy in copies:
        copy.wait()


def slot_rows(place_ref, slot, half, rows):
    return pl.ds(pl.multiple_of((place_ref[2 + slot] * 2 + half) * rows, rows), rows)


def half_copies(place_ref, mine_ref, other_ref, whole_ref, sems, outward):
    core = place_ref[1]
    slots, rows = mine_ref.shape[0], mine_ref.shape[1]
    copies = []
    for slot in range(slots):
        for part, (ref, half) in enumerate(((mine_ref, core), (other_ref, 1 - core))):
            inside = whole_ref.at[slot_rows(place_ref, slot, half, rows), :]
            pair = (inside, ref.at[slot]) if outward else (ref.at[slot], inside)
            copies.append(pltpu.make_async_copy(*pair, sems.at[slot, part]))
    return copies


def pack(block):
    half = block.shape[0] // 2
    return jnp.concatenate([block[:half], block[half:]], 1)


def unpack(block):
    half = block.shape[1] // 2
    return jnp.concatenate([block[:, :half], block[:, half:]], 0)


ANYWHERE = pl.BlockSpec(memory_space=pl.ANY)
SCALARS = pl.BlockSpec(memory_space=pltpu.SMEM)
WHOLE = pl.BlockSpec(memory_space=pltpu.VMEM)


def window_start(block_id, rows, span):
    if span == rows:
        return 0
    start = jnp.clip(block_id * BLOCK - WINDOW // 2, 0, rows - span)
    return pl.multiple_of(start, WINDOW // 2)


def key_mask(start, span, first, last):
    keys = start + lax.broadcasted_iota(jnp.int32, (span, BLOCK), 0)
    return (keys >= first) & (keys < last)


def attend_kernel(
    span, place_ref, own_ref, one_ref, two_ref, head_ref, tail_ref, mine_ref, other_ref,
    cos_ref, sin_ref, first_ref, last_ref,
    mixed0_ref, mixed1_ref, mixed2_ref, mixed3_ref, queries_ref, keys_ref, values_ref, mass_ref,
    normed_ref, qkv_ref, key_rows, value_rows, proj, mixed_rows, sems, weight_sems,
):
    width, rows = queries_ref.shape
    heads = width // HEAD_DIM
    half = HEAD_DIM // 2
    local = rows // 4
    me = place_ref[0]
    copies = half_copies(place_ref, mine_ref, other_ref, qkv_ref, weight_sems, False)
    pieces = (
        (own_ref, 0, 0), (one_ref, 1, 0), (two_ref, 2, 0), (head_ref, 3, 0), (tail_ref, 3, local // 2)
    )
    for index, (ref, bit, shift) in enumerate(pieces):
        low = pl.multiple_of((me ^ bit) * local + shift, local // 2)
        target = normed_ref.at[pl.ds(low, ref.shape[0]), :]
        copies.append(pltpu.make_async_copy(ref, target, sems.at[index]))
    run_all(copies)
    proj[...] = dot(qkv_ref[...].T, normed_ref[...], NT)
    cosines, sines = cos_ref[...], sin_ref[...]
    for head in range(heads):
        low = head * HEAD_DIM
        for part, ref in ((0, queries_ref), (1, keys_ref)):
            upper = proj[part * width + low : part * width + low + half, :]
            lower = proj[part * width + low + half : part * width + low + HEAD_DIM, :]
            turned = jnp.concatenate(
                [upper * cosines - lower * sines, lower * cosines + upper * sines], 0
            )
            ref[low : low + HEAD_DIM, :] = turned.astype(BF16)
            if part == 1:
                key_rows[head] = turned.T.astype(BF16)
        value = proj[2 * width + low : 2 * width + low + HEAD_DIM, :]
        values_ref[low : low + HEAD_DIM, :] = value.astype(BF16)
        value_rows[head] = value.T.astype(BF16)
    mass_ref[...] = jnp.zeros_like(mass_ref)

    def block(block_id, carry):
        start = window_start(block_id, rows, span)
        columns = pl.ds(pl.multiple_of(block_id * BLOCK, BLOCK), BLOCK)
        mask = key_mask(start, span, first_ref[:, columns], last_ref[:, columns])
        outs = []
        for head in range(heads):
            low = head * HEAD_DIM
            query = queries_ref[low : low + HEAD_DIM, columns] * BF16(HEAD_DIM**-0.5)
            scores = dot(key_rows[head, pl.ds(start, span), :], query, NN)
            scores = jnp.where(mask, scores, -1e30)
            top = jnp.max(scores, axis=0, keepdims=True)
            expos = jnp.exp(scores - top)
            total = jnp.sum(expos, axis=0, keepdims=True)
            probs = (expos * (1.0 / total)).astype(BF16)
            if span == rows:
                value = values_ref[low : low + HEAD_DIM, :]
            else:
                value = value_rows[head, pl.ds(start, span), :].T
            outs.append(dot(value, probs, NN))
            mass_ref[head : head + 1, columns] = top + jnp.log(total)
        mixed_rows[columns, :] = jnp.concatenate(outs, 0).T.astype(BF16)
        return carry

    lax.fori_loop(0, rows // BLOCK, block, 0)
    for bit, ref in enumerate((mixed0_ref, mixed1_ref, mixed2_ref, mixed3_ref)):
        low = pl.multiple_of((me ^ bit) * local, local)
        ref[...] = pack(mixed_rows[pl.ds(low, local), :])


def attend(place, pieces, mine, other, cosines, sines, first, last, is_local):
    local, model = pieces[0].shape
    rows = 4 * local
    width = mine.shape[2] // 3
    heads = width // HEAD_DIM
    span = min(rows, BLOCK + WINDOW) if is_local else rows
    shape = jax.ShapeDtypeStruct((width, rows), BF16)
    mixed = jax.ShapeDtypeStruct((local // 2, 2 * width), BF16)
    return pl.pallas_call(
        functools.partial(attend_kernel, span),
        out_shape=(
            mixed, mixed, mixed, mixed, shape, shape, shape, jax.ShapeDtypeStruct((8, rows), F32),
            jax.ShapeDtypeStruct((rows, model), BF16),
            jax.ShapeDtypeStruct((model, 3 * width), BF16),
        ),
        in_specs=[SCALARS] + [ANYWHERE] * 7 + [WHOLE] * 4,
        scratch_shapes=[
            pltpu.VMEM((heads, rows, HEAD_DIM), BF16),
            pltpu.VMEM((heads, rows, HEAD_DIM), BF16),
            pltpu.VMEM((3 * width, rows), F32),
            pltpu.VMEM((rows, width), BF16),
            pltpu.SemaphoreType.DMA((5,)),
            pltpu.SemaphoreType.DMA((mine.shape[0], 2)),
        ],
        compiler_params=pltpu.CompilerParams(vmem_limit_bytes=VMEM_BYTES),
        cost_estimate=cost(11 if is_local else 20),
        name="attend_local" if is_local else "attend_global",
    )(place, *pieces, mine, other, cosines, sines, first, last)


def attend_back_kernel(
    span, place_ref, queries_ref, keys_ref, values_ref, mass_ref,
    grad0_ref, grad1_ref, grad2_ref, grad3_ref,
    cos_ref, sin_ref, first_ref, last_ref, qkv_ref,
    part0_ref, part1_ref, part2_ref, part3_ref, out_ref,
    query_rows, key_rows, value_rows, grad_cols, grad_all, grad_rows, sum_q, sum_k, sum_v, flat,
):
    width, rows = queries_ref.shape
    heads = width // HEAD_DIM
    half = HEAD_DIM // 2
    local = rows // 4
    scale = HEAD_DIM**-0.5
    me = place_ref[0]
    for bit, ref in enumerate((grad0_ref, grad1_ref, grad2_ref, grad3_ref)):
        low = pl.multiple_of((me ^ bit) * local, local)
        grad_all[pl.ds(low, local), :] = unpack(ref[...])
    grad_cols[...] = grad_all[...].T
    for head in range(heads):
        cut = slice(head * HEAD_DIM, (head + 1) * HEAD_DIM)
        query_rows[head] = (queries_ref[cut, :] * BF16(scale)).T
        key_rows[head] = keys_ref[cut, :].T
        value_rows[head] = values_ref[cut, :].T
        grad_rows[head] = grad_all[:, cut]
    sum_k[...] = jnp.zeros_like(sum_k)
    sum_v[...] = jnp.zeros_like(sum_v)

    def block(block_id, carry):
        start = window_start(block_id, rows, span)
        window = pl.ds(start, span)
        columns = pl.ds(pl.multiple_of(block_id * BLOCK, BLOCK), BLOCK)
        mask = key_mask(start, span, first_ref[:, columns], last_ref[:, columns])
        for head in range(heads):
            cut = slice(head * HEAD_DIM, (head + 1) * HEAD_DIM)
            query = queries_ref[cut, columns] * BF16(scale)
            key = key_rows[head, window, :]
            scores = dot(key, query, NN) - mass_ref[head : head + 1, columns]
            probs = jnp.exp(jnp.where(mask, scores, -1e30))
            grad_probs = dot(value_rows[head, window, :], grad_cols[cut, columns], NN)
            weighted = probs * grad_probs
            inner = jnp.sum(weighted, axis=0, keepdims=True)
            grad_scores = (weighted - probs * inner).astype(BF16)
            sum_v[head, window, :] += dot(probs.astype(BF16), grad_rows[head, columns, :], NN)
            sum_k[head, window, :] += dot(grad_scores, query_rows[head, columns, :], NN)
            key_cols = keys_ref[cut, :] if span == rows else key.T
            sum_q[cut, columns] = dot(key_cols, grad_scores, NN)
        return carry

    lax.fori_loop(0, rows // BLOCK, block, 0)
    cosines, sines = cos_ref[...], sin_ref[...]
    for head in range(heads):
        low = head * HEAD_DIM
        turned_q = sum_q[low : low + HEAD_DIM, :] * scale
        for part, turned in ((0, turned_q), (1, sum_k[head].T)):
            upper, lower = turned[:half], turned[half:]
            raw = jnp.concatenate(
                [upper * cosines + lower * sines, lower * cosines - upper * sines], 0
            )
            flat[part * width + low : part * width + low + HEAD_DIM, :] = raw.astype(BF16)
        flat[2 * width + low : 2 * width + low + HEAD_DIM, :] = sum_v[head].T.astype(BF16)
    out_ref[...] = flat[...].T
    for bit, ref in enumerate((part0_ref, part1_ref, part2_ref, part3_ref)):
        low = pl.multiple_of((me ^ bit) * local, local)
        ref[...] = dot(out_ref[pl.ds(low, local), :], qkv_ref[...], NT).astype(BF16)


def attend_back(place, queries, keys, values, mass, grads, cosines, sines, first, last, qkv, is_local):
    width, rows = queries.shape
    model = qkv.shape[0]
    heads = width // HEAD_DIM
    span = min(rows, BLOCK + WINDOW) if is_local else rows
    low_rows = pltpu.VMEM((heads, rows, HEAD_DIM), BF16)
    sums = pltpu.VMEM((heads, rows, HEAD_DIM), F32)
    part = jax.ShapeDtypeStruct((rows // 4, model), BF16)
    return pl.pallas_call(
        functools.partial(attend_back_kernel, span),
        out_shape=(part, part, part, part, jax.ShapeDtypeStruct((rows, 3 * width), BF16)),
        in_specs=[SCALARS] + [WHOLE] * 13,
        scratch_shapes=[
            low_rows, low_rows, low_rows, pltpu.VMEM((width, rows), BF16),
            pltpu.VMEM((rows, width), BF16), low_rows,
            pltpu.VMEM((width, rows), F32), sums, sums, pltpu.VMEM((3 * width, rows), BF16),
        ],
        compiler_params=pltpu.CompilerParams(vmem_limit_bytes=VMEM_BYTES),
        cost_estimate=cost(11 if is_local else 21),
        name="attend_back_local" if is_local else "attend_back_global",
    )(place, queries, keys, values, mass, *grads, cosines, sines, first, last, qkv)


def qkv_grad_kernel(place_ref, normed_ref, grad_ref, mine_ref, other_ref, whole, sems):
    whole[...] = dot(normed_ref[...].T, grad_ref[...], NN).astype(BF16)
    run_all(half_copies(place_ref, mine_ref, other_ref, whole, sems, True))


def qkv_grad(place, normed, grad, shape):
    part = jax.ShapeDtypeStruct(shape, BF16)
    return pl.pallas_call(
        qkv_grad_kernel,
        out_shape=(part, part),
        in_specs=[SCALARS, WHOLE, WHOLE],
        out_specs=(ANYWHERE, ANYWHERE),
        scratch_shapes=[
            pltpu.VMEM((normed.shape[1], grad.shape[1]), BF16),
            pltpu.SemaphoreType.DMA((shape[0], 2)),
        ],
        compiler_params=pltpu.CompilerParams(vmem_limit_bytes=VMEM_BYTES),
        cost_estimate=cost(4),
        name="qkv_grad",
    )(place, normed, grad)


def erf_parts(gate):
    cumulative = 0.5 * (1.0 + lax.erf(gate * 0.7071067811865476))
    density = 0.3989422804014327 * jnp.exp(-0.5 * gate * gate)
    return cumulative, density


def token_kernel(
    pair, place_ref, mixed0_ref, mixed1_ref, mixed2_ref, mixed3_ref, in_ref, mine_ref, other_ref,
    gain_ref, next_ref, mid_ref, out_ref, normed_ref, sums, mats, sems,
):
    parts = mats.shape[0]
    width = mixed0_ref.shape[1] // 2
    units = pair // 2
    copies = []
    for part in range(parts):
        copies += half_copies(
            place_ref, mine_ref.at[part], other_ref.at[part], mats.at[part], sems.at[part], False
        )
    run_all(copies)
    mid = in_ref[...].astype(F32)
    for part, ref in enumerate((mixed0_ref, mixed1_ref, mixed2_ref, mixed3_ref)):
        mid += dot(unpack(ref[...]), mats[part, :, pair : pair + width], NT)
    mid_ref[...] = mid
    sums[...] = mid
    normed = (norm_parts(mid)[0] * gain_ref[...]).astype(BF16)

    def feed(part, carry):
        gate_up = dot(normed, mats[part, :, :pair], NN)
        gate = gate_up[:, :units]
        hidden = (gate * erf_parts(gate)[0] * gate_up[:, units:]).astype(BF16)
        sums[...] += dot(hidden, mats[part, :, pair + width :], NT)
        return carry

    lax.fori_loop(0, parts, feed, 0)
    low = sums[...].astype(BF16)
    out_ref[...] = low
    normed_ref[...] = (norm_parts(low.astype(F32))[0] * next_ref[...]).astype(BF16)


def token_forward(place, mixed, layer_in, mine, other, gain, next_gain, pair):
    shape = layer_in.shape
    parts, slots = mine.shape[:2]
    return pl.pallas_call(
        functools.partial(token_kernel, pair),
        out_shape=(
            jax.ShapeDtypeStruct(shape, F32),
            jax.ShapeDtypeStruct(shape, BF16),
            jax.ShapeDtypeStruct(shape, BF16),
        ),
        in_specs=[SCALARS] + [WHOLE] * 5 + [ANYWHERE] * 2 + [WHOLE] * 2,
        scratch_shapes=[
            pltpu.VMEM(shape, F32),
            pltpu.VMEM((parts, shape[1], mine.shape[3]), BF16),
            pltpu.SemaphoreType.DMA((parts, slots, 2)),
        ],
        compiler_params=pltpu.CompilerParams(vmem_limit_bytes=VMEM_BYTES),
        cost_estimate=cost(10),
        name="token_forward",
    )(place, *mixed, layer_in, mine, other, gain, next_gain)


def token_back_kernel(
    pair, place_ref, grad_ref, mid_ref, mixed0_ref, mixed1_ref, mixed2_ref, mixed3_ref,
    mine_ref, other_ref, gain_ref,
    mine_grad_ref, other_grad_ref, mixed_grad0_ref, mixed_grad1_ref, mixed_grad2_ref, mixed_grad3_ref,
    grad_mid_ref, gain_grad_ref, sums, mats, grads, sems,
):
    parts = mats.shape[0]
    width = mixed0_ref.shape[1] // 2
    units = pair // 2
    copies = []
    for part in range(parts):
        copies += half_copies(
            place_ref, mine_ref.at[part], other_ref.at[part], mats.at[part], sems.at[part], False
        )
    run_all(copies)
    grad = grad_ref[...].astype(F32)
    grad_low = grad.astype(BF16)
    grad_flip = grad.T.astype(BF16)
    unit, scale = norm_parts(mid_ref[...])
    gained = unit * gain_ref[...]
    normed = gained.astype(BF16)
    normed_flip = gained.T.astype(BF16)
    sums[...] = jnp.zeros_like(sums)

    def feed(part, carry):
        gate_up = dot(normed, mats[part, :, :pair], NN)
        gate, up = gate_up[:, :units], gate_up[:, units:]
        cumulative, density = erf_parts(gate)
        gelu = gate * cumulative
        hidden = (gelu * up).astype(BF16)
        grad_hidden = dot(grad_low, mats[part, :, pair + width :], NN)
        grad_gate = grad_hidden * up * (cumulative + gate * density)
        grad_up = grad_hidden * gelu
        grad_pair = jnp.concatenate([grad_gate, grad_up], 1).astype(BF16)
        grads[part, :, pair + width :] = dot(grad_flip, hidden, NN).astype(BF16)
        grads[part, :, :pair] = dot(normed_flip, grad_pair, NN).astype(BF16)
        sums[...] += dot(grad_pair, mats[part, :, :pair], NT)
        return carry

    lax.fori_loop(0, parts, feed, 0)
    grad_normed = sums[...]
    gain_grad_ref[...] = jnp.sum(grad_normed * unit, axis=0, keepdims=True)
    grad_mid = grad + norm_back(grad_normed, unit, scale, gain_ref[...])
    grad_mid_ref[...] = grad_mid
    mid_low = grad_mid.astype(BF16)
    mid_flip = grad_mid.T.astype(BF16)
    mixed_refs = (mixed0_ref, mixed1_ref, mixed2_ref, mixed3_ref)
    mixed_grad_refs = (mixed_grad0_ref, mixed_grad1_ref, mixed_grad2_ref, mixed_grad3_ref)
    copies = []
    for part in range(parts):
        weight = mats[part, :, pair : pair + width]
        mixed_grad_refs[part][...] = pack(dot(mid_low, weight, NN).astype(BF16))
        grads[part, :, pair : pair + width] = dot(
            mid_flip, unpack(mixed_refs[part][...]), NN
        ).astype(BF16)
        batch = half_copies(
            place_ref, mine_grad_ref.at[part], other_grad_ref.at[part], grads.at[part],
            sems.at[part], True,
        )
        for copy in batch:
            copy.start()
        copies += batch
    for copy in copies:
        copy.wait()


def token_back(place, grad, mid, mixed, mine, other, gain, pair):
    parts, slots = mine.shape[:2]
    mats = pltpu.VMEM((parts, mid.shape[1], mine.shape[3]), BF16)
    half = jax.ShapeDtypeStruct(mine.shape, BF16)
    mixed_grad = jax.ShapeDtypeStruct(mixed[0].shape, BF16)
    return pl.pallas_call(
        functools.partial(token_back_kernel, pair),
        out_shape=(
            half, half, mixed_grad, mixed_grad, mixed_grad, mixed_grad,
            jax.ShapeDtypeStruct(mid.shape, F32),
            jax.ShapeDtypeStruct((1, mid.shape[1]), F32),
        ),
        in_specs=[SCALARS] + [WHOLE] * 6 + [ANYWHERE] * 2 + [WHOLE],
        out_specs=(ANYWHERE, ANYWHERE) + (WHOLE,) * 6,
        scratch_shapes=[
            pltpu.VMEM(mid.shape, F32), mats, mats, pltpu.SemaphoreType.DMA((parts, slots, 2)),
        ],
        compiler_params=pltpu.CompilerParams(vmem_limit_bytes=VMEM_BYTES),
        cost_estimate=cost(20),
        name="token_back",
    )(place, grad, mid, *mixed, mine, other, gain)


def frequencies(theta_base, half_dim):
    return theta_base ** (-(jnp.arange(half_dim, dtype=F32) * 2.0) / (2.0 * half_dim))


def sequences(seq_lengths, rows):
    seq_ends = jnp.cumsum(seq_lengths)
    positions = jnp.arange(rows, dtype=jnp.int32)
    seq_of = jnp.sum((positions[:, None] >= seq_ends[None, :]).astype(jnp.int32), axis=1)
    matches = jnp.arange(seq_lengths.shape[0], dtype=jnp.int32)[None, :] == seq_of[:, None]
    last = jnp.sum(jnp.where(matches, seq_ends[None, :], 0), axis=1)
    first = jnp.sum(jnp.where(matches, (seq_ends - seq_lengths)[None, :], 0), axis=1)
    return first[None], last[None], positions[None]


def body(
    tokens, lengths, qkv_weight, out_weight, gate_up_weight, down_weight, gains, out_cotangent
):
    core = lax.axis_index("pipe")
    model = tokens.shape[-1]
    local_rows = tokens.shape[2]
    rows = 4 * local_rows
    shard_rows = qkv_weight.shape[1]
    width = qkv_weight.shape[3]
    pair = 2 * gate_up_weight.shape[3]

    stream = take(tokens[0], core)
    cotangent = take(out_cotangent[0], core)
    first, last, positions = sequences(take(lengths[0], core), rows)
    bounds = (
        (jnp.maximum(first, positions - WINDOW // 2), jnp.minimum(last, positions + WINDOW // 2 + 1)),
        (first, last),
    )
    tables = []
    for base in (10000.0, 160000.0):
        turns = frequencies(base, HEAD_DIM // 2)[:, None] * (positions - first).astype(F32)
        tables.append((jnp.cos(turns), jnp.sin(turns)))

    other_gains = swap_cores(gains[0])
    gain_rows = (
        jnp.where(core == 0, gains[0], other_gains)[None],
        jnp.where(core == 0, other_gains, gains[0])[None],
    )
    place = placement()

    normed = (norm_parts(stream.astype(F32))[0] * gain_rows[0][:, :model]).astype(BF16)
    qkv_halves = layer_halves(qkv_weight[0].reshape(shard_rows, 3 * width))
    mats_halves = layer_halves(
        jnp.concatenate(
            [gate_up_weight[0].reshape(shard_rows, pair), out_weight[0].T, down_weight[0].T], 1
        )
    )
    qkv_first = gather_dp(qkv_halves[0])
    mats_first = gather_dp(mats_halves[0])
    qkv_second, mats_second = lax.optimization_barrier(
        (qkv_halves[1], mats_halves[1], qkv_first, mats_first)
    )[:2]
    qkv_gathered = (qkv_first, gather_dp(qkv_second))
    mats_gathered = (mats_first, gather_dp(mats_second))

    layer_in = stream
    saved = []
    for layer in (0, 1):
        pieces = spread_tensor(normed)
        qkv_mine, qkv_other = halves(qkv_gathered[layer])
        own, one, two, head, tail = spread_tensor(mats_gathered[layer])
        mats_mine, mats_other = halves(
            jnp.stack([own, one, two, jnp.concatenate([head, tail], 0)])
        )
        *mixed, queries, keys, values, mass, normed_full, qkv = attend(
            place, pieces, qkv_mine, qkv_other, *tables[layer], *bounds[layer], layer == 0
        )
        mixed = swap_tensor(mixed)
        mid, layer_out, normed = token_forward(
            place, mixed, layer_in, mats_mine, mats_other,
            gain_rows[layer][:, model:], gain_rows[1][:, :model], pair,
        )
        saved.append(
            (layer_in, qkv, qkv_mine.shape, mats_mine, mats_other, normed_full,
             queries, keys, values, mass, mixed, mid)
        )
        layer_in = layer_out
        if layer == 0:
            first_out = layer_out
    second_out = layer_in

    grad = cotangent
    reduced = [None, None]
    gain_grads = [None, None]
    input_grads = [None, None]
    for layer in (1, 0):
        (stream, qkv, qkv_shape, mats_mine, mats_other, normed_full,
         queries, keys, values, mass, mixed, mid) = saved[layer]
        mine_grad, other_grad, *mixed_grad, grad_mid, gain_mlp = token_back(
            place, grad, mid, mixed, mats_mine, mats_other, gain_rows[layer][:, model:], pair
        )
        mixed_grad = swap_tensor(mixed_grad)
        *partial_in, grad_projected = attend_back(
            place, queries, keys, values, mass, mixed_grad, *tables[layer], *bounds[layer], qkv,
            layer == 0,
        )
        grad_normed = scatter_tensor(*partial_in)
        unit, scale = norm_parts(stream.astype(F32))
        gain_attn = jnp.sum(grad_normed * unit, axis=0, keepdims=True)
        grad_in = grad_mid + norm_back(grad_normed, unit, scale, gain_rows[layer][:, :model])
        gain_grads[layer] = jnp.concatenate([gain_attn, gain_mlp], 1)

        mats_kept, mats_came = half_sums(mine_grad, other_grad)
        mats_sum = scatter_tensor(*(add_low(mats_kept[i], mats_came[i]) for i in range(4)))
        qkv_kept, qkv_came = half_sums(
            *qkv_grad(place, normed_full, grad_projected, qkv_shape)
        )
        qkv_sum = qkv_kept.astype(F32) + qkv_came.astype(F32)
        reduced[layer] = scatter_dp(jnp.concatenate([mats_sum, qkv_sum], -1), BF16)
        if layer == 1:
            grad = grad_in.astype(BF16)
            grad_in = grad.astype(F32)
        input_grads[layer] = grad_in

    weight_grad = own_layer(*reduced)
    out_low, down_low = pair + width, pair + width + down_weight.shape[1]
    n = lax.axis_size("dp")
    gain_mine = jnp.where(core == 0, gain_grads[0], gain_grads[1])
    gain_other = swap_cores(jnp.where(core == 0, gain_grads[1], gain_grads[0]))
    gain_blocks = jnp.moveaxis((gain_mine + gain_other).reshape(n, 4, -1), 1, 0)
    me = lax.axis_index("tensor")
    gain_blocks = sum(swap_tensor([take(gain_blocks, me ^ bit) for bit in range(4)]))
    if few_dp():
        rank = lax.axis_index("dp")
        gain_blocks = jnp.stack([take(gain_blocks, (rank - step) % n) for step in range(n)])
    gain_part = scatter_dp(gain_blocks, F32)

    activations = join_halves(
        jnp.where(core == 0, first_out, second_out),
        swap_cores(jnp.where(core == 0, second_out, first_out)),
        0,
    )
    grads_in = join_halves(
        jnp.where(core == 0, input_grads[0], input_grads[1]),
        swap_cores(jnp.where(core == 0, input_grads[1], input_grads[0])),
        0,
    )
    return (
        activations[None, None],
        grads_in[None, None],
        weight_grad[:, down_low:].reshape(qkv_weight.shape),
        weight_grad[:, pair:out_low].T[None],
        weight_grad[:, :pair].reshape(gate_up_weight.shape),
        weight_grad[:, out_low:down_low].T[None],
        gain_part[None],
    )


def solution(mesh):
    return jax.shard_map(
        body,
        mesh=mesh,
        in_specs=(
            P("dp", None, "tensor", None),
            P("dp", None, None),
            P("pipe", "dp", None, "tensor"),
            P("pipe", "tensor", "dp"),
            P("pipe", "dp", None, "tensor"),
            P("pipe", "tensor", "dp"),
            P("pipe", None),
            P("dp", None, "tensor", None),
        ),
        out_specs=(
            P("pipe", "dp", None, "tensor", None),
            P("pipe", "dp", None, "tensor", None),
            P("pipe", "dp", None, "tensor"),
            P("pipe", "tensor", "dp"),
            P("pipe", "dp", None, "tensor"),
            P("pipe", "tensor", "dp"),
            P("pipe", ("dp", "tensor")),
        ),
        check_vma=False,
    )
```

```python
import functools

import jax
import jax.numpy as jnp
from jax import lax
from jax.experimental import pallas as pl
from jax.experimental.pallas import tpu as pltpu
from jax.sharding import PartitionSpec as P

HEAD_DIM = 64
WINDOW = 128
EPS = 1e-05
BLOCK = 256
BF16 = jnp.bfloat16
F32 = jnp.float32
VMEM_BYTES = 36 * 1024 * 1024


def swap_cores(block):
    return lax.ppermute(block, "pipe", [(0, 1), (1, 0)])


def to_mate(block, bit):
    size = lax.axis_size("tensor")
    return lax.ppermute(block, "tensor", [(i, i ^ bit) for i in range(size)])


def put(buffer, block, index):
    return lax.dynamic_update_slice_in_dim(buffer, block[None], index, 0)


def take(buffer, index):
    return lax.dynamic_index_in_dim(buffer, index, 0, keepdims=False)


def to_neighbours(block):
    return to_mate(block, 1), to_mate(block, 2)


def to_far(one, two):
    half = one.shape[0] // 2
    return to_mate(two[:half], 1), to_mate(one[half:], 2)


def after(blocks, *earlier):
    return lax.optimization_barrier((blocks, earlier))[0]


def far_terms(far):
    half = far.shape[0] // 2
    return to_mate(far[:half], 1), to_mate(far[half:], 2)


def near_terms(one, two, head, tail):
    half = head.shape[0]
    one = jnp.concatenate([one[:half], add_low(one[half:], tail)], 0)
    two = jnp.concatenate([add_low(two[:half], head), two[half:]], 0)
    return one, two


def to_near(pair):
    return to_mate(pair[0], 1), to_mate(pair[1], 2)


def slot_sums(kept, came, near):
    return [
        add_up(kept[0][slot], came[0][slot], near[0][slot], near[1][slot]).astype(BF16)
        for slot in range(kept.shape[1])
    ]


def add_low(left, right):
    return (left.astype(F32) + right.astype(F32)).astype(BF16)


def add_up(*terms):
    return sum(term.astype(F32) for term in terms)


def swap_tensor(blocks):
    return (blocks[0],) + tuple(to_mate(blocks[bit], bit) for bit in (1, 2, 3))


def four_dp():
    return lax.axis_size("dp") == 4


def to_peer(block, bit):
    return lax.ppermute(block, "dp", [(i, i ^ bit) for i in range(4)])


def gather_dp(block):
    if four_dp():
        return [block] + [to_peer(block, bit) for bit in (1, 2, 3)]
    return [lax.all_gather(block, "dp", axis=0)]


def stacked(blocks, low, high):
    if four_dp():
        return jnp.stack([block[low:high] for block in blocks])
    return blocks[0][:, low:high]


def scatter_dp(blocks):
    return tuple(to_peer(blocks[bit], bit) for bit in (1, 2, 3)) if four_dp() else ()


def scatter_sum(blocks, came):
    if four_dp():
        return add_up(blocks[0], *came)
    return lax.psum_scatter(
        jnp.stack(blocks), "dp", scatter_dimension=0, tiled=False
    ).astype(F32)


def join_halves(mine, other, axis):
    core = lax.axis_index("pipe")
    out = jnp.stack([mine, other], axis)
    return jnp.where(core == 0, out, jnp.stack([other, mine], axis))


def layer_halves(shard):
    core = lax.axis_index("pipe")
    rows = shard.shape[0] // 2
    mine = lax.dynamic_slice_in_dim(shard, core * rows, rows, 0)
    other = lax.dynamic_slice_in_dim(shard, (1 - core) * rows, rows, 0)
    got = swap_cores(other)
    first = jnp.where(core == 0, mine, got)
    second = jnp.where(core == 0, got, mine)
    return first, second


def placement():
    me = lax.axis_index("tensor")
    if not four_dp():
        return jnp.stack([me, 0, 0]).astype(jnp.int32)
    slots = [lax.axis_index("dp") ^ bit for bit in range(4)]
    return jnp.stack([me, lax.axis_index("pipe")] + slots).astype(jnp.int32)


def halves(block):
    other = swap_cores(block)
    if four_dp():
        return block, other
    both = join_halves(block, other, block.ndim - 2)
    both = both.reshape(block.shape[:-3] + (2, -1, block.shape[-1]))
    return both[..., :1, :, :], both[..., 1:, :, :]


def piece_halves(pieces):
    if four_dp():
        return pieces, tuple(swap_cores(piece) for piece in pieces)
    whole = pieces[:3] + (jnp.concatenate(pieces[3:], 0),)
    return tuple(zip(*(halves(piece) for piece in whole)))


def half_sums(mine, other):
    if four_dp():
        return mine, swap_cores(other)
    core = lax.axis_index("pipe")
    n = lax.axis_size("dp")
    full = jnp.concatenate([mine, other], -3)
    full = full.reshape(full.shape[:-3] + (n, 2, -1, full.shape[-1]))
    axis = full.ndim - 3
    kept = lax.dynamic_index_in_dim(full, core, axis, keepdims=False)
    return kept, swap_cores(lax.dynamic_index_in_dim(full, 1 - core, axis, keepdims=False))


def own_layer(first, second):
    core = lax.axis_index("pipe")
    mine = jnp.where(core == 0, first, second)
    other = swap_cores(jnp.where(core == 0, second, first))
    return join_halves(mine, other, 0).reshape(-1, first.shape[-1])


def norm_parts(stream):
    average = jnp.mean(stream, axis=-1, keepdims=True)
    centred = stream - average
    spread = jnp.mean(centred * centred, axis=-1, keepdims=True)
    scale = lax.rsqrt(spread + EPS)
    return centred * scale, scale


def norm_back(grad, unit, scale, gain):
    scaled = grad * gain
    mean_one = jnp.mean(scaled, axis=-1, keepdims=True)
    mean_two = jnp.mean(scaled * unit, axis=-1, keepdims=True)
    return scale * (scaled - mean_one - unit * mean_two)


def dot(left, right, dims):
    return lax.dot_general(left, right, (dims, ((), ())), preferred_element_type=F32)


NN = ((1,), (0,))
NT = ((1,), (1,))
TN = ((0,), (0,))


def cost(micros):
    return pl.CostEstimate(
        flops=int(micros * 1.15e9), bytes_accessed=int(micros * 3.6e6), transcendentals=0
    )


def slot_rows(place_ref, slot, half, rows):
    return pl.ds(pl.multiple_of((place_ref[2 + slot] * 2 + half) * rows, rows), rows)


def load_halves(place_ref, mine_ref, other_ref, whole_ref, low=0):
    core = place_ref[1]
    slots, rows = mine_ref.shape[0], mine_ref.shape[1]
    packed = mine_ref.shape[2] == 2 * whole_ref.shape[1]
    for slot in range(slots):
        for ref, half in ((mine_ref, core), (other_ref, 1 - core)):
            target = slot_rows(place_ref, low + slot, half, 2 * rows if packed else rows)
            whole_ref[target, :] = unpack(ref[slot]) if packed else ref[slot]


def store_halves(place_ref, whole_ref, mine_ref, other_ref, columns):
    core = place_ref[1]
    slots, rows = mine_ref.shape[0], mine_ref.shape[1]
    for slot in range(slots):
        for ref, half in ((mine_ref, core), (other_ref, 1 - core)):
            ref[slot, :, columns] = whole_ref[slot_rows(place_ref, slot, half, rows), columns]


def load_pieces(place_ref, mine_refs, other_refs, whole_ref):
    for index, (mine_ref, other_ref) in enumerate(zip(mine_refs, other_refs)):
        low = mine_refs[3].shape[0] if index == 4 else 0
        load_halves(place_ref, mine_ref, other_ref, whole_ref.at[min(index, 3)], low)


def pack(block):
    half = block.shape[0] // 2
    return jnp.concatenate([block[:half], block[half:]], 1)


def unpack(block):
    half = block.shape[1] // 2
    return jnp.concatenate([block[:, :half], block[:, half:]], 0)


SCALARS = pl.BlockSpec(memory_space=pltpu.SMEM)
WHOLE = pl.BlockSpec(memory_space=pltpu.VMEM)


def window_start(block_id, rows, span):
    if span == rows:
        return 0
    start = jnp.clip(block_id * BLOCK - WINDOW // 2, 0, rows - span)
    return pl.multiple_of(start, WINDOW // 2)


def key_mask(start, span, first, last):
    keys = start + lax.broadcasted_iota(jnp.int32, (span, BLOCK), 0)
    return (keys >= first) & (keys < last)


def attend_kernel(
    span, place_ref, own_ref, one_ref, two_ref, head_ref, tail_ref, mine_ref, other_ref,
    cos_ref, sin_ref, first_ref, last_ref,
    mixed0_ref, mixed1_ref, mixed2_ref, mixed3_ref, queries_ref, keys_ref, values_ref, mass_ref,
    normed_ref, qkv_ref, key_rows, value_rows, proj, mixed_rows,
):
    width, rows = queries_ref.shape
    heads = width // HEAD_DIM
    half = HEAD_DIM // 2
    local = rows // 4
    me = place_ref[0]
    load_halves(place_ref, mine_ref, other_ref, qkv_ref)
    pieces = (
        (own_ref, 0, 0), (one_ref, 1, 0), (two_ref, 2, 0), (head_ref, 3, 0), (tail_ref, 3, local // 2)
    )
    for ref, bit, shift in pieces:
        low = pl.multiple_of((me ^ bit) * local + shift, local // 2)
        normed_ref[pl.ds(low, ref.shape[0]), :] = ref[...]
    proj[...] = dot(qkv_ref[...].T, normed_ref[...], NT)
    cosines, sines = cos_ref[...], sin_ref[...]
    for head in range(heads):
        low = head * HEAD_DIM
        for part, ref in ((0, queries_ref), (1, keys_ref)):
            upper = proj[part * width + low : part * width + low + half, :]
            lower = proj[part * width + low + half : part * width + low + HEAD_DIM, :]
            turned = jnp.concatenate(
                [upper * cosines - lower * sines, lower * cosines + upper * sines], 0
            )
            ref[low : low + HEAD_DIM, :] = turned.astype(BF16)
            if part == 1:
                key_rows[head] = turned.T.astype(BF16)
        value = proj[2 * width + low : 2 * width + low + HEAD_DIM, :]
        values_ref[low : low + HEAD_DIM, :] = value.astype(BF16)
        value_rows[head] = value.T.astype(BF16)
    mass_ref[...] = jnp.zeros_like(mass_ref)

    def block(block_id, carry):
        start = window_start(block_id, rows, span)
        columns = pl.ds(pl.multiple_of(block_id * BLOCK, BLOCK), BLOCK)
        mask = key_mask(start, span, first_ref[:, columns], last_ref[:, columns])
        outs = []
        for head in range(heads):
            low = head * HEAD_DIM
            query = queries_ref[low : low + HEAD_DIM, columns] * BF16(HEAD_DIM**-0.5)
            scores = dot(key_rows[head, pl.ds(start, span), :], query, NN)
            scores = jnp.where(mask, scores, -1e30)
            top = jnp.max(scores, axis=0, keepdims=True)
            expos = jnp.exp(scores - top)
            total = jnp.sum(expos, axis=0, keepdims=True)
            probs = (expos * (1.0 / total)).astype(BF16)
            if span == rows:
                value = values_ref[low : low + HEAD_DIM, :]
            else:
                value = value_rows[head, pl.ds(start, span), :].T
            outs.append(dot(value, probs, NN))
            mass_ref[head : head + 1, columns] = top + jnp.log(total)
        mixed_rows[columns, :] = jnp.concatenate(outs, 0).T.astype(BF16)
        return carry

    lax.fori_loop(0, rows // BLOCK, block, 0)
    for bit, ref in enumerate((mixed0_ref, mixed1_ref, mixed2_ref, mixed3_ref)):
        low = pl.multiple_of((me ^ bit) * local, local)
        ref[...] = pack(mixed_rows[pl.ds(low, local), :])


def attend(place, pieces, mine, other, width, cosines, sines, first, last, is_local):
    local, model = pieces[0].shape
    rows = 4 * local
    heads = width // HEAD_DIM
    span = min(rows, BLOCK + WINDOW) if is_local else rows
    shape = jax.ShapeDtypeStruct((width, rows), BF16)
    mixed = jax.ShapeDtypeStruct((local // 2, 2 * width), BF16)
    return pl.pallas_call(
        functools.partial(attend_kernel, span),
        out_shape=(
            mixed, mixed, mixed, mixed, shape, shape, shape, jax.ShapeDtypeStruct((8, rows), F32),
            jax.ShapeDtypeStruct((rows, model), BF16),
            jax.ShapeDtypeStruct((model, 3 * width), BF16),
        ),
        in_specs=[SCALARS] + [WHOLE] * 11,
        scratch_shapes=[
            pltpu.VMEM((heads, rows, HEAD_DIM), BF16),
            pltpu.VMEM((heads, rows, HEAD_DIM), BF16),
            pltpu.VMEM((3 * width, rows), F32),
            pltpu.VMEM((rows, width), BF16),
        ],
        compiler_params=pltpu.CompilerParams(vmem_limit_bytes=VMEM_BYTES),
        cost_estimate=cost(11 if is_local else 20),
        name="attend_local" if is_local else "attend_global",
    )(place, *pieces, mine, other, cosines, sines, first, last)


def attend_back_kernel(
    span, place_ref, queries_ref, keys_ref, values_ref, mass_ref,
    grad0_ref, grad1_ref, grad2_ref, grad3_ref,
    cos_ref, sin_ref, first_ref, last_ref, qkv_ref,
    part0_ref, part1_ref, part2_ref, part3_ref, out_ref,
    query_rows, key_rows, value_rows, grad_cols, grad_all, grad_rows, sum_q, sum_k, sum_v, flat,
):
    width, rows = queries_ref.shape
    heads = width // HEAD_DIM
    half = HEAD_DIM // 2
    local = rows // 4
    scale = HEAD_DIM**-0.5
    me = place_ref[0]
    for bit, ref in enumerate((grad0_ref, grad1_ref, grad2_ref, grad3_ref)):
        low = pl.multiple_of((me ^ bit) * local, local)
        grad_all[pl.ds(low, local), :] = unpack(ref[...])
    grad_cols[...] = grad_all[...].T
    for head in range(heads):
        cut = slice(head * HEAD_DIM, (head + 1) * HEAD_DIM)
        query_rows[head] = (queries_ref[cut, :] * BF16(scale)).T
        key_rows[head] = keys_ref[cut, :].T
        value_rows[head] = values_ref[cut, :].T
        grad_rows[head] = grad_all[:, cut]
    sum_k[...] = jnp.zeros_like(sum_k)
    sum_v[...] = jnp.zeros_like(sum_v)

    def block(block_id, carry):
        start = window_start(block_id, rows, span)
        window = pl.ds(start, span)
        columns = pl.ds(pl.multiple_of(block_id * BLOCK, BLOCK), BLOCK)
        mask = key_mask(start, span, first_ref[:, columns], last_ref[:, columns])
        for head in range(heads):
            cut = slice(head * HEAD_DIM, (head + 1) * HEAD_DIM)
            query = queries_ref[cut, columns] * BF16(scale)
            key = key_rows[head, window, :]
            scores = dot(key, query, NN) - mass_ref[head : head + 1, columns]
            probs = jnp.exp(jnp.where(mask, scores, -1e30))
            grad_probs = dot(value_rows[head, window, :], grad_cols[cut, columns], NN)
            weighted = probs * grad_probs
            inner = jnp.sum(weighted, axis=0, keepdims=True)
            grad_scores = (weighted - probs * inner).astype(BF16)
            sum_v[head, window, :] += dot(probs.astype(BF16), grad_rows[head, columns, :], NN)
            sum_k[head, window, :] += dot(grad_scores, query_rows[head, columns, :], NN)
            key_cols = keys_ref[cut, :] if span == rows else key.T
            sum_q[cut, columns] = dot(key_cols, grad_scores, NN)
        return carry

    lax.fori_loop(0, rows // BLOCK, block, 0)
    cosines, sines = cos_ref[...], sin_ref[...]
    for head in range(heads):
        low = head * HEAD_DIM
        turned_q = sum_q[low : low + HEAD_DIM, :] * scale
        for part, turned in ((0, turned_q), (1, sum_k[head].T)):
            upper, lower = turned[:half], turned[half:]
            raw = jnp.concatenate(
                [upper * cosines + lower * sines, lower * cosines - upper * sines], 0
            )
            flat[part * width + low : part * width + low + HEAD_DIM, :] = raw.astype(BF16)
        flat[2 * width + low : 2 * width + low + HEAD_DIM, :] = sum_v[head].T.astype(BF16)
    out_ref[...] = flat[...].T
    for bit, ref in enumerate((part0_ref, part1_ref, part2_ref, part3_ref)):
        low = pl.multiple_of((me ^ bit) * local, local)
        ref[...] = dot(out_ref[pl.ds(low, local), :], qkv_ref[...], NT).astype(BF16)


def attend_back(place, queries, keys, values, mass, grads, cosines, sines, first, last, qkv, is_local):
    width, rows = queries.shape
    model = qkv.shape[0]
    heads = width // HEAD_DIM
    span = min(rows, BLOCK + WINDOW) if is_local else rows
    low_rows = pltpu.VMEM((heads, rows, HEAD_DIM), BF16)
    sums = pltpu.VMEM((heads, rows, HEAD_DIM), F32)
    part = jax.ShapeDtypeStruct((rows // 4, model), BF16)
    return pl.pallas_call(
        functools.partial(attend_back_kernel, span),
        out_shape=(part, part, part, part, jax.ShapeDtypeStruct((rows, 3 * width), BF16)),
        in_specs=[SCALARS] + [WHOLE] * 13,
        scratch_shapes=[
            low_rows, low_rows, low_rows, pltpu.VMEM((width, rows), BF16),
            pltpu.VMEM((rows, width), BF16), low_rows,
            pltpu.VMEM((width, rows), F32), sums, sums, pltpu.VMEM((3 * width, rows), BF16),
        ],
        compiler_params=pltpu.CompilerParams(vmem_limit_bytes=VMEM_BYTES),
        cost_estimate=cost(11 if is_local else 21),
        name="attend_back_local" if is_local else "attend_back_global",
    )(place, queries, keys, values, mass, *grads, cosines, sines, first, last, qkv)


def qkv_grad_kernel(place_ref, normed_ref, grad_ref, qkv_ref, mine_ref, other_ref, gain_ref, whole):
    grad = dot(normed_ref[...].T, grad_ref[...], NN)
    gain_ref[...] = jnp.sum(grad * qkv_ref[...].astype(F32), axis=1, keepdims=True)
    whole[...] = grad.astype(BF16)
    store_halves(place_ref, whole, mine_ref, other_ref, slice(None))


def qkv_grad(place, normed, grad, qkv, shape):
    part = jax.ShapeDtypeStruct(shape, BF16)
    return pl.pallas_call(
        qkv_grad_kernel,
        out_shape=(part, part, jax.ShapeDtypeStruct((qkv.shape[0], 1), F32)),
        in_specs=[SCALARS, WHOLE, WHOLE, WHOLE],
        scratch_shapes=[pltpu.VMEM((normed.shape[1], grad.shape[1]), BF16)],
        compiler_params=pltpu.CompilerParams(vmem_limit_bytes=VMEM_BYTES),
        cost_estimate=cost(4),
        name="qkv_grad",
    )(place, normed, grad, qkv)


def erf_parts(gate):
    cumulative = 0.5 * (1.0 + lax.erf(gate * 0.7071067811865476))
    density = 0.3989422804014327 * jnp.exp(-0.5 * gate * gate)
    return cumulative, density


def token_kernel(pair, place_ref, mixed0_ref, mixed1_ref, mixed2_ref, mixed3_ref, in_ref, *refs):
    pieces = (len(refs) - 7) // 2
    mine_refs, other_refs = refs[:pieces], refs[pieces : 2 * pieces]
    gain_ref, next_ref, mid_ref, out_ref, normed_ref, sums, mats = refs[2 * pieces :]
    parts = mats.shape[0]
    width = mixed0_ref.shape[1] // 2
    units = pair // 2
    load_pieces(place_ref, mine_refs, other_refs, mats)
    mid = in_ref[...].astype(F32)
    for part, ref in enumerate((mixed0_ref, mixed1_ref, mixed2_ref, mixed3_ref)):
        mid += dot(unpack(ref[...]), mats[part, :, pair : pair + width], NT)
    mid_ref[...] = mid
    sums[...] = mid
    normed = (norm_parts(mid)[0] * gain_ref[...]).astype(BF16)

    def feed(part, carry):
        gate_up = dot(normed, mats[part, :, :pair], NN)
        gate = gate_up[:, :units]
        hidden = (gate * erf_parts(gate)[0] * gate_up[:, units:]).astype(BF16)
        sums[...] += dot(hidden, mats[part, :, pair + width : pair + width + units], NT)
        return carry

    lax.fori_loop(0, parts, feed, 0)
    low = sums[...].astype(BF16)
    out_ref[...] = low
    normed_ref[...] = (norm_parts(low.astype(F32))[0] * next_ref[...]).astype(BF16)


def token_forward(place, mixed, layer_in, mine, other, gain, next_gain, pair):
    shape = layer_in.shape
    return pl.pallas_call(
        functools.partial(token_kernel, pair),
        out_shape=(
            jax.ShapeDtypeStruct(shape, F32),
            jax.ShapeDtypeStruct(shape, BF16),
            jax.ShapeDtypeStruct(shape, BF16),
        ),
        in_specs=[SCALARS] + [WHOLE] * (7 + 2 * len(mine)),
        scratch_shapes=[
            pltpu.VMEM(shape, F32),
            pltpu.VMEM((4, shape[1], mine[0].shape[2]), BF16),
        ],
        compiler_params=pltpu.CompilerParams(vmem_limit_bytes=VMEM_BYTES),
        cost_estimate=cost(10),
        name="token_forward",
    )(place, *mixed, layer_in, *mine, *other, gain, next_gain)


def token_back_kernel(
    pair, place_ref, grad_ref, mid_ref, mixed0_ref, mixed1_ref, mixed2_ref, mixed3_ref, *refs
):
    pieces = (len(refs) - 12) // 2
    mine_refs, other_refs = refs[:pieces], refs[pieces : 2 * pieces]
    (gain_ref, mine_grad_ref, other_grad_ref, mixed_grad0_ref, mixed_grad1_ref, mixed_grad2_ref,
     mixed_grad3_ref, grad_mid_ref, gain_grad_ref, sums, mats, grads) = refs[2 * pieces :]
    parts = mats.shape[0]
    width = mixed0_ref.shape[1] // 2
    units = pair // 2
    load_pieces(place_ref, mine_refs, other_refs, mats)
    grad = grad_ref[...].astype(F32)
    grad_low = grad.astype(BF16)
    grad_flip = grad.T.astype(BF16)
    unit, scale = norm_parts(mid_ref[...])
    gained = unit * gain_ref[...]
    normed = gained.astype(BF16)
    normed_flip = gained.T.astype(BF16)
    sums[...] = jnp.zeros_like(sums)

    def feed(part, carry):
        gate_up = dot(normed, mats[part, :, :pair], NN)
        gate, up = gate_up[:, :units], gate_up[:, units:]
        cumulative, density = erf_parts(gate)
        gelu = gate * cumulative
        hidden = (gelu * up).astype(BF16)
        grad_hidden = dot(grad_low, mats[part, :, pair + width : pair + width + units], NN)
        grad_gate = grad_hidden * up * (cumulative + gate * density)
        grad_up = grad_hidden * gelu
        grad_pair = jnp.concatenate([grad_gate, grad_up], 1).astype(BF16)
        grads[:, pair + width :] = dot(grad_flip, hidden, NN).astype(BF16)
        grads[:, :pair] = dot(normed_flip, grad_pair, NN).astype(BF16)
        for columns in (slice(0, pair), slice(pair + width, None)):
            store_halves(
                place_ref, grads, mine_grad_ref.at[part], other_grad_ref.at[part], columns
            )
        sums[...] += dot(grad_pair, mats[part, :, :pair], NT)
        return carry

    lax.fori_loop(0, parts, feed, 0)
    grad_normed = sums[...]
    gain_grad_ref[...] = jnp.sum(grad_normed * unit, axis=0, keepdims=True)
    grad_mid = grad + norm_back(grad_normed, unit, scale, gain_ref[...])
    grad_mid_ref[...] = grad_mid
    mid_low = grad_mid.astype(BF16)
    mid_flip = grad_mid.T.astype(BF16)
    mixed_refs = (mixed0_ref, mixed1_ref, mixed2_ref, mixed3_ref)
    mixed_grad_refs = (mixed_grad0_ref, mixed_grad1_ref, mixed_grad2_ref, mixed_grad3_ref)
    for part in range(parts):
        weight = mats[part, :, pair : pair + width]
        mixed_grad_refs[part][...] = pack(dot(mid_low, weight, NN).astype(BF16))
        grads[:, pair : pair + width] = dot(mid_flip, unpack(mixed_refs[part][...]), NN).astype(BF16)
        store_halves(
            place_ref, grads, mine_grad_ref.at[part], other_grad_ref.at[part],
            slice(pair, pair + width),
        )


def token_back(place, grad, mid, mixed, mine, other, gain, pair):
    shape = mine[0].shape
    total = pair + mixed[0].shape[1] // 2 + pair // 2
    half = jax.ShapeDtypeStruct((4,) + shape[:2] + (total,), BF16)
    mixed_grad = jax.ShapeDtypeStruct(mixed[0].shape, BF16)
    return pl.pallas_call(
        functools.partial(token_back_kernel, pair),
        out_shape=(
            half, half, mixed_grad, mixed_grad, mixed_grad, mixed_grad,
            jax.ShapeDtypeStruct(mid.shape, F32),
            jax.ShapeDtypeStruct((1, mid.shape[1]), F32),
        ),
        in_specs=[SCALARS] + [WHOLE] * (7 + 2 * len(mine)),
        scratch_shapes=[
            pltpu.VMEM(mid.shape, F32),
            pltpu.VMEM((4, mid.shape[1], shape[2]), BF16),
            pltpu.VMEM((mid.shape[1], total), BF16),
        ],
        compiler_params=pltpu.CompilerParams(vmem_limit_bytes=VMEM_BYTES),
        cost_estimate=cost(20),
        name="token_back",
    )(place, grad, mid, *mixed, *mine, *other, gain)


def frequencies(theta_base, half_dim):
    return theta_base ** (-(jnp.arange(half_dim, dtype=F32) * 2.0) / (2.0 * half_dim))


def sequences(seq_lengths, rows):
    seq_ends = jnp.cumsum(seq_lengths)
    positions = jnp.arange(rows, dtype=jnp.int32)
    seq_of = jnp.sum((positions[:, None] >= seq_ends[None, :]).astype(jnp.int32), axis=1)
    matches = jnp.arange(seq_lengths.shape[0], dtype=jnp.int32)[None, :] == seq_of[:, None]
    last = jnp.sum(jnp.where(matches, seq_ends[None, :], 0), axis=1)
    first = jnp.sum(jnp.where(matches, (seq_ends - seq_lengths)[None, :], 0), axis=1)
    return first[None], last[None], positions[None]


def body(
    tokens, lengths, qkv_weight, out_weight, gate_up_weight, down_weight, gains, out_cotangent
):
    core = lax.axis_index("pipe")
    model = tokens.shape[-1]
    local_rows = tokens.shape[2]
    rows = 4 * local_rows
    shard_rows = qkv_weight.shape[1]
    width = qkv_weight.shape[3]
    pair = 2 * gate_up_weight.shape[3]

    stream = take(tokens[0], core)
    cotangent = take(out_cotangent[0], core)
    first, last, positions = sequences(take(lengths[0], core), rows)
    bounds = (
        (jnp.maximum(first, positions - WINDOW // 2), jnp.minimum(last, positions + WINDOW // 2 + 1)),
        (first, last),
    )
    tables = []
    for base in (10000.0, 160000.0):
        turns = frequencies(base, HEAD_DIM // 2)[:, None] * (positions - first).astype(F32)
        tables.append((jnp.cos(turns), jnp.sin(turns)))

    other_gains = swap_cores(gains[0])
    gain_rows = (
        jnp.where(core == 0, gains[0], other_gains)[None],
        jnp.where(core == 0, other_gains, gains[0])[None],
    )
    place = placement()

    normed = (norm_parts(stream.astype(F32))[0] * gain_rows[0][:, :model]).astype(BF16)
    mats = jnp.concatenate(
        [gate_up_weight[0].reshape(shard_rows, pair), out_weight[0].T, down_weight[0].T], 1
    )
    spare = 6 * width - mats.shape[1]
    mats = jnp.pad(mats, ((0, 0), (0, spare))).reshape(2, shard_rows // 2, 6 * width)
    qkv = qkv_weight[0].reshape(2, 2, shard_rows // 4, 3 * width)
    qkv = jnp.concatenate([qkv[:, 0], qkv[:, 1]], -1)
    first_half, second_half = layer_halves(
        jnp.concatenate([mats, qkv], 1).reshape(-1, 6 * width)
    )
    split = shard_rows // 2
    total = first_half.shape[0]
    qkv_shape = (4, split, 3 * width) if four_dp() else (1, model // 2, 3 * width)

    def qkv_halves(blocks):
        block = stacked(blocks, split, total)
        if not four_dp():
            block = jnp.concatenate([block[..., : 3 * width], block[..., 3 * width :]], 1)
        return halves(block)

    normed, first_half, second_half = after((normed, first_half, second_half))
    near, blocks = to_neighbours(normed), gather_dp(first_half)
    far = to_far(*after(near))
    far, blocks = after((far, blocks))
    mats_first = stacked(blocks, 0, split)
    qkv_parts = [qkv_halves(blocks), None]
    mats_first, second_half = after((mats_first, second_half), qkv_parts[0])
    pieces = (normed,) + near + far
    saved_attend = [None, None]
    saved_token = [None, None]

    mats_near = to_neighbours(mats_first)
    second_blocks = gather_dp(second_half)
    second_blocks, second_late = second_blocks[:3], second_blocks[3:]
    *mixed, queries, keys, values, mass, normed_full, qkv = attend(
        place, pieces, *qkv_parts[0], width, *tables[0], *bounds[0], True
    )
    saved_attend[0] = (queries, keys, values, mass, normed_full, qkv)
    mixed, mats_first, mats_near, second_blocks = after(
        (mixed, mats_first, mats_near, second_blocks)
    )
    mixed, mats_far = after((swap_tensor(mixed), to_far(*mats_near)))
    mats = piece_halves((mats_first,) + mats_near + mats_far)
    mid, first_out, normed = token_forward(
        place, mixed, stream, *mats, gain_rows[0][:, model:], gain_rows[1][:, :model], pair
    )
    saved_token[0] = (mid, mixed) + mats

    normed, second_late = after((normed, second_late))
    near = after(to_neighbours(normed))
    blocks = second_blocks + second_late
    qkv_parts[1] = qkv_halves(blocks)
    far, qkv_parts[1] = after((to_far(*near), qkv_parts[1]))
    pieces = (normed,) + near + far
    mats_second = after(stacked(blocks, 0, split), far)
    second_near = to_neighbours(mats_second)
    *mixed, queries, keys, values, mass, normed_full, qkv = attend(
        place, pieces, *qkv_parts[1], width, *tables[1], *bounds[1], False
    )
    saved_attend[1] = (queries, keys, values, mass, normed_full, qkv)
    mixed, second_near = after((mixed, second_near))
    mixed, second_far = after((swap_tensor(mixed), to_far(*second_near)))
    mats = piece_halves((mats_second,) + second_near + second_far)
    mid, second_out, _ = token_forward(
        place, mixed, first_out, *mats, gain_rows[1][:, model:], gain_rows[1][:, :model], pair
    )
    saved_token[1] = (mid, mixed) + mats

    def token_step(layer, grad):
        mid, mixed, mine, other = saved_token[layer]
        return token_back(
            place, grad, mid, mixed, mine, other, gain_rows[layer][:, model:], pair
        )

    def attend_step(layer, mixed_grad):
        queries, keys, values, mass, _, qkv = saved_attend[layer]
        return attend_back(
            place, queries, keys, values, mass, mixed_grad, *tables[layer], *bounds[layer],
            qkv, layer == 0,
        )

    def weight_step(layer, grad_projected):
        normed_full, qkv = saved_attend[layer][4:]
        mine, other, gain_sum = qkv_grad(
            place, normed_full, grad_projected, qkv, qkv_shape
        )
        return half_sums(mine, other) + (gain_sum.reshape(1, model) / gain_rows[layer][:, :model],)

    def norm_step(layer, partial_in, near, grad_mid):
        grad_normed = add_up(partial_in[0], *near)
        unit, scale = norm_parts((stream, first_out)[layer].astype(F32))
        return grad_mid + norm_back(grad_normed, unit, scale, gain_rows[layer][:, :model])

    def qkv_blocks(kept, came):
        return [add_low(kept[slot], came[slot]) for slot in range(kept.shape[0])]

    mine_grad, other_grad, *mixed_grad, grad_mid, gain_mlp = token_step(1, cotangent)
    mixed_grad = swap_tensor(mixed_grad)
    kept, came = half_sums(mine_grad, other_grad)
    mixed_grad, kept, came = after((mixed_grad, kept, came))
    far = far_terms(add_low(kept[3], came[3]))
    *partial_in, grad_projected = attend_step(1, mixed_grad)
    partial_in, grad_projected, far = after((partial_in, grad_projected, far))
    in_far = far_terms(partial_in[3])
    pair_terms = near_terms(add_low(kept[1], came[1]), add_low(kept[2], came[2]), *far)
    qkv_kept, qkv_came, gain_attn = weight_step(1, grad_projected)
    second_gain = jnp.concatenate([gain_attn, gain_mlp], 1)
    in_far, qkv_kept, qkv_came = after((in_far, qkv_kept, qkv_came))
    second_qkv = qkv_blocks(qkv_kept, qkv_came)
    in_near = to_near(near_terms(partial_in[1], partial_in[2], *in_far))
    in_near, pair_terms, second_qkv = after((in_near, pair_terms, second_qkv))
    near, second_qkv_came = to_near(pair_terms), scatter_dp(second_qkv)
    grad = norm_step(1, partial_in, in_near, grad_mid).astype(BF16)
    second_grad = grad.astype(F32)

    second_kept, second_came = kept, came
    mine_grad, other_grad, *mixed_grad, grad_mid, gain_mlp = token_step(0, grad)
    mixed_grad, other_grad, near, second_qkv_came = after(
        (mixed_grad, other_grad, near, second_qkv_came)
    )
    mixed_grad = swap_tensor(mixed_grad)
    kept, came = half_sums(mine_grad, other_grad)
    second_mats = slot_sums(second_kept, second_came, near)
    mixed_grad, kept, came, second_mats = after((mixed_grad, kept, came, second_mats))
    far = far_terms(add_low(kept[3], came[3]))
    second_mats_came = scatter_dp(second_mats)
    second_early, second_late = second_mats_came[1:], second_mats_came[:1]
    *partial_in, grad_projected = attend_step(0, mixed_grad)
    partial_in, grad_projected, far, kept, came, second_early = after(
        (partial_in, grad_projected, far, kept, came, second_early)
    )
    second_mats_came = second_late + second_early

    near = to_near(near_terms(add_low(kept[1], came[1]), add_low(kept[2], came[2]), *far))
    qkv_kept, qkv_came, gain_attn = weight_step(0, grad_projected)
    first_gain = jnp.concatenate([gain_attn, gain_mlp], 1)
    first_qkv = qkv_blocks(qkv_kept, qkv_came)
    first_qkv_came = scatter_dp(first_qkv)
    gain_sum = jnp.where(core == 0, first_gain, second_gain)
    gain_sum += swap_cores(jnp.where(core == 0, second_gain, first_gain))
    near, first_qkv_came, second_mats_came, partial_in, gain_sum = after(
        (near, first_qkv_came, second_mats_came, partial_in, gain_sum)
    )
    first_mats = slot_sums(kept, came, near)
    first_mats_came, in_far = scatter_dp(first_mats), far_terms(partial_in[3])
    gain_sum += to_mate(gain_sum, 1)
    first_mats_came, in_far, partial_in, gain_sum = after(
        (first_mats_came, in_far, partial_in, gain_sum)
    )
    in_near = to_near(near_terms(partial_in[1], partial_in[2], *in_far))
    gain_sum += to_mate(gain_sum, 2)
    chunk = model * 2 // (4 * lax.axis_size("dp"))
    me = lax.axis_index("dp") * 4 + lax.axis_index("tensor")
    if four_dp():
        gain_sum += to_peer(gain_sum, 1)
        gain_sum += to_peer(gain_sum, 2)
    else:
        gain_sum = lax.psum(gain_sum, "dp")
    gain_part = lax.dynamic_slice_in_dim(gain_sum[0], me * chunk, chunk, 0)
    first_grad = norm_step(0, partial_in, in_near, grad_mid)
    input_grads = (first_grad, second_grad)

    qkv_total = own_layer(
        scatter_sum(first_qkv, first_qkv_came), scatter_sum(second_qkv, second_qkv_came)
    )
    mats_total = own_layer(
        scatter_sum(first_mats, first_mats_came), scatter_sum(second_mats, second_mats_came)
    )
    activations = join_halves(
        jnp.where(core == 0, first_out, second_out),
        swap_cores(jnp.where(core == 0, second_out, first_out)),
        0,
    )
    grads_in = join_halves(
        jnp.where(core == 0, input_grads[0], input_grads[1]),
        swap_cores(jnp.where(core == 0, input_grads[1], input_grads[0])),
        0,
    )
    return (
        activations[None, None],
        grads_in[None, None],
        qkv_total.reshape(qkv_weight.shape),
        mats_total[:, pair : pair + width].T[None],
        mats_total[:, :pair].reshape(gate_up_weight.shape),
        mats_total[:, pair + width :].T[None],
        gain_part[None],
    )


def solution(mesh):
    return jax.shard_map(
        body,
        mesh=mesh,
        in_specs=(
            P("dp", None, "tensor", None),
            P("dp", None, None),
            P("pipe", "dp", None, "tensor"),
            P("pipe", "tensor", "dp"),
            P("pipe", "dp", None, "tensor"),
            P("pipe", "tensor", "dp"),
            P("pipe", None),
            P("dp", None, "tensor", None),
        ),
        out_specs=(
            P("pipe", "dp", None, "tensor", None),
            P("pipe", "dp", None, "tensor", None),
            P("pipe", "dp", None, "tensor"),
            P("pipe", "tensor", "dp"),
            P("pipe", "dp", None, "tensor"),
            P("pipe", "tensor", "dp"),
            P("pipe", ("dp", "tensor")),
        ),
        check_vma=False,
    )
```

```python
import functools

import jax
import jax.numpy as jnp
from jax import lax
from jax.experimental import pallas as pl
from jax.experimental.pallas import tpu as pltpu
from jax.sharding import PartitionSpec as P

HEAD_DIM = 64
WINDOW = 128
EPS = 1e-05
BLOCK = 256
CHUNK = 128
BF16 = jnp.bfloat16
F32 = jnp.float32
VMEM_BYTES = 36 * 1024 * 1024


def swap_cores(block):
    return lax.ppermute(block, "pipe", [(0, 1), (1, 0)])


def to_mate(block, bit):
    size = lax.axis_size("tensor")
    return lax.ppermute(block, "tensor", [(i, i ^ bit) for i in range(size)])


def put(buffer, block, index):
    return lax.dynamic_update_slice_in_dim(buffer, block[None], index, 0)


def take(buffer, index):
    return lax.dynamic_index_in_dim(buffer, index, 0, keepdims=False)


def to_neighbours(block):
    return to_mate(block, 1), to_mate(block, 2)


def to_far(one, two):
    half = one.shape[0] // 2
    return to_mate(two[:half], 1), to_mate(one[half:], 2)


def after(blocks, *earlier):
    return lax.optimization_barrier((blocks, earlier))[0]


def far_terms(far):
    half = far.shape[0] // 2
    return to_mate(far[:half], 1), to_mate(far[half:], 2)


def near_terms(one, two, head, tail):
    half = head.shape[0]
    one = jnp.concatenate([one[:half], add_low(one[half:], tail)], 0)
    two = jnp.concatenate([add_low(two[:half], head), two[half:]], 0)
    return one, two


def rows_early(parts):
    _, one0, _, _, two1, far0, far1 = parts
    return to_mate(far0, 1), to_mate(far1, 2), to_mate(one0, 1), to_mate(two1, 2)


def rows_late(parts, early):
    _, _, one1, two0, _, _, _ = parts
    return to_mate(add_low(one1, early[1]), 1), to_mate(add_low(two0, early[0]), 2)


def rows_sum(parts, early, late):
    half = early[2].shape[0]
    upper = add_up(parts[0][:half], early[2], late[1])
    lower = add_up(parts[0][half:], late[0], early[3])
    return jnp.concatenate([upper, lower], 0)


def to_near(pair):
    return to_mate(pair[0], 1), to_mate(pair[1], 2)


def slot_sums(kept, came, near):
    return [
        add_up(kept[0][slot], came[0][slot], near[0][slot], near[1][slot]).astype(BF16)
        for slot in range(kept.shape[1])
    ]


def add_low(left, right):
    return (left.astype(F32) + right.astype(F32)).astype(BF16)


def add_up(*terms):
    return sum(term.astype(F32) for term in terms)


def swap_tensor(blocks):
    return (blocks[0],) + tuple(to_mate(blocks[bit], bit) for bit in (1, 2, 3))


def four_dp():
    return lax.axis_size("dp") == 4


def to_peer(block, bit):
    return lax.ppermute(block, "dp", [(i, i ^ bit) for i in range(4)])


def gather_dp(block):
    if four_dp():
        return [block] + [to_peer(block, bit) for bit in (1, 2, 3)]
    return [lax.all_gather(block, "dp", axis=0)]


def scatter_dp(blocks):
    return tuple(to_peer(blocks[bit], bit) for bit in (1, 2, 3)) if four_dp() else ()


def scatter_sum(blocks, came):
    if four_dp():
        return add_up(blocks[0], *came)
    return lax.psum_scatter(
        jnp.stack(blocks), "dp", scatter_dimension=0, tiled=False
    ).astype(F32)


def join_halves(mine, other, axis):
    core = lax.axis_index("pipe")
    out = jnp.stack([mine, other], axis)
    return jnp.where(core == 0, out, jnp.stack([other, mine], axis))


def layer_halves(shard):
    core = lax.axis_index("pipe")
    rows = shard.shape[0] // 2
    mine = lax.dynamic_slice_in_dim(shard, core * rows, rows, 0)
    other = lax.dynamic_slice_in_dim(shard, (1 - core) * rows, rows, 0)
    got = swap_cores(other)
    first = jnp.where(core == 0, mine, got)
    second = jnp.where(core == 0, got, mine)
    return first, second


def placement():
    me = lax.axis_index("tensor")
    if not four_dp():
        return jnp.stack([me, 0, 0]).astype(jnp.int32)
    slots = [lax.axis_index("dp") ^ bit for bit in range(4)]
    return jnp.stack([me, lax.axis_index("pipe")] + slots).astype(jnp.int32)


def halves(block):
    other = swap_cores(block)
    if four_dp():
        return block, other
    both = join_halves(block, other, block.ndim - 2)
    both = both.reshape(block.shape[:-3] + (2, -1, block.shape[-1]))
    return both[..., :1, :, :], both[..., 1:, :, :]


def piece_halves(pieces):
    if four_dp():
        return pieces, tuple(swap_cores(piece) for piece in pieces)
    whole = pieces[:3] + (jnp.concatenate(pieces[3:], 0),)
    return tuple(zip(*(halves(piece) for piece in whole)))


def half_sums(mine, other):
    if four_dp():
        return mine, swap_cores(other)
    core = lax.axis_index("pipe")
    n = lax.axis_size("dp")
    full = jnp.concatenate([mine, other], -3)
    full = full.reshape(full.shape[:-3] + (n, 2, -1, full.shape[-1]))
    axis = full.ndim - 3
    kept = lax.dynamic_index_in_dim(full, core, axis, keepdims=False)
    return kept, swap_cores(lax.dynamic_index_in_dim(full, 1 - core, axis, keepdims=False))


def own_layer(first, second):
    core = lax.axis_index("pipe")
    mine = jnp.where(core == 0, first, second)
    other = swap_cores(jnp.where(core == 0, second, first))
    return join_halves(mine, other, 0).reshape(-1, first.shape[-1])


def norm_parts(stream):
    average = jnp.mean(stream, axis=-1, keepdims=True)
    centred = stream - average
    spread = jnp.mean(centred * centred, axis=-1, keepdims=True)
    scale = lax.rsqrt(spread + EPS)
    return centred * scale, scale


def norm_back(grad, unit, scale, gain):
    scaled = grad * gain
    mean_one = jnp.mean(scaled, axis=-1, keepdims=True)
    mean_two = jnp.mean(scaled * unit, axis=-1, keepdims=True)
    return scale * (scaled - mean_one - unit * mean_two)


def dot(left, right, dims):
    return lax.dot_general(left, right, (dims, ((), ())), preferred_element_type=F32)


NN = ((1,), (0,))
NT = ((1,), (1,))
TN = ((0,), (0,))


def cost(micros):
    return pl.CostEstimate(
        flops=int(micros * 1.15e9), bytes_accessed=int(micros * 3.6e6), transcendentals=0
    )


def slot_rows(place_ref, slot, half, rows):
    return pl.ds(pl.multiple_of((place_ref[2 + slot] * 2 + half) * rows, rows), rows)


def load_halves(place_ref, mine_ref, other_ref, whole_ref, low=0):
    core = place_ref[1]
    slots, rows = mine_ref.shape[0], mine_ref.shape[1]
    packed = mine_ref.shape[2] == 2 * whole_ref.shape[1]
    for slot in range(slots):
        for ref, half in ((mine_ref, core), (other_ref, 1 - core)):
            target = slot_rows(place_ref, low + slot, half, 2 * rows if packed else rows)
            whole_ref[target, :] = unpack(ref[slot]) if packed else ref[slot]


def store_halves(place_ref, whole_ref, mine_ref, other_ref, columns):
    core = place_ref[1]
    slots, rows = mine_ref.shape[0], mine_ref.shape[1]
    packed = mine_ref.shape[2] == 2 * whole_ref.shape[1]
    for slot in range(slots):
        for ref, half in ((mine_ref, core), (other_ref, 1 - core)):
            if packed:
                ref[slot] = pack(whole_ref[slot_rows(place_ref, slot, half, 2 * rows), :])
            else:
                ref[slot, :, columns] = whole_ref[slot_rows(place_ref, slot, half, rows), columns]


def load_pieces(place_ref, mine_refs, other_refs, whole_ref):
    for index, (mine_ref, other_ref) in enumerate(zip(mine_refs, other_refs)):
        low = mine_refs[3].shape[0] if index == 4 else 0
        load_halves(place_ref, mine_ref, other_ref, whole_ref.at[min(index, 3)], low)


def pack(block):
    half = block.shape[0] // 2
    return jnp.concatenate([block[:half], block[half:]], 1)


def unpack(block):
    half = block.shape[1] // 2
    return jnp.concatenate([block[:, :half], block[:, half:]], 0)


SCALARS = pl.BlockSpec(memory_space=pltpu.SMEM)
WHOLE = pl.BlockSpec(memory_space=pltpu.VMEM)


def window_start(block_id, rows, span):
    if span == rows:
        return 0
    start = jnp.clip(block_id * BLOCK - WINDOW // 2, 0, rows - span)
    return pl.multiple_of(start, WINDOW // 2)


def key_mask(start, span, first, last):
    keys = start + lax.broadcasted_iota(jnp.int32, (span, BLOCK), 0)
    return (keys >= first) & (keys < last)


def stack_kernel(split, block0_ref, block1_ref, block2_ref, block3_ref, upper_ref, lower_ref):
    for slot, ref in enumerate((block0_ref, block1_ref, block2_ref, block3_ref)):
        upper_ref[slot] = ref[:split]
        lower_ref[slot] = ref[split:]


def stack_blocks(blocks, split):
    rows, columns = blocks[0].shape
    return pl.pallas_call(
        functools.partial(stack_kernel, split),
        out_shape=(
            jax.ShapeDtypeStruct((4, split, columns), BF16),
            jax.ShapeDtypeStruct((4, rows - split, columns), BF16),
        ),
        in_specs=[WHOLE] * 4,
        compiler_params=pltpu.CompilerParams(vmem_limit_bytes=VMEM_BYTES),
        cost_estimate=cost(2),
        name="stack_blocks",
    )(*blocks)


def attend_kernel(
    span, place_ref, own_ref, one_ref, two_ref, head_ref, tail_ref, mine_ref, other_ref,
    cos_ref, sin_ref, first_ref, last_ref,
    mixed0_ref, mixed1_ref, mixed2_ref, mixed3_ref, queries_ref, keys_ref, values_ref, mass_ref,
    normed_ref, qkv_ref, outs_ref, key_rows, value_rows, proj, mixed_rows, bias, scores,
):
    width, rows = queries_ref.shape
    heads = width // HEAD_DIM
    half = HEAD_DIM // 2
    local = rows // 4
    me = place_ref[0]
    load_halves(place_ref, mine_ref, other_ref, qkv_ref)
    pieces = (
        (own_ref, 0, 0), (one_ref, 1, 0), (two_ref, 2, 0), (head_ref, 3, 0), (tail_ref, 3, local // 2)
    )
    for ref, bit, shift in pieces:
        low = pl.multiple_of((me ^ bit) * local + shift, local // 2)
        normed_ref[pl.ds(low, ref.shape[0]), :] = ref[...]
    proj[...] = dot(qkv_ref[...].T, normed_ref[...], NT)
    cosines, sines = cos_ref[...], sin_ref[...]
    for head in range(heads):
        low = head * HEAD_DIM
        for part, ref in ((0, queries_ref), (1, keys_ref)):
            upper = proj[part * width + low : part * width + low + half, :]
            lower = proj[part * width + low + half : part * width + low + HEAD_DIM, :]
            turned = jnp.concatenate(
                [upper * cosines - lower * sines, lower * cosines + upper * sines], 0
            )
            ref[low : low + HEAD_DIM, :] = turned.astype(BF16)
            if part == 1:
                key_rows[head] = turned.T.astype(BF16)
        value = proj[2 * width + low : 2 * width + low + HEAD_DIM, :]
        values_ref[low : low + HEAD_DIM, :] = value.astype(BF16)
        value_rows[head] = value.T.astype(BF16)
    mass_ref[...] = jnp.zeros_like(mass_ref)

    def block(block_id, carry):
        start = window_start(block_id, rows, span)
        columns = pl.ds(pl.multiple_of(block_id * BLOCK, BLOCK), BLOCK)
        mask = key_mask(start, span, first_ref[:, columns], last_ref[:, columns])
        bias[...] = jnp.where(mask, 0.0, -1e30)
        outs = []
        for head in range(heads):
            low = head * HEAD_DIM
            query = queries_ref[low : low + HEAD_DIM, columns] * BF16(HEAD_DIM**-0.5)
            top = jnp.full((1, BLOCK), -2e30, F32)
            for part in range(0, span, CHUNK):
                key = key_rows[head, pl.ds(start + part, CHUNK), :]
                score = dot(key, query, NN) + bias[part : part + CHUNK]
                scores[part : part + CHUNK] = score
                top = jnp.maximum(top, jnp.max(score, axis=0, keepdims=True))
            total = jnp.zeros((1, BLOCK), F32)
            out = jnp.zeros((HEAD_DIM, BLOCK), F32)
            for part in range(0, span, CHUNK):
                expos = jnp.exp(scores[part : part + CHUNK] - top)
                total += jnp.sum(expos, axis=0, keepdims=True)
                if span == rows:
                    value = values_ref[low : low + HEAD_DIM, part : part + CHUNK]
                else:
                    value = value_rows[head, pl.ds(start + part, CHUNK), :].T
                out += dot(value, expos.astype(BF16), NN)
            outs.append(out * (1.0 / total))
            mass_ref[head : head + 1, columns] = top + jnp.log(total)
        outs_ref[:, columns] = jnp.concatenate(outs, 0)
        mixed_rows[columns, :] = jnp.concatenate(outs, 0).T.astype(BF16)
        return carry

    lax.fori_loop(0, rows // BLOCK, block, 0)
    for bit, ref in enumerate((mixed0_ref, mixed1_ref, mixed2_ref, mixed3_ref)):
        low = pl.multiple_of((me ^ bit) * local, local)
        ref[...] = pack(mixed_rows[pl.ds(low, local), :])


def attend(place, pieces, mine, other, width, cosines, sines, first, last, is_local):
    local, model = pieces[0].shape
    rows = 4 * local
    heads = width // HEAD_DIM
    span = min(rows, BLOCK + WINDOW) if is_local else rows
    shape = jax.ShapeDtypeStruct((width, rows), BF16)
    mixed = jax.ShapeDtypeStruct((local // 2, 2 * width), BF16)
    return pl.pallas_call(
        functools.partial(attend_kernel, span),
        out_shape=(
            mixed, mixed, mixed, mixed, shape, shape, shape, jax.ShapeDtypeStruct((8, rows), F32),
            jax.ShapeDtypeStruct((rows, model), BF16),
            jax.ShapeDtypeStruct((model, 3 * width), BF16),
            jax.ShapeDtypeStruct((width, rows), F32),
        ),
        in_specs=[SCALARS] + [WHOLE] * 11,
        scratch_shapes=[
            pltpu.VMEM((heads, rows, HEAD_DIM), BF16),
            pltpu.VMEM((heads, rows, HEAD_DIM), BF16),
            pltpu.VMEM((3 * width, rows), F32),
            pltpu.VMEM((rows, width), BF16),
            pltpu.VMEM((span, BLOCK), F32),
            pltpu.VMEM((span, BLOCK), F32),
        ],
        compiler_params=pltpu.CompilerParams(vmem_limit_bytes=VMEM_BYTES),
        cost_estimate=cost(11 if is_local else 20),
        name="attend_local" if is_local else "attend_global",
    )(place, *pieces, mine, other, cosines, sines, first, last)


def attend_back_kernel(
    span, place_ref, queries_ref, keys_ref, values_ref, mass_ref,
    grad0_ref, grad1_ref, grad2_ref, grad3_ref,
    cos_ref, sin_ref, first_ref, last_ref, qkv_ref, outs_ref,
    own_ref, one0_ref, one1_ref, two0_ref, two1_ref, far0_ref, far1_ref, out_ref,
    query_rows, key_rows, value_rows, grad_cols, grad_all, grad_rows, sum_q, sum_k, sum_v, flat, bias,
    probs_low, scores_low,
):
    width, rows = queries_ref.shape
    heads = width // HEAD_DIM
    half = HEAD_DIM // 2
    local = rows // 4
    scale = HEAD_DIM**-0.5
    me = place_ref[0]
    for bit, ref in enumerate((grad0_ref, grad1_ref, grad2_ref, grad3_ref)):
        low = pl.multiple_of((me ^ bit) * local, local)
        grad_all[pl.ds(low, local), :] = unpack(ref[...])
    grad_cols[...] = grad_all[...].T
    for head in range(heads):
        cut = slice(head * HEAD_DIM, (head + 1) * HEAD_DIM)
        query_rows[head] = (queries_ref[cut, :] * BF16(scale)).T
        key_rows[head] = keys_ref[cut, :].T
        value_rows[head] = values_ref[cut, :].T
        grad_rows[head] = grad_all[:, cut]
    sum_k[...] = jnp.zeros_like(sum_k)
    sum_v[...] = jnp.zeros_like(sum_v)

    def block(block_id, carry):
        start = window_start(block_id, rows, span)
        columns = pl.ds(pl.multiple_of(block_id * BLOCK, BLOCK), BLOCK)
        mask = key_mask(start, span, first_ref[:, columns], last_ref[:, columns])
        bias[...] = jnp.where(mask, 0.0, -1e30)
        for head in range(heads):
            cut = slice(head * HEAD_DIM, (head + 1) * HEAD_DIM)
            query = queries_ref[cut, columns] * BF16(scale)
            grad = grad_cols[cut, columns]
            mass = mass_ref[head : head + 1, columns]
            inner = jnp.sum(grad.astype(F32) * outs_ref[cut, columns], axis=0, keepdims=True)
            for part in range(0, span, CHUNK):
                window = pl.ds(start + part, CHUNK)
                scores = dot(key_rows[head, window, :], query, NN)
                probs = jnp.exp(scores - mass + bias[part : part + CHUNK])
                grad_probs = dot(value_rows[head, window, :], grad, NN)
                probs_low[part : part + CHUNK] = probs.astype(BF16)
                scores_low[part : part + CHUNK] = (probs * (grad_probs - inner)).astype(BF16)
            window = pl.ds(start, span)
            key_cols = keys_ref[cut, :] if span == rows else key_rows[head, window, :].T
            sum_v[head, window, :] += dot(probs_low[...], grad_rows[head, columns, :], NN)
            sum_k[head, window, :] += dot(scores_low[...], query_rows[head, columns, :], NN)
            sum_q[cut, columns] = dot(key_cols, scores_low[...], NN)
        return carry

    lax.fori_loop(0, rows // BLOCK, block, 0)
    cosines, sines = cos_ref[...], sin_ref[...]
    for head in range(heads):
        low = head * HEAD_DIM
        turned_q = sum_q[low : low + HEAD_DIM, :] * scale
        for part, turned in ((0, turned_q), (1, sum_k[head].T)):
            upper, lower = turned[:half], turned[half:]
            raw = jnp.concatenate(
                [upper * cosines + lower * sines, lower * cosines - upper * sines], 0
            )
            flat[part * width + low : part * width + low + HEAD_DIM, :] = raw.astype(BF16)
        flat[2 * width + low : 2 * width + low + HEAD_DIM, :] = sum_v[head].T.astype(BF16)
    out_ref[...] = flat[...].T
    targets = ((own_ref,), (one0_ref, one1_ref), (two0_ref, two1_ref), (far0_ref, far1_ref))
    for bit, refs in enumerate(targets):
        low = pl.multiple_of((me ^ bit) * local, local)
        part = dot(out_ref[pl.ds(low, local), :], qkv_ref[...], NT).astype(BF16)
        size = local // len(refs)
        for index, ref in enumerate(refs):
            ref[...] = part[index * size : (index + 1) * size]


def attend_back(
    place, queries, keys, values, mass, grads, cosines, sines, first, last, qkv, outs, is_local
):
    width, rows = queries.shape
    model = qkv.shape[0]
    heads = width // HEAD_DIM
    span = min(rows, BLOCK + WINDOW) if is_local else rows
    low_rows = pltpu.VMEM((heads, rows, HEAD_DIM), BF16)
    sums = pltpu.VMEM((heads, rows, HEAD_DIM), F32)
    part = jax.ShapeDtypeStruct((rows // 4, model), BF16)
    half = jax.ShapeDtypeStruct((rows // 8, model), BF16)
    return pl.pallas_call(
        functools.partial(attend_back_kernel, span),
        out_shape=(part,) + (half,) * 6 + (jax.ShapeDtypeStruct((rows, 3 * width), BF16),),
        in_specs=[SCALARS] + [WHOLE] * 14,
        scratch_shapes=[
            low_rows, low_rows, low_rows, pltpu.VMEM((width, rows), BF16),
            pltpu.VMEM((rows, width), BF16), low_rows,
            pltpu.VMEM((width, rows), F32), sums, sums, pltpu.VMEM((3 * width, rows), BF16),
            pltpu.VMEM((span, BLOCK), F32), pltpu.VMEM((span, BLOCK), BF16),
            pltpu.VMEM((span, BLOCK), BF16),
        ],
        compiler_params=pltpu.CompilerParams(vmem_limit_bytes=VMEM_BYTES),
        cost_estimate=cost(11 if is_local else 21),
        name="attend_back_local" if is_local else "attend_back_global",
    )(place, queries, keys, values, mass, *grads, cosines, sines, first, last, qkv, outs)


def qkv_grad_kernel(place_ref, normed_ref, grad_ref, qkv_ref, mine_ref, other_ref, gain_ref, whole):
    grad = dot(normed_ref[...].T, grad_ref[...], NN)
    gain_ref[...] = jnp.sum(grad * qkv_ref[...].astype(F32), axis=1, keepdims=True)
    whole[...] = grad.astype(BF16)
    store_halves(place_ref, whole, mine_ref, other_ref, slice(None))


def qkv_grad(place, normed, grad, qkv, shape):
    part = jax.ShapeDtypeStruct(shape, BF16)
    return pl.pallas_call(
        qkv_grad_kernel,
        out_shape=(part, part, jax.ShapeDtypeStruct((qkv.shape[0], 1), F32)),
        in_specs=[SCALARS, WHOLE, WHOLE, WHOLE],
        scratch_shapes=[pltpu.VMEM((normed.shape[1], grad.shape[1]), BF16)],
        compiler_params=pltpu.CompilerParams(vmem_limit_bytes=VMEM_BYTES),
        cost_estimate=cost(4),
        name="qkv_grad",
    )(place, normed, grad, qkv)


def erf_parts(gate):
    cumulative = 0.5 * (1.0 + lax.erf(gate * 0.7071067811865476))
    density = 0.3989422804014327 * jnp.exp(-0.5 * gate * gate)
    return cumulative, density


def token_kernel(pair, place_ref, mixed0_ref, mixed1_ref, mixed2_ref, mixed3_ref, in_ref, *refs):
    pieces = (len(refs) - 7) // 2
    mine_refs, other_refs = refs[:pieces], refs[pieces : 2 * pieces]
    gain_ref, next_ref, mid_ref, out_ref, normed_ref, sums, mats = refs[2 * pieces :]
    parts = mats.shape[0]
    width = mixed0_ref.shape[1] // 2
    units = pair // 2
    load_pieces(place_ref, mine_refs, other_refs, mats)
    mid = in_ref[...].astype(F32)
    for part, ref in enumerate((mixed0_ref, mixed1_ref, mixed2_ref, mixed3_ref)):
        mid += dot(unpack(ref[...]), mats[part, :, pair : pair + width], NT)
    mid_ref[...] = mid
    sums[...] = mid
    normed = (norm_parts(mid)[0] * gain_ref[...]).astype(BF16)

    def feed(part, carry):
        gate_up = dot(normed, mats[part, :, :pair], NN)
        gate = gate_up[:, :units]
        hidden = (gate * erf_parts(gate)[0] * gate_up[:, units:]).astype(BF16)
        sums[...] += dot(hidden, mats[part, :, pair + width : pair + width + units], NT)
        return carry

    lax.fori_loop(0, parts, feed, 0)
    low = sums[...].astype(BF16)
    out_ref[...] = low
    normed_ref[...] = (norm_parts(low.astype(F32))[0] * next_ref[...]).astype(BF16)


def token_forward(place, mixed, layer_in, mine, other, gain, next_gain, pair):
    shape = layer_in.shape
    return pl.pallas_call(
        functools.partial(token_kernel, pair),
        out_shape=(
            jax.ShapeDtypeStruct(shape, F32),
            jax.ShapeDtypeStruct(shape, BF16),
            jax.ShapeDtypeStruct(shape, BF16),
        ),
        in_specs=[SCALARS] + [WHOLE] * (7 + 2 * len(mine)),
        scratch_shapes=[
            pltpu.VMEM(shape, F32),
            pltpu.VMEM((4, shape[1], mine[0].shape[2]), BF16),
        ],
        compiler_params=pltpu.CompilerParams(vmem_limit_bytes=VMEM_BYTES),
        cost_estimate=cost(10),
        name="token_forward",
    )(place, *mixed, layer_in, *mine, *other, gain, next_gain)


def token_back_kernel(
    pair, place_ref, grad_ref, mid_ref, mixed0_ref, mixed1_ref, mixed2_ref, mixed3_ref, *refs
):
    pieces = (len(refs) - 12) // 2
    mine_refs, other_refs = refs[:pieces], refs[pieces : 2 * pieces]
    (gain_ref, mine_grad_ref, other_grad_ref, mixed_grad0_ref, mixed_grad1_ref, mixed_grad2_ref,
     mixed_grad3_ref, grad_mid_ref, gain_grad_ref, sums, mats, grads) = refs[2 * pieces :]
    parts = mats.shape[0]
    width = mixed0_ref.shape[1] // 2
    units = pair // 2
    load_pieces(place_ref, mine_refs, other_refs, mats)
    grad = grad_ref[...].astype(F32)
    grad_low = grad.astype(BF16)
    grad_flip = grad.T.astype(BF16)
    unit, scale = norm_parts(mid_ref[...])
    gained = unit * gain_ref[...]
    normed = gained.astype(BF16)
    normed_flip = gained.T.astype(BF16)
    sums[...] = jnp.zeros_like(sums)
    used = pair + width + units
    grads[:, used:] = jnp.zeros((grads.shape[0], grads.shape[1] - used), BF16)

    def feed(part, carry):
        gate_up = dot(normed, mats[part, :, :pair], NN)
        gate, up = gate_up[:, :units], gate_up[:, units:]
        cumulative, density = erf_parts(gate)
        gelu = gate * cumulative
        hidden = (gelu * up).astype(BF16)
        grad_hidden = dot(grad_low, mats[part, :, pair + width : pair + width + units], NN)
        grad_gate = grad_hidden * up * (cumulative + gate * density)
        grad_up = grad_hidden * gelu
        grad_pair = jnp.concatenate([grad_gate, grad_up], 1).astype(BF16)
        grads[:, pair + width : used] = dot(grad_flip, hidden, NN).astype(BF16)
        grads[:, :pair] = dot(normed_flip, grad_pair, NN).astype(BF16)
        for columns in (slice(0, pair), slice(pair + width, None)):
            store_halves(
                place_ref, grads, mine_grad_ref.at[part], other_grad_ref.at[part], columns
            )
        sums[...] += dot(grad_pair, mats[part, :, :pair], NT)
        return carry

    lax.fori_loop(0, parts, feed, 0)
    grad_normed = sums[...]
    gain_grad_ref[...] = jnp.sum(grad_normed * unit, axis=0, keepdims=True)
    grad_mid = grad + norm_back(grad_normed, unit, scale, gain_ref[...])
    grad_mid_ref[...] = grad_mid
    mid_low = grad_mid.astype(BF16)
    mid_flip = grad_mid.T.astype(BF16)
    mixed_refs = (mixed0_ref, mixed1_ref, mixed2_ref, mixed3_ref)
    mixed_grad_refs = (mixed_grad0_ref, mixed_grad1_ref, mixed_grad2_ref, mixed_grad3_ref)
    for part in range(parts):
        weight = mats[part, :, pair : pair + width]
        mixed_grad_refs[part][...] = pack(dot(mid_low, weight, NN).astype(BF16))
        grads[:, pair : pair + width] = dot(mid_flip, unpack(mixed_refs[part][...]), NN).astype(BF16)
        store_halves(
            place_ref, grads, mine_grad_ref.at[part], other_grad_ref.at[part],
            slice(pair, pair + width),
        )


def token_back(place, grad, mid, mixed, mine, other, gain, pair):
    shape = mine[0].shape
    half = jax.ShapeDtypeStruct((4,) + shape, BF16)
    mixed_grad = jax.ShapeDtypeStruct(mixed[0].shape, BF16)
    return pl.pallas_call(
        functools.partial(token_back_kernel, pair),
        out_shape=(
            half, half, mixed_grad, mixed_grad, mixed_grad, mixed_grad,
            jax.ShapeDtypeStruct(mid.shape, F32),
            jax.ShapeDtypeStruct((1, mid.shape[1]), F32),
        ),
        in_specs=[SCALARS] + [WHOLE] * (7 + 2 * len(mine)),
        scratch_shapes=[
            pltpu.VMEM(mid.shape, F32),
            pltpu.VMEM((4, mid.shape[1], shape[2]), BF16),
            pltpu.VMEM((mid.shape[1], shape[2]), BF16),
        ],
        compiler_params=pltpu.CompilerParams(vmem_limit_bytes=VMEM_BYTES),
        cost_estimate=cost(20),
        name="token_back",
    )(place, grad, mid, *mixed, *mine, *other, gain)


def frequencies(theta_base, half_dim):
    return theta_base ** (-(jnp.arange(half_dim, dtype=F32) * 2.0) / (2.0 * half_dim))


def sequences(seq_lengths, rows):
    seq_ends = jnp.cumsum(seq_lengths)
    positions = jnp.arange(rows, dtype=jnp.int32)
    seq_of = jnp.sum((positions[:, None] >= seq_ends[None, :]).astype(jnp.int32), axis=1)
    matches = jnp.arange(seq_lengths.shape[0], dtype=jnp.int32)[None, :] == seq_of[:, None]
    last = jnp.sum(jnp.where(matches, seq_ends[None, :], 0), axis=1)
    first = jnp.sum(jnp.where(matches, (seq_ends - seq_lengths)[None, :], 0), axis=1)
    return first[None], last[None], positions[None]


def body(
    tokens, lengths, qkv_weight, out_weight, gate_up_weight, down_weight, gains, out_cotangent
):
    core = lax.axis_index("pipe")
    model = tokens.shape[-1]
    local_rows = tokens.shape[2]
    rows = 4 * local_rows
    shard_rows = qkv_weight.shape[1]
    width = qkv_weight.shape[3]
    pair = 2 * gate_up_weight.shape[3]

    stream = take(tokens[0], core)
    cotangent = take(out_cotangent[0], core)
    first, last, positions = sequences(take(lengths[0], core), rows)
    bounds = (
        (jnp.maximum(first, positions - WINDOW // 2), jnp.minimum(last, positions + WINDOW // 2 + 1)),
        (first, last),
    )
    tables = []
    for base in (10000.0, 160000.0):
        turns = frequencies(base, HEAD_DIM // 2)[:, None] * (positions - first).astype(F32)
        tables.append((jnp.cos(turns), jnp.sin(turns)))

    other_gains = swap_cores(gains[0])
    gain_rows = (
        jnp.where(core == 0, gains[0], other_gains)[None],
        jnp.where(core == 0, other_gains, gains[0])[None],
    )
    place = placement()

    normed = (norm_parts(stream.astype(F32))[0] * gain_rows[0][:, :model]).astype(BF16)
    mats = jnp.concatenate(
        [gate_up_weight[0].reshape(shard_rows, pair), out_weight[0].T, down_weight[0].T], 1
    )
    spare = 6 * width - mats.shape[1]
    mats = jnp.pad(mats, ((0, 0), (0, spare))).reshape(2, shard_rows // 2, 6 * width)
    qkv = qkv_weight[0].reshape(2, 2, shard_rows // 4, 3 * width)
    qkv = jnp.concatenate([qkv[:, 0], qkv[:, 1]], -1)
    first_half, second_half = layer_halves(
        jnp.concatenate([mats, qkv], 1).reshape(-1, 6 * width)
    )
    split = shard_rows // 2
    total = first_half.shape[0]
    qkv_shape = (4, split // 2, 6 * width) if four_dp() else (1, model // 2, 3 * width)

    def split_blocks(blocks):
        if four_dp():
            upper, lower = stack_blocks(blocks, split)
            return upper, halves(lower)
        upper, lower = blocks[0][:, :split], blocks[0][:, split:]
        lower = jnp.concatenate([lower[..., : 3 * width], lower[..., 3 * width :]], 1)
        return upper, halves(lower)

    normed, first_half, second_half = after((normed, first_half, second_half))
    near, blocks = to_neighbours(normed), gather_dp(first_half)
    far = to_far(*after(near))
    far, blocks = after((far, blocks))
    mats_first, qkv_first = split_blocks(blocks)
    mats_first, second_half = after((mats_first, second_half), qkv_first)
    pieces = (normed,) + near + far
    saved_attend = [None, None]
    saved_token = [None, None]

    mats_near = to_neighbours(mats_first)
    second_blocks = gather_dp(second_half)
    second_blocks, second_late = second_blocks[:3], second_blocks[3:]
    *mixed, queries, keys, values, mass, normed_full, qkv, outs = attend(
        place, pieces, *qkv_first, width, *tables[0], *bounds[0], True
    )
    saved_attend[0] = (queries, keys, values, mass, normed_full, qkv, outs)
    mixed, mats_first, mats_near, second_blocks = after(
        (mixed, mats_first, mats_near, second_blocks)
    )
    mixed, mats_far = after((swap_tensor(mixed), to_far(*mats_near)))
    mats = piece_halves((mats_first,) + mats_near + mats_far)
    mid, first_out, normed = token_forward(
        place, mixed, stream, *mats, gain_rows[0][:, model:], gain_rows[1][:, :model], pair
    )
    saved_token[0] = (mid, mixed) + mats

    near, second_late = after((to_neighbours(normed), second_late))
    blocks = second_blocks + second_late
    mats_second, qkv_second = split_blocks(blocks)
    far, qkv_second = after((to_far(*near), qkv_second))
    pieces = (normed,) + near + far
    mats_second = after(mats_second, far)
    second_near = to_neighbours(mats_second)
    *mixed, queries, keys, values, mass, normed_full, qkv, outs = attend(
        place, pieces, *qkv_second, width, *tables[1], *bounds[1], False
    )
    saved_attend[1] = (queries, keys, values, mass, normed_full, qkv, outs)
    mixed, second_near = after((mixed, second_near))
    mixed, second_far = after((swap_tensor(mixed), to_far(*second_near)))
    mats = piece_halves((mats_second,) + second_near + second_far)
    mid, second_out, _ = token_forward(
        place, mixed, first_out, *mats, gain_rows[1][:, model:], gain_rows[1][:, :model], pair
    )
    saved_token[1] = (mid, mixed) + mats

    def token_step(layer, grad):
        mid, mixed, mine, other = saved_token[layer]
        return token_back(
            place, grad, mid, mixed, mine, other, gain_rows[layer][:, model:], pair
        )

    def attend_step(layer, mixed_grad):
        queries, keys, values, mass, _, qkv, outs = saved_attend[layer]
        return attend_back(
            place, queries, keys, values, mass, mixed_grad, *tables[layer], *bounds[layer],
            qkv, outs, layer == 0,
        )

    def weight_step(layer, grad_projected):
        normed_full, qkv = saved_attend[layer][4:6]
        mine, other, gain_sum = qkv_grad(
            place, normed_full, grad_projected, qkv, qkv_shape
        )
        return half_sums(mine, other) + (gain_sum.reshape(1, model) / gain_rows[layer][:, :model],)

    def norm_step(layer, grad_normed, grad_mid):
        unit, scale = norm_parts((stream, first_out)[layer].astype(F32))
        return grad_mid + norm_back(grad_normed, unit, scale, gain_rows[layer][:, :model])

    def qkv_blocks(kept, came):
        return [add_low(kept[slot], came[slot]) for slot in range(kept.shape[0])]

    mine_grad, other_grad, *mixed_grad, grad_mid, gain_mlp = token_step(1, cotangent)
    mixed_grad = swap_tensor(mixed_grad)
    kept, came = half_sums(mine_grad, other_grad)
    mixed_grad, kept, came = after((mixed_grad, kept, came))
    far = far_terms(add_low(kept[3], came[3]))
    *parts, grad_projected = attend_step(1, mixed_grad)
    parts, grad_projected, far = after((parts, grad_projected, far))
    early = rows_early(parts)
    pair_terms = near_terms(add_low(kept[1], came[1]), add_low(kept[2], came[2]), *far)
    qkv_kept, qkv_came, gain_attn = weight_step(1, grad_projected)
    second_gain = jnp.concatenate([gain_attn, gain_mlp], 1)
    late = rows_late(parts, early)
    late, pair_terms, qkv_kept, qkv_came = after((late, pair_terms, qkv_kept, qkv_came), early)
    near = to_near(pair_terms)
    grad = norm_step(1, rows_sum(parts, early, late), grad_mid).astype(BF16)
    second_grad = grad.astype(F32)

    second_kept, second_came, second_qkv = kept, came, qkv_blocks(qkv_kept, qkv_came)
    mine_grad, other_grad, *mixed_grad, grad_mid, gain_mlp = token_step(0, grad)
    mixed_grad, other_grad, near = after((mixed_grad, other_grad, near))
    mixed_grad = swap_tensor(mixed_grad)
    kept, came = half_sums(mine_grad, other_grad)
    second = slot_sums(second_kept, second_came, near)
    if four_dp():
        second = [jnp.concatenate(block, 0) for block in zip(second, second_qkv)]
    mixed_grad, kept, came, second = after((mixed_grad, kept, came, second))
    far = far_terms(add_low(kept[3], came[3]))
    *parts, grad_projected = attend_step(0, mixed_grad)
    parts, grad_projected, far, kept, came = after((parts, grad_projected, far, kept, came))

    pair_terms = near_terms(add_low(kept[1], came[1]), add_low(kept[2], came[2]), *far)
    pair_terms, grad_projected = after((pair_terms, grad_projected))
    near, second_came = to_near(pair_terms), scatter_dp(second)
    qkv_kept, qkv_came, gain_attn = weight_step(0, grad_projected)
    first_gain = jnp.concatenate([gain_attn, gain_mlp], 1)
    gain_sum = jnp.where(core == 0, first_gain, second_gain)
    gain_sum += swap_cores(jnp.where(core == 0, second_gain, first_gain))
    first_qkv = qkv_blocks(qkv_kept, qkv_came)
    near, second_came, parts, gain_sum, first_qkv = after(
        (near, second_came, parts, gain_sum, first_qkv)
    )
    first = slot_sums(kept, came, near)
    if four_dp():
        first = [jnp.concatenate(block, 0) for block in zip(first, first_qkv)]
    first_came = scatter_dp(first)
    gain_sum += to_mate(gain_sum, 1)
    rows_far = (to_mate(parts[5], 1), to_mate(parts[6], 2))
    rows_far, parts, gain_sum = after((rows_far, parts, gain_sum))
    rows_near = to_near(
        (
            jnp.concatenate([parts[1], add_low(parts[2], rows_far[1])], 0),
            jnp.concatenate([add_low(parts[3], rows_far[0]), parts[4]], 0),
        )
    )
    gain_sum += to_mate(gain_sum, 2)
    gain_sum, first_came = after((gain_sum, first_came))
    chunk = model * 2 // (4 * lax.axis_size("dp"))
    me = lax.axis_index("dp") * 4 + lax.axis_index("tensor")
    if four_dp():
        gain_sum += to_peer(gain_sum, 1)
        gain_sum += to_peer(gain_sum, 2)
    else:
        gain_sum = lax.psum(gain_sum, "dp")
    gain_part = lax.dynamic_slice_in_dim(gain_sum[0], me * chunk, chunk, 0)
    first_grad = norm_step(0, add_up(parts[0], *rows_near), grad_mid)
    input_grads = (first_grad, second_grad)

    if four_dp():
        total_grad = own_layer(scatter_sum(first, first_came), scatter_sum(second, second_came))
        total_grad = total_grad.reshape(2, total, 6 * width)
        mats_total = total_grad[:, :split].reshape(shard_rows, 6 * width)
        qkv_total = total_grad[:, split:].reshape(-1, 6 * width)
    else:
        mats_total = own_layer(scatter_sum(first, ()), scatter_sum(second, ()))
        qkv_total = own_layer(scatter_sum(first_qkv, ()), scatter_sum(second_qkv, ()))
    if four_dp():
        qkv_total = qkv_total.reshape(2, shard_rows // 4, 2, 3 * width)
        qkv_total = jnp.moveaxis(qkv_total, 2, 1).reshape(shard_rows, 3 * width)

    activations = join_halves(
        jnp.where(core == 0, first_out, second_out),
        swap_cores(jnp.where(core == 0, second_out, first_out)),
        0,
    )
    grads_in = join_halves(
        jnp.where(core == 0, input_grads[0], input_grads[1]),
        swap_cores(jnp.where(core == 0, input_grads[1], input_grads[0])),
        0,
    )
    return (
        activations[None, None],
        grads_in[None, None],
        qkv_total.reshape(qkv_weight.shape),
        mats_total[:, pair : pair + width].T[None],
        mats_total[:, :pair].reshape(gate_up_weight.shape),
        mats_total[:, pair + width : pair + width + pair // 2].T[None],
        gain_part[None],
    )


def solution(mesh):
    return jax.shard_map(
        body,
        mesh=mesh,
        in_specs=(
            P("dp", None, "tensor", None),
            P("dp", None, None),
            P("pipe", "dp", None, "tensor"),
            P("pipe", "tensor", "dp"),
            P("pipe", "dp", None, "tensor"),
            P("pipe", "tensor", "dp"),
            P("pipe", None),
            P("dp", None, "tensor", None),
        ),
        out_specs=(
            P("pipe", "dp", None, "tensor", None),
            P("pipe", "dp", None, "tensor", None),
            P("pipe", "dp", None, "tensor"),
            P("pipe", "tensor", "dp"),
            P("pipe", "dp", None, "tensor"),
            P("pipe", "tensor", "dp"),
            P("pipe", ("dp", "tensor")),
        ),
        check_vma=False,
    )
```

```python
import functools

import jax
import jax.numpy as jnp
from jax import lax
from jax.experimental import pallas as pl
from jax.experimental.pallas import tpu as pltpu
from jax.sharding import PartitionSpec as P

HEAD_DIM = 64
WINDOW = 128
EPS = 1e-05
BLOCK = 256
CHUNK = 128
BF16 = jnp.bfloat16
F32 = jnp.float32
VMEM_BYTES = 36 * 1024 * 1024


def swap_cores(block):
    return lax.ppermute(block, "pipe", [(0, 1), (1, 0)])


def to_mate(block, bit):
    size = lax.axis_size("tensor")
    return lax.ppermute(block, "tensor", [(i, i ^ bit) for i in range(size)])


def put(buffer, block, index):
    return lax.dynamic_update_slice_in_dim(buffer, block[None], index, 0)


def take(buffer, index):
    return lax.dynamic_index_in_dim(buffer, index, 0, keepdims=False)


def to_neighbours(block):
    return to_mate(block, 1), to_mate(block, 2)


def to_far(one, two):
    half = one.shape[0] // 2
    return to_mate(two[:half], 1), to_mate(one[half:], 2)


def after(blocks, *earlier):
    return lax.optimization_barrier((blocks, earlier))[0]


def far_terms(far):
    half = far.shape[0] // 2
    return to_mate(far[:half], 1), to_mate(far[half:], 2)


def near_terms(one, two, head, tail):
    half = head.shape[0]
    one = jnp.concatenate([one[:half], add_low(one[half:], tail)], 0)
    two = jnp.concatenate([add_low(two[:half], head), two[half:]], 0)
    return one, two


def rows_early(parts):
    _, one0, _, _, two1, far0, far1 = parts
    return to_mate(far0, 1), to_mate(far1, 2), to_mate(one0, 1), to_mate(two1, 2)


def rows_late(parts, early):
    _, _, one1, two0, _, _, _ = parts
    return to_mate(add_low(one1, early[1]), 1), to_mate(add_low(two0, early[0]), 2)


def rows_sum(parts, early, late):
    half = early[2].shape[0]
    upper = add_up(parts[0][:half], early[2], late[1])
    lower = add_up(parts[0][half:], late[0], early[3])
    return jnp.concatenate([upper, lower], 0)


def to_near(pair):
    return to_mate(pair[0], 1), to_mate(pair[1], 2)


def slot_sums(kept, came, near):
    return [
        add_up(kept[0][slot], came[0][slot], near[0][slot], near[1][slot]).astype(BF16)
        for slot in range(kept.shape[1])
    ]


def add_low(left, right):
    return (left.astype(F32) + right.astype(F32)).astype(BF16)


def add_up(*terms):
    return sum(term.astype(F32) for term in terms)


def swap_tensor(blocks):
    return (blocks[0],) + tuple(to_mate(blocks[bit], bit) for bit in (1, 2, 3))


def four_dp():
    return lax.axis_size("dp") == 4


def to_peer(block, bit):
    return lax.ppermute(block, "dp", [(i, i ^ bit) for i in range(4)])


def gather_dp(block):
    if four_dp():
        return [block] + [to_peer(block, bit) for bit in (1, 2, 3)]
    return [lax.all_gather(block, "dp", axis=0)]


def scatter_dp(blocks, bits=(1, 2, 3)):
    return tuple(to_peer(blocks[bit], bit) for bit in bits) if four_dp() else ()


def scatter_sum(blocks, came):
    if four_dp():
        return add_up(blocks[0], *came)
    return lax.psum_scatter(
        jnp.stack(blocks), "dp", scatter_dimension=0, tiled=False
    ).astype(F32)


def join_halves(mine, other, axis):
    core = lax.axis_index("pipe")
    out = jnp.stack([mine, other], axis)
    return jnp.where(core == 0, out, jnp.stack([other, mine], axis))


def layer_halves(shard):
    core = lax.axis_index("pipe")
    rows = shard.shape[0] // 2
    mine = lax.dynamic_slice_in_dim(shard, core * rows, rows, 0)
    other = lax.dynamic_slice_in_dim(shard, (1 - core) * rows, rows, 0)
    got = swap_cores(other)
    first = jnp.where(core == 0, mine, got)
    second = jnp.where(core == 0, got, mine)
    return first, second


def placement():
    me = lax.axis_index("tensor")
    if not four_dp():
        return jnp.stack([me, 0, 0]).astype(jnp.int32)
    slots = [lax.axis_index("dp") ^ bit for bit in range(4)]
    return jnp.stack([me, lax.axis_index("pipe")] + slots).astype(jnp.int32)


def halves(block):
    other = swap_cores(block)
    if four_dp():
        return block, other
    both = join_halves(block, other, block.ndim - 2)
    both = both.reshape(block.shape[:-3] + (2, -1, block.shape[-1]))
    return both[..., :1, :, :], both[..., 1:, :, :]


def piece_halves(pieces):
    if four_dp():
        return pieces, tuple(swap_cores(piece) for piece in pieces)
    whole = pieces[:3] + (jnp.concatenate(pieces[3:], 0),)
    return tuple(zip(*(halves(piece) for piece in whole)))


def half_sums(mine, other):
    if four_dp():
        return mine, swap_cores(other)
    core = lax.axis_index("pipe")
    n = lax.axis_size("dp")
    full = jnp.concatenate([mine, other], -3)
    full = full.reshape(full.shape[:-3] + (n, 2, -1, full.shape[-1]))
    axis = full.ndim - 3
    kept = lax.dynamic_index_in_dim(full, core, axis, keepdims=False)
    return kept, swap_cores(lax.dynamic_index_in_dim(full, 1 - core, axis, keepdims=False))


def own_layer(first, second):
    core = lax.axis_index("pipe")
    mine = jnp.where(core == 0, first, second)
    other = swap_cores(jnp.where(core == 0, second, first))
    return join_halves(mine, other, 0).reshape(-1, first.shape[-1])


def norm_parts(stream):
    average = jnp.mean(stream, axis=-1, keepdims=True)
    centred = stream - average
    spread = jnp.mean(centred * centred, axis=-1, keepdims=True)
    scale = lax.rsqrt(spread + EPS)
    return centred * scale, scale


def norm_back(grad, unit, scale, gain):
    scaled = grad * gain
    mean_one = jnp.mean(scaled, axis=-1, keepdims=True)
    mean_two = jnp.mean(scaled * unit, axis=-1, keepdims=True)
    return scale * (scaled - mean_one - unit * mean_two)


def dot(left, right, dims):
    return lax.dot_general(left, right, (dims, ((), ())), preferred_element_type=F32)


NN = ((1,), (0,))
NT = ((1,), (1,))
TN = ((0,), (0,))


def cost(micros):
    return pl.CostEstimate(
        flops=int(micros * 1.15e9), bytes_accessed=int(micros * 3.6e6), transcendentals=0
    )


def slot_rows(place_ref, slot, half, rows):
    return pl.ds(pl.multiple_of((place_ref[2 + slot] * 2 + half) * rows, rows), rows)


def load_halves(place_ref, mine_ref, other_ref, whole_ref, low=0):
    core = place_ref[1]
    slots, rows = mine_ref.shape[0], mine_ref.shape[1]
    packed = mine_ref.shape[2] == 2 * whole_ref.shape[1]
    for slot in range(slots):
        for ref, half in ((mine_ref, core), (other_ref, 1 - core)):
            target = slot_rows(place_ref, low + slot, half, 2 * rows if packed else rows)
            whole_ref[target, :] = unpack(ref[slot]) if packed else ref[slot]


def store_halves(place_ref, whole_ref, mine_ref, other_ref, columns):
    core = place_ref[1]
    slots, rows = mine_ref.shape[0], mine_ref.shape[1]
    packed = mine_ref.shape[2] == 2 * whole_ref.shape[1]
    for slot in range(slots):
        for ref, half in ((mine_ref, core), (other_ref, 1 - core)):
            if packed:
                ref[slot] = pack(whole_ref[slot_rows(place_ref, slot, half, 2 * rows), :])
            else:
                ref[slot, :, columns] = whole_ref[slot_rows(place_ref, slot, half, rows), columns]


def load_pieces(place_ref, mine_refs, other_refs, whole_ref):
    for index, (mine_ref, other_ref) in enumerate(zip(mine_refs, other_refs)):
        low = mine_refs[3].shape[0] if index == 4 else 0
        load_halves(place_ref, mine_ref, other_ref, whole_ref.at[min(index, 3)], low)


def pack(block):
    half = block.shape[0] // 2
    return jnp.concatenate([block[:half], block[half:]], 1)


def unpack(block):
    half = block.shape[1] // 2
    return jnp.concatenate([block[:, :half], block[:, half:]], 0)


SCALARS = pl.BlockSpec(memory_space=pltpu.SMEM)
WHOLE = pl.BlockSpec(memory_space=pltpu.VMEM)


def window_start(block_id, rows, span):
    if span == rows:
        return 0
    start = jnp.clip(block_id * BLOCK - WINDOW // 2, 0, rows - span)
    return pl.multiple_of(start, WINDOW // 2)


def key_mask(start, span, first, last):
    keys = start + lax.broadcasted_iota(jnp.int32, (span, BLOCK), 0)
    return (keys >= first) & (keys < last)


def stack_kernel(split, block0_ref, block1_ref, block2_ref, block3_ref, upper_ref, lower_ref):
    for slot, ref in enumerate((block0_ref, block1_ref, block2_ref, block3_ref)):
        upper_ref[slot] = ref[:split]
        lower_ref[slot] = ref[split:]


def stack_blocks(blocks, split):
    rows, columns = blocks[0].shape
    return pl.pallas_call(
        functools.partial(stack_kernel, split),
        out_shape=(
            jax.ShapeDtypeStruct((4, split, columns), BF16),
            jax.ShapeDtypeStruct((4, rows - split, columns), BF16),
        ),
        in_specs=[WHOLE] * 4,
        compiler_params=pltpu.CompilerParams(vmem_limit_bytes=VMEM_BYTES),
        cost_estimate=cost(2),
        name="stack_blocks",
    )(*blocks)


def attend_kernel(
    span, place_ref, own_ref, one_ref, two_ref, head_ref, tail_ref, mine_ref, other_ref,
    cos_ref, sin_ref, first_ref, last_ref,
    mixed0_ref, mixed1_ref, mixed2_ref, mixed3_ref, queries_ref, keys_ref, values_ref, mass_ref,
    normed_ref, qkv_ref, outs_ref, key_rows, value_rows, proj, mixed_rows, bias, scores,
):
    width, rows = queries_ref.shape
    heads = width // HEAD_DIM
    half = HEAD_DIM // 2
    local = rows // 4
    me = place_ref[0]
    load_halves(place_ref, mine_ref, other_ref, qkv_ref)
    pieces = (
        (own_ref, 0, 0), (one_ref, 1, 0), (two_ref, 2, 0), (head_ref, 3, 0), (tail_ref, 3, local // 2)
    )
    for ref, bit, shift in pieces:
        low = pl.multiple_of((me ^ bit) * local + shift, local // 2)
        normed_ref[pl.ds(low, ref.shape[0]), :] = ref[...]
    proj[...] = dot(qkv_ref[...].T, normed_ref[...], NT)
    cosines, sines = cos_ref[...], sin_ref[...]
    for head in range(heads):
        low = head * HEAD_DIM
        for part, ref in ((0, queries_ref), (1, keys_ref)):
            upper = proj[part * width + low : part * width + low + half, :]
            lower = proj[part * width + low + half : part * width + low + HEAD_DIM, :]
            turned = jnp.concatenate(
                [upper * cosines - lower * sines, lower * cosines + upper * sines], 0
            )
            ref[low : low + HEAD_DIM, :] = turned.astype(BF16)
            if part == 1:
                key_rows[head] = turned.T.astype(BF16)
        value = proj[2 * width + low : 2 * width + low + HEAD_DIM, :]
        values_ref[low : low + HEAD_DIM, :] = value.astype(BF16)
        value_rows[head] = value.T.astype(BF16)
    mass_ref[...] = jnp.zeros_like(mass_ref)

    def block(block_id, carry):
        start = window_start(block_id, rows, span)
        columns = pl.ds(pl.multiple_of(block_id * BLOCK, BLOCK), BLOCK)
        mask = key_mask(start, span, first_ref[:, columns], last_ref[:, columns])
        bias[...] = jnp.where(mask, 0.0, -1e30)
        outs = []
        for head in range(heads):
            low = head * HEAD_DIM
            query = queries_ref[low : low + HEAD_DIM, columns] * BF16(HEAD_DIM**-0.5)
            top = jnp.full((1, BLOCK), -2e30, F32)
            for part in range(0, span, CHUNK):
                key = key_rows[head, pl.ds(start + part, CHUNK), :]
                score = dot(key, query, NN) + bias[part : part + CHUNK]
                scores[part : part + CHUNK] = score
                top = jnp.maximum(top, jnp.max(score, axis=0, keepdims=True))
            total = jnp.zeros((1, BLOCK), F32)
            out = jnp.zeros((HEAD_DIM, BLOCK), F32)
            for part in range(0, span, CHUNK):
                expos = jnp.exp(scores[part : part + CHUNK] - top)
                total += jnp.sum(expos, axis=0, keepdims=True)
                if span == rows:
                    value = values_ref[low : low + HEAD_DIM, part : part + CHUNK]
                else:
                    value = value_rows[head, pl.ds(start + part, CHUNK), :].T
                out += dot(value, expos.astype(BF16), NN)
            outs.append(out * (1.0 / total))
            mass_ref[head : head + 1, columns] = top + jnp.log(total)
        outs_ref[:, columns] = jnp.concatenate(outs, 0)
        mixed_rows[columns, :] = jnp.concatenate(outs, 0).T.astype(BF16)
        return carry

    lax.fori_loop(0, rows // BLOCK, block, 0)
    for bit, ref in enumerate((mixed0_ref, mixed1_ref, mixed2_ref, mixed3_ref)):
        low = pl.multiple_of((me ^ bit) * local, local)
        ref[...] = pack(mixed_rows[pl.ds(low, local), :])


def attend(place, pieces, mine, other, width, cosines, sines, first, last, is_local):
    local, model = pieces[0].shape
    rows = 4 * local
    heads = width // HEAD_DIM
    span = min(rows, BLOCK + WINDOW) if is_local else rows
    shape = jax.ShapeDtypeStruct((width, rows), BF16)
    mixed = jax.ShapeDtypeStruct((local // 2, 2 * width), BF16)
    return pl.pallas_call(
        functools.partial(attend_kernel, span),
        out_shape=(
            mixed, mixed, mixed, mixed, shape, shape, shape, jax.ShapeDtypeStruct((8, rows), F32),
            jax.ShapeDtypeStruct((rows, model), BF16),
            jax.ShapeDtypeStruct((model, 3 * width), BF16),
            jax.ShapeDtypeStruct((width, rows), F32),
        ),
        in_specs=[SCALARS] + [WHOLE] * 11,
        scratch_shapes=[
            pltpu.VMEM((heads, rows, HEAD_DIM), BF16),
            pltpu.VMEM((heads, rows, HEAD_DIM), BF16),
            pltpu.VMEM((3 * width, rows), F32),
            pltpu.VMEM((rows, width), BF16),
            pltpu.VMEM((span, BLOCK), F32),
            pltpu.VMEM((span, BLOCK), F32),
        ],
        compiler_params=pltpu.CompilerParams(vmem_limit_bytes=VMEM_BYTES),
        cost_estimate=cost(11 if is_local else 20),
        name="attend_local" if is_local else "attend_global",
    )(place, *pieces, mine, other, cosines, sines, first, last)


def attend_back_kernel(
    span, place_ref, queries_ref, keys_ref, values_ref, mass_ref,
    grad0_ref, grad1_ref, grad2_ref, grad3_ref,
    cos_ref, sin_ref, first_ref, last_ref, qkv_ref, outs_ref,
    own_ref, one0_ref, one1_ref, two0_ref, two1_ref, far0_ref, far1_ref, out_ref,
    query_rows, key_rows, value_rows, grad_cols, grad_all, grad_rows, sum_q, sum_k, sum_v, flat, bias,
    probs_low, scores_low,
):
    width, rows = queries_ref.shape
    heads = width // HEAD_DIM
    half = HEAD_DIM // 2
    local = rows // 4
    scale = HEAD_DIM**-0.5
    me = place_ref[0]
    for bit, ref in enumerate((grad0_ref, grad1_ref, grad2_ref, grad3_ref)):
        low = pl.multiple_of((me ^ bit) * local, local)
        grad_all[pl.ds(low, local), :] = unpack(ref[...])
    grad_cols[...] = grad_all[...].T
    for head in range(heads):
        cut = slice(head * HEAD_DIM, (head + 1) * HEAD_DIM)
        query_rows[head] = (queries_ref[cut, :] * BF16(scale)).T
        key_rows[head] = keys_ref[cut, :].T
        value_rows[head] = values_ref[cut, :].T
        grad_rows[head] = grad_all[:, cut]
    sum_k[...] = jnp.zeros_like(sum_k)
    sum_v[...] = jnp.zeros_like(sum_v)

    def block(block_id, carry):
        start = window_start(block_id, rows, span)
        columns = pl.ds(pl.multiple_of(block_id * BLOCK, BLOCK), BLOCK)
        mask = key_mask(start, span, first_ref[:, columns], last_ref[:, columns])
        bias[...] = jnp.where(mask, 0.0, -1e30)
        for head in range(heads):
            cut = slice(head * HEAD_DIM, (head + 1) * HEAD_DIM)
            query = queries_ref[cut, columns] * BF16(scale)
            grad = grad_cols[cut, columns]
            mass = mass_ref[head : head + 1, columns]
            inner = jnp.sum(grad.astype(F32) * outs_ref[cut, columns], axis=0, keepdims=True)
            for part in range(0, span, CHUNK):
                window = pl.ds(start + part, CHUNK)
                scores = dot(key_rows[head, window, :], query, NN)
                probs = jnp.exp(scores - mass + bias[part : part + CHUNK])
                grad_probs = dot(value_rows[head, window, :], grad, NN)
                probs_low[part : part + CHUNK] = probs.astype(BF16)
                scores_low[part : part + CHUNK] = (probs * (grad_probs - inner)).astype(BF16)
            window = pl.ds(start, span)
            key_cols = keys_ref[cut, :] if span == rows else key_rows[head, window, :].T
            sum_v[head, window, :] += dot(probs_low[...], grad_rows[head, columns, :], NN)
            sum_k[head, window, :] += dot(scores_low[...], query_rows[head, columns, :], NN)
            sum_q[cut, columns] = dot(key_cols, scores_low[...], NN)
        return carry

    lax.fori_loop(0, rows // BLOCK, block, 0)
    cosines, sines = cos_ref[...], sin_ref[...]
    for head in range(heads):
        low = head * HEAD_DIM
        turned_q = sum_q[low : low + HEAD_DIM, :] * scale
        for part, turned in ((0, turned_q), (1, sum_k[head].T)):
            upper, lower = turned[:half], turned[half:]
            raw = jnp.concatenate(
                [upper * cosines + lower * sines, lower * cosines - upper * sines], 0
            )
            flat[part * width + low : part * width + low + HEAD_DIM, :] = raw.astype(BF16)
        flat[2 * width + low : 2 * width + low + HEAD_DIM, :] = sum_v[head].T.astype(BF16)
    out_ref[...] = flat[...].T
    targets = ((own_ref,), (one0_ref, one1_ref), (two0_ref, two1_ref), (far0_ref, far1_ref))
    for bit, refs in enumerate(targets):
        low = pl.multiple_of((me ^ bit) * local, local)
        part = dot(out_ref[pl.ds(low, local), :], qkv_ref[...], NT).astype(BF16)
        size = local // len(refs)
        for index, ref in enumerate(refs):
            ref[...] = part[index * size : (index + 1) * size]


def attend_back(
    place, queries, keys, values, mass, grads, cosines, sines, first, last, qkv, outs, is_local
):
    width, rows = queries.shape
    model = qkv.shape[0]
    heads = width // HEAD_DIM
    span = min(rows, BLOCK + WINDOW) if is_local else rows
    low_rows = pltpu.VMEM((heads, rows, HEAD_DIM), BF16)
    sums = pltpu.VMEM((heads, rows, HEAD_DIM), F32)
    part = jax.ShapeDtypeStruct((rows // 4, model), BF16)
    half = jax.ShapeDtypeStruct((rows // 8, model), BF16)
    return pl.pallas_call(
        functools.partial(attend_back_kernel, span),
        out_shape=(part,) + (half,) * 6 + (jax.ShapeDtypeStruct((rows, 3 * width), BF16),),
        in_specs=[SCALARS] + [WHOLE] * 14,
        scratch_shapes=[
            low_rows, low_rows, low_rows, pltpu.VMEM((width, rows), BF16),
            pltpu.VMEM((rows, width), BF16), low_rows,
            pltpu.VMEM((width, rows), F32), sums, sums, pltpu.VMEM((3 * width, rows), BF16),
            pltpu.VMEM((span, BLOCK), F32), pltpu.VMEM((span, BLOCK), BF16),
            pltpu.VMEM((span, BLOCK), BF16),
        ],
        compiler_params=pltpu.CompilerParams(vmem_limit_bytes=VMEM_BYTES),
        cost_estimate=cost(11 if is_local else 21),
        name="attend_back_local" if is_local else "attend_back_global",
    )(place, queries, keys, values, mass, *grads, cosines, sines, first, last, qkv, outs)


def qkv_grad_kernel(place_ref, normed_ref, grad_ref, qkv_ref, mine_ref, other_ref, gain_ref, whole):
    grad = dot(normed_ref[...].T, grad_ref[...], NN)
    gain_ref[...] = jnp.sum(grad * qkv_ref[...].astype(F32), axis=1, keepdims=True)
    whole[...] = grad.astype(BF16)
    store_halves(place_ref, whole, mine_ref, other_ref, slice(None))


def qkv_grad(place, normed, grad, qkv, shape):
    part = jax.ShapeDtypeStruct(shape, BF16)
    return pl.pallas_call(
        qkv_grad_kernel,
        out_shape=(part, part, jax.ShapeDtypeStruct((qkv.shape[0], 1), F32)),
        in_specs=[SCALARS, WHOLE, WHOLE, WHOLE],
        scratch_shapes=[pltpu.VMEM((normed.shape[1], grad.shape[1]), BF16)],
        compiler_params=pltpu.CompilerParams(vmem_limit_bytes=VMEM_BYTES),
        cost_estimate=cost(4),
        name="qkv_grad",
    )(place, normed, grad, qkv)


def erf_parts(gate):
    cumulative = 0.5 * (1.0 + lax.erf(gate * 0.7071067811865476))
    density = 0.3989422804014327 * jnp.exp(-0.5 * gate * gate)
    return cumulative, density


def forward_step(pair, mixed_refs, in_ref, gain_ref, mid_ref, sums, mats):
    parts = mats.shape[0]
    width = mixed_refs[0].shape[1] // 2
    units = pair // 2
    mid = in_ref[...].astype(F32)
    for part, ref in enumerate(mixed_refs):
        mid += dot(unpack(ref[...]), mats[part, :, pair : pair + width], NT)
    mid_ref[...] = mid
    sums[...] = mid
    normed = (norm_parts(mid)[0] * gain_ref[...]).astype(BF16)

    def feed(part, carry):
        gate_up = dot(normed, mats[part, :, :pair], NN)
        gate = gate_up[:, :units]
        hidden = (gate * erf_parts(gate)[0] * gate_up[:, units:]).astype(BF16)
        sums[...] += dot(hidden, mats[part, :, pair + width : pair + width + units], NT)
        return carry

    lax.fori_loop(0, parts, feed, 0)


def token_kernel(pair, place_ref, mixed0_ref, mixed1_ref, mixed2_ref, mixed3_ref, in_ref, *refs):
    pieces = (len(refs) - 7) // 2
    mine_refs, other_refs = refs[:pieces], refs[pieces : 2 * pieces]
    gain_ref, next_ref, mid_ref, out_ref, normed_ref, sums, mats = refs[2 * pieces :]
    load_pieces(place_ref, mine_refs, other_refs, mats)
    mixed_refs = (mixed0_ref, mixed1_ref, mixed2_ref, mixed3_ref)
    forward_step(pair, mixed_refs, in_ref, gain_ref, mid_ref, sums, mats)
    low = sums[...].astype(BF16)
    out_ref[...] = low
    normed_ref[...] = (norm_parts(low.astype(F32))[0] * next_ref[...]).astype(BF16)


def token_forward(place, mixed, layer_in, mine, other, gain, next_gain, pair):
    shape = layer_in.shape
    return pl.pallas_call(
        functools.partial(token_kernel, pair),
        out_shape=(
            jax.ShapeDtypeStruct(shape, F32),
            jax.ShapeDtypeStruct(shape, BF16),
            jax.ShapeDtypeStruct(shape, BF16),
        ),
        in_specs=[SCALARS] + [WHOLE] * (7 + 2 * len(mine)),
        scratch_shapes=[
            pltpu.VMEM(shape, F32),
            pltpu.VMEM((4, shape[1], mine[0].shape[2]), BF16),
        ],
        compiler_params=pltpu.CompilerParams(vmem_limit_bytes=VMEM_BYTES),
        cost_estimate=cost(10),
        name="token_forward",
    )(place, *mixed, layer_in, *mine, *other, gain, next_gain)


def token_back_kernel(
    pair, place_ref, grad_ref, mid_ref, mixed0_ref, mixed1_ref, mixed2_ref, mixed3_ref, *refs
):
    pieces = (len(refs) - 12) // 2
    mats = refs[-2]
    load_pieces(place_ref, refs[:pieces], refs[pieces : 2 * pieces], mats)
    mixed_refs = (mixed0_ref, mixed1_ref, mixed2_ref, mixed3_ref)
    back_step(pair, place_ref, grad_ref, mid_ref, mixed_refs, *refs[2 * pieces :])


def token_last_kernel(
    pair, place_ref, grad_ref, in_ref, mixed0_ref, mixed1_ref, mixed2_ref, mixed3_ref, *refs
):
    pieces = (len(refs) - 14) // 2
    mats, sums = refs[-3], refs[-4]
    load_pieces(place_ref, refs[:pieces], refs[pieces : 2 * pieces], mats)
    mixed_refs = (mixed0_ref, mixed1_ref, mixed2_ref, mixed3_ref)
    rest = refs[2 * pieces :]
    gain_ref, out_ref, mid = rest[0], rest[9], rest[13]
    forward_step(pair, mixed_refs, in_ref, gain_ref, mid, sums, mats)
    out_ref[...] = sums[...].astype(BF16)
    back_step(pair, place_ref, grad_ref, mid, mixed_refs, *rest[:9], *rest[10:13])


def back_step(
    pair, place_ref, grad_ref, mid_ref, mixed_refs, gain_ref, mine_grad_ref, other_grad_ref,
    mixed_grad0_ref, mixed_grad1_ref, mixed_grad2_ref, mixed_grad3_ref, grad_mid_ref,
    gain_grad_ref, sums, mats, grads,
):
    parts = mats.shape[0]
    width = mixed_refs[0].shape[1] // 2
    units = pair // 2
    grad = grad_ref[...].astype(F32)
    grad_low = grad.astype(BF16)
    grad_flip = grad.T.astype(BF16)
    unit, scale = norm_parts(mid_ref[...])
    gained = unit * gain_ref[...]
    normed = gained.astype(BF16)
    normed_flip = gained.T.astype(BF16)
    sums[...] = jnp.zeros_like(sums)
    used = pair + width + units
    grads[:, used:] = jnp.zeros((grads.shape[0], grads.shape[1] - used), BF16)

    def feed(part, carry):
        gate_up = dot(normed, mats[part, :, :pair], NN)
        gate, up = gate_up[:, :units], gate_up[:, units:]
        cumulative, density = erf_parts(gate)
        gelu = gate * cumulative
        hidden = (gelu * up).astype(BF16)
        grad_hidden = dot(grad_low, mats[part, :, pair + width : pair + width + units], NN)
        grad_gate = grad_hidden * up * (cumulative + gate * density)
        grad_up = grad_hidden * gelu
        grad_pair = jnp.concatenate([grad_gate, grad_up], 1).astype(BF16)
        grads[:, pair + width : used] = dot(grad_flip, hidden, NN).astype(BF16)
        grads[:, :pair] = dot(normed_flip, grad_pair, NN).astype(BF16)
        for columns in (slice(0, pair), slice(pair + width, None)):
            store_halves(
                place_ref, grads, mine_grad_ref.at[part], other_grad_ref.at[part], columns
            )
        sums[...] += dot(grad_pair, mats[part, :, :pair], NT)
        return carry

    lax.fori_loop(0, parts, feed, 0)
    grad_normed = sums[...]
    gain_grad_ref[...] = jnp.sum(grad_normed * unit, axis=0, keepdims=True)
    grad_mid = grad + norm_back(grad_normed, unit, scale, gain_ref[...])
    grad_mid_ref[...] = grad_mid
    mid_low = grad_mid.astype(BF16)
    mid_flip = grad_mid.T.astype(BF16)
    mixed_grad_refs = (mixed_grad0_ref, mixed_grad1_ref, mixed_grad2_ref, mixed_grad3_ref)
    for part in range(parts):
        weight = mats[part, :, pair : pair + width]
        mixed_grad_refs[part][...] = pack(dot(mid_low, weight, NN).astype(BF16))
        grads[:, pair : pair + width] = dot(mid_flip, unpack(mixed_refs[part][...]), NN).astype(BF16)
        store_halves(
            place_ref, grads, mine_grad_ref.at[part], other_grad_ref.at[part],
            slice(pair, pair + width),
        )


def token_back(place, grad, mid, mixed, mine, other, gain, pair):
    shape = mine[0].shape
    half = jax.ShapeDtypeStruct((4,) + shape, BF16)
    mixed_grad = jax.ShapeDtypeStruct(mixed[0].shape, BF16)
    return pl.pallas_call(
        functools.partial(token_back_kernel, pair),
        out_shape=(
            half, half, mixed_grad, mixed_grad, mixed_grad, mixed_grad,
            jax.ShapeDtypeStruct(mid.shape, F32),
            jax.ShapeDtypeStruct((1, mid.shape[1]), F32),
        ),
        in_specs=[SCALARS] + [WHOLE] * (7 + 2 * len(mine)),
        scratch_shapes=[
            pltpu.VMEM(mid.shape, F32),
            pltpu.VMEM((4, mid.shape[1], shape[2]), BF16),
            pltpu.VMEM((mid.shape[1], shape[2]), BF16),
        ],
        compiler_params=pltpu.CompilerParams(vmem_limit_bytes=VMEM_BYTES),
        cost_estimate=cost(20),
        name="token_back",
    )(place, grad, mid, *mixed, *mine, *other, gain)


def token_last(place, grad, layer_in, mixed, mine, other, gain, pair):
    shape, rows = mine[0].shape, layer_in.shape
    half = jax.ShapeDtypeStruct((4,) + shape, BF16)
    mixed_grad = jax.ShapeDtypeStruct(mixed[0].shape, BF16)
    return pl.pallas_call(
        functools.partial(token_last_kernel, pair),
        out_shape=(
            half, half, mixed_grad, mixed_grad, mixed_grad, mixed_grad,
            jax.ShapeDtypeStruct(rows, F32),
            jax.ShapeDtypeStruct((1, rows[1]), F32),
            jax.ShapeDtypeStruct(rows, BF16),
        ),
        in_specs=[SCALARS] + [WHOLE] * (7 + 2 * len(mine)),
        scratch_shapes=[
            pltpu.VMEM(rows, F32),
            pltpu.VMEM((4, rows[1], shape[2]), BF16),
            pltpu.VMEM((rows[1], shape[2]), BF16),
            pltpu.VMEM(rows, F32),
        ],
        compiler_params=pltpu.CompilerParams(vmem_limit_bytes=VMEM_BYTES),
        cost_estimate=cost(20),
        name="token_last",
    )(place, grad, layer_in, *mixed, *mine, *other, gain)


def frequencies(theta_base, half_dim):
    return theta_base ** (-(jnp.arange(half_dim, dtype=F32) * 2.0) / (2.0 * half_dim))


def sequences(seq_lengths, rows):
    seq_ends = jnp.cumsum(seq_lengths)
    positions = jnp.arange(rows, dtype=jnp.int32)
    seq_of = jnp.sum((positions[:, None] >= seq_ends[None, :]).astype(jnp.int32), axis=1)
    matches = jnp.arange(seq_lengths.shape[0], dtype=jnp.int32)[None, :] == seq_of[:, None]
    last = jnp.sum(jnp.where(matches, seq_ends[None, :], 0), axis=1)
    first = jnp.sum(jnp.where(matches, (seq_ends - seq_lengths)[None, :], 0), axis=1)
    return first[None], last[None], positions[None]


def body(
    tokens, lengths, qkv_weight, out_weight, gate_up_weight, down_weight, gains, out_cotangent
):
    core = lax.axis_index("pipe")
    model = tokens.shape[-1]
    local_rows = tokens.shape[2]
    rows = 4 * local_rows
    shard_rows = qkv_weight.shape[1]
    width = qkv_weight.shape[3]
    pair = 2 * gate_up_weight.shape[3]

    stream = take(tokens[0], core)
    cotangent = take(out_cotangent[0], core)
    first, last, positions = sequences(take(lengths[0], core), rows)
    bounds = (
        (jnp.maximum(first, positions - WINDOW // 2), jnp.minimum(last, positions + WINDOW // 2 + 1)),
        (first, last),
    )
    tables = []
    for base in (10000.0, 160000.0):
        turns = frequencies(base, HEAD_DIM // 2)[:, None] * (positions - first).astype(F32)
        tables.append((jnp.cos(turns), jnp.sin(turns)))

    other_gains = swap_cores(gains[0])
    gain_rows = (
        jnp.where(core == 0, gains[0], other_gains)[None],
        jnp.where(core == 0, other_gains, gains[0])[None],
    )
    place = placement()

    normed = (norm_parts(stream.astype(F32))[0] * gain_rows[0][:, :model]).astype(BF16)
    mats = jnp.concatenate(
        [gate_up_weight[0].reshape(shard_rows, pair), out_weight[0].T, down_weight[0].T], 1
    )
    spare = 6 * width - mats.shape[1]
    mats = jnp.pad(mats, ((0, 0), (0, spare))).reshape(2, shard_rows // 2, 6 * width)
    qkv = qkv_weight[0].reshape(2, 2, shard_rows // 4, 3 * width)
    qkv = jnp.concatenate([qkv[:, 0], qkv[:, 1]], -1)
    first_half, second_half = layer_halves(
        jnp.concatenate([mats, qkv], 1).reshape(-1, 6 * width)
    )
    split = shard_rows // 2
    total = first_half.shape[0]
    qkv_shape = (4, split // 2, 6 * width) if four_dp() else (1, model // 2, 3 * width)

    def split_blocks(blocks):
        if four_dp():
            upper, lower = stack_blocks(blocks, split)
            return upper, halves(lower)
        upper, lower = blocks[0][:, :split], blocks[0][:, split:]
        lower = jnp.concatenate([lower[..., : 3 * width], lower[..., 3 * width :]], 1)
        return upper, halves(lower)

    normed, first_half, second_half = after((normed, first_half, second_half))
    near, blocks = to_neighbours(normed), gather_dp(first_half)
    far = to_far(*after(near))
    far, blocks = after((far, blocks))
    mats_first, qkv_first = split_blocks(blocks)
    mats_first, second_half = after((mats_first, second_half), qkv_first)
    pieces = (normed,) + near + far
    saved_attend = [None, None]
    saved_token = [None, None]

    mats_near = to_neighbours(mats_first)
    second_blocks = gather_dp(second_half)
    second_blocks, second_late = second_blocks[:3], second_blocks[3:]
    *mixed, queries, keys, values, mass, normed_full, qkv, outs = attend(
        place, pieces, *qkv_first, width, *tables[0], *bounds[0], True
    )
    saved_attend[0] = (queries, keys, values, mass, normed_full, qkv, outs)
    mixed, mats_first, mats_near, second_blocks = after(
        (mixed, mats_first, mats_near, second_blocks)
    )
    mixed, mats_far = after((swap_tensor(mixed), to_far(*mats_near)))
    mats = piece_halves((mats_first,) + mats_near + mats_far)
    mid, first_out, normed = token_forward(
        place, mixed, stream, *mats, gain_rows[0][:, model:], gain_rows[1][:, :model], pair
    )
    saved_token[0] = (mid, mixed) + mats

    near, second_late = after((to_neighbours(normed), second_late))
    blocks = second_blocks + second_late
    mats_second, qkv_second = split_blocks(blocks)
    far, qkv_second = after((to_far(*near), qkv_second))
    pieces = (normed,) + near + far
    mats_second = after(mats_second, far)
    second_near = to_neighbours(mats_second)
    *mixed, queries, keys, values, mass, normed_full, qkv, outs = attend(
        place, pieces, *qkv_second, width, *tables[1], *bounds[1], False
    )
    saved_attend[1] = (queries, keys, values, mass, normed_full, qkv, outs)
    mixed, second_near = after((mixed, second_near))
    mixed, second_far = after((swap_tensor(mixed), to_far(*second_near)))
    mats = piece_halves((mats_second,) + second_near + second_far)
    def token_step(layer, grad):
        mid, mixed, mine, other = saved_token[layer]
        return token_back(
            place, grad, mid, mixed, mine, other, gain_rows[layer][:, model:], pair
        )

    def attend_step(layer, mixed_grad):
        queries, keys, values, mass, _, qkv, outs = saved_attend[layer]
        return attend_back(
            place, queries, keys, values, mass, mixed_grad, *tables[layer], *bounds[layer],
            qkv, outs, layer == 0,
        )

    def weight_step(layer, grad_projected):
        normed_full, qkv = saved_attend[layer][4:6]
        mine, other, gain_sum = qkv_grad(
            place, normed_full, grad_projected, qkv, qkv_shape
        )
        return half_sums(mine, other) + (gain_sum.reshape(1, model) / gain_rows[layer][:, :model],)

    def norm_step(layer, grad_normed, grad_mid):
        unit, scale = norm_parts((stream, first_out)[layer].astype(F32))
        return grad_mid + norm_back(grad_normed, unit, scale, gain_rows[layer][:, :model])

    def qkv_blocks(kept, came):
        return [add_low(kept[slot], came[slot]) for slot in range(kept.shape[0])]

    mine_grad, other_grad, *mixed_grad, grad_mid, gain_mlp, second_out = token_last(
        place, cotangent, first_out, mixed, *mats, gain_rows[1][:, model:], pair
    )
    mixed_grad = swap_tensor(mixed_grad)
    kept, came = half_sums(mine_grad, other_grad)
    mixed_grad, kept, came = after((mixed_grad, kept, came))
    far = far_terms(add_low(kept[3], came[3]))
    *parts, grad_projected = attend_step(1, mixed_grad)
    parts, grad_projected, far = after((parts, grad_projected, far))
    early = rows_early(parts)
    pair_terms = near_terms(add_low(kept[1], came[1]), add_low(kept[2], came[2]), *far)
    qkv_kept, qkv_came, gain_attn = weight_step(1, grad_projected)
    second_gain = jnp.concatenate([gain_attn, gain_mlp], 1)
    late = rows_late(parts, early)
    late, pair_terms, qkv_kept, qkv_came = after((late, pair_terms, qkv_kept, qkv_came), early)
    near = to_near(pair_terms)
    grad = norm_step(1, rows_sum(parts, early, late), grad_mid).astype(BF16)
    second_grad = grad.astype(F32)

    second_kept, second_came, second_qkv = kept, came, qkv_blocks(qkv_kept, qkv_came)
    mine_grad, other_grad, *mixed_grad, grad_mid, gain_mlp = token_step(0, grad)
    mixed_grad, other_grad, near = after((mixed_grad, other_grad, near))
    mixed_grad = swap_tensor(mixed_grad)
    kept, came = half_sums(mine_grad, other_grad)
    second = slot_sums(second_kept, second_came, near)
    if four_dp():
        second = [jnp.concatenate(block, 0) for block in zip(second, second_qkv)]
    mixed_grad, kept, came, second = after((mixed_grad, kept, came, second))
    far = far_terms(add_low(kept[3], came[3]))
    came_early = scatter_dp(second, (1, 2))
    *parts, grad_projected = attend_step(0, mixed_grad)
    parts, grad_projected, far, kept, came, came_early, second = after(
        (parts, grad_projected, far, kept, came, came_early, second)
    )

    pair_terms = near_terms(add_low(kept[1], came[1]), add_low(kept[2], came[2]), *far)
    pair_terms, grad_projected = after((pair_terms, grad_projected))
    near, came_late = to_near(pair_terms), scatter_dp(second, (3,))
    qkv_kept, qkv_came, gain_attn = weight_step(0, grad_projected)
    first_gain = jnp.concatenate([gain_attn, gain_mlp], 1)
    gain_sum = jnp.where(core == 0, first_gain, second_gain)
    gain_sum += swap_cores(jnp.where(core == 0, second_gain, first_gain))
    first_qkv = qkv_blocks(qkv_kept, qkv_came)
    near, came_late, parts, gain_sum, first_qkv = after(
        (near, came_late, parts, gain_sum, first_qkv)
    )
    second_came = came_early + came_late
    first = slot_sums(kept, came, near)
    if four_dp():
        first = [jnp.concatenate(block, 0) for block in zip(first, first_qkv)]
    first_came = scatter_dp(first)
    gain_sum += to_mate(gain_sum, 1)
    rows_far = (to_mate(parts[5], 1), to_mate(parts[6], 2))
    rows_far, parts, gain_sum = after((rows_far, parts, gain_sum))
    rows_near = to_near(
        (
            jnp.concatenate([parts[1], add_low(parts[2], rows_far[1])], 0),
            jnp.concatenate([add_low(parts[3], rows_far[0]), parts[4]], 0),
        )
    )
    gain_sum += to_mate(gain_sum, 2)
    gain_sum, first_came = after((gain_sum, first_came))
    chunk = model * 2 // (4 * lax.axis_size("dp"))
    me = lax.axis_index("dp") * 4 + lax.axis_index("tensor")
    if four_dp():
        gain_sum += to_peer(gain_sum, 1)
        gain_sum += to_peer(gain_sum, 2)
    else:
        gain_sum = lax.psum(gain_sum, "dp")
    gain_part = lax.dynamic_slice_in_dim(gain_sum[0], me * chunk, chunk, 0)
    first_grad = norm_step(0, add_up(parts[0], *rows_near), grad_mid)
    input_grads = (first_grad, second_grad)

    if four_dp():
        total_grad = own_layer(scatter_sum(first, first_came), scatter_sum(second, second_came))
        total_grad = total_grad.reshape(2, total, 6 * width)
        mats_total = total_grad[:, :split].reshape(shard_rows, 6 * width)
        qkv_total = total_grad[:, split:].reshape(-1, 6 * width)
    else:
        mats_total = own_layer(scatter_sum(first, ()), scatter_sum(second, ()))
        qkv_total = own_layer(scatter_sum(first_qkv, ()), scatter_sum(second_qkv, ()))
    if four_dp():
        qkv_total = qkv_total.reshape(2, shard_rows // 4, 2, 3 * width)
        qkv_total = jnp.moveaxis(qkv_total, 2, 1).reshape(shard_rows, 3 * width)

    activations = join_halves(
        jnp.where(core == 0, first_out, second_out),
        swap_cores(jnp.where(core == 0, second_out, first_out)),
        0,
    )
    grads_in = join_halves(
        jnp.where(core == 0, input_grads[0], input_grads[1]),
        swap_cores(jnp.where(core == 0, input_grads[1], input_grads[0])),
        0,
    )
    return (
        activations[None, None],
        grads_in[None, None],
        qkv_total.reshape(qkv_weight.shape),
        mats_total[:, pair : pair + width].T[None],
        mats_total[:, :pair].reshape(gate_up_weight.shape),
        mats_total[:, pair + width : pair + width + pair // 2].T[None],
        gain_part[None],
    )


def solution(mesh):
    return jax.shard_map(
        body,
        mesh=mesh,
        in_specs=(
            P("dp", None, "tensor", None),
            P("dp", None, None),
            P("pipe", "dp", None, "tensor"),
            P("pipe", "tensor", "dp"),
            P("pipe", "dp", None, "tensor"),
            P("pipe", "tensor", "dp"),
            P("pipe", None),
            P("dp", None, "tensor", None),
        ),
        out_specs=(
            P("pipe", "dp", None, "tensor", None),
            P("pipe", "dp", None, "tensor", None),
            P("pipe", "dp", None, "tensor"),
            P("pipe", "tensor", "dp"),
            P("pipe", "dp", None, "tensor"),
            P("pipe", "tensor", "dp"),
            P("pipe", ("dp", "tensor")),
        ),
        check_vma=False,
    )
```

```python
import functools

import jax
import jax.numpy as jnp
from jax import lax
from jax.experimental import pallas as pl
from jax.experimental.pallas import tpu as pltpu
from jax.sharding import PartitionSpec as P

HEAD_DIM = 64
WINDOW = 128
EPS = 1e-05
BLOCK = 256
CHUNK = 128
BF16 = jnp.bfloat16
F32 = jnp.float32
VMEM_BYTES = 36 * 1024 * 1024


def swap_cores(block):
    return lax.ppermute(block, "pipe", [(0, 1), (1, 0)])


def to_mate(block, bit):
    size = lax.axis_size("tensor")
    return lax.ppermute(block, "tensor", [(i, i ^ bit) for i in range(size)])


def put(buffer, block, index):
    return lax.dynamic_update_slice_in_dim(buffer, block[None], index, 0)


def take(buffer, index):
    return lax.dynamic_index_in_dim(buffer, index, 0, keepdims=False)


def to_neighbours(block):
    return to_mate(block, 1), to_mate(block, 2)


def to_far(one, two):
    half = one.shape[0] // 2
    return to_mate(two[:half], 1), to_mate(one[half:], 2)


def after(blocks, *earlier):
    return lax.optimization_barrier((blocks, earlier))[0]


def far_terms(far):
    half = far.shape[0] // 2
    return to_mate(far[:half], 1), to_mate(far[half:], 2)


def near_terms(one, two, head, tail):
    half = head.shape[0]
    one = jnp.concatenate([one[:half], add_low(one[half:], tail)], 0)
    two = jnp.concatenate([add_low(two[:half], head), two[half:]], 0)
    return one, two


def rows_early(parts):
    _, one0, _, _, two1, far0, far1 = parts
    return to_mate(far0, 1), to_mate(far1, 2), to_mate(one0, 1), to_mate(two1, 2)


def rows_late(parts, early):
    _, _, one1, two0, _, _, _ = parts
    return to_mate(add_low(one1, early[1]), 1), to_mate(add_low(two0, early[0]), 2)


def rows_sum(parts, early, late):
    half = early[2].shape[0]
    upper = add_up(parts[0][:half], early[2], late[1])
    lower = add_up(parts[0][half:], late[0], early[3])
    return jnp.concatenate([upper, lower], 0)


def to_near(pair):
    return to_mate(pair[0], 1), to_mate(pair[1], 2)


def slot_sums(kept, came, near):
    return [
        add_up(kept[0][slot], came[0][slot], near[0][slot], near[1][slot]).astype(BF16)
        for slot in range(kept.shape[1])
    ]


def add_low(left, right):
    return (left.astype(F32) + right.astype(F32)).astype(BF16)


def add_up(*terms):
    return sum(term.astype(F32) for term in terms)


def swap_tensor(blocks):
    return (blocks[0],) + tuple(to_mate(blocks[bit], bit) for bit in (1, 2, 3))


def four_dp():
    return lax.axis_size("dp") == 4


def to_peer(block, bit):
    return lax.ppermute(block, "dp", [(i, i ^ bit) for i in range(4)])


def gather_dp(block):
    if four_dp():
        return [block] + [to_peer(block, bit) for bit in (1, 2, 3)]
    return [lax.all_gather(block, "dp", axis=0)]


def scatter_dp(blocks, bits=(1, 2, 3)):
    return tuple(to_peer(blocks[bit], bit) for bit in bits) if four_dp() else ()


def scatter_sum(blocks, came):
    if four_dp():
        return add_up(blocks[0], *came)
    return lax.psum_scatter(
        jnp.stack(blocks), "dp", scatter_dimension=0, tiled=False
    ).astype(F32)


def join_halves(mine, other, axis):
    core = lax.axis_index("pipe")
    out = jnp.stack([mine, other], axis)
    return jnp.where(core == 0, out, jnp.stack([other, mine], axis))


def layer_halves(shard):
    core = lax.axis_index("pipe")
    rows = shard.shape[0] // 2
    mine = lax.dynamic_slice_in_dim(shard, core * rows, rows, 0)
    other = lax.dynamic_slice_in_dim(shard, (1 - core) * rows, rows, 0)
    got = swap_cores(other)
    first = jnp.where(core == 0, mine, got)
    second = jnp.where(core == 0, got, mine)
    return first, second


def placement():
    me = lax.axis_index("tensor")
    if not four_dp():
        return jnp.stack([me, 0, 0]).astype(jnp.int32)
    slots = [lax.axis_index("dp") ^ bit for bit in range(4)]
    return jnp.stack([me, lax.axis_index("pipe")] + slots).astype(jnp.int32)


def halves(block):
    other = swap_cores(block)
    if four_dp():
        return block, other
    both = join_halves(block, other, block.ndim - 2)
    both = both.reshape(block.shape[:-3] + (2, -1, block.shape[-1]))
    return both[..., :1, :, :], both[..., 1:, :, :]


def piece_halves(pieces):
    if four_dp():
        return pieces, tuple(swap_cores(piece) for piece in pieces)
    whole = pieces[:3] + (jnp.concatenate(pieces[3:], 0),)
    return tuple(zip(*(halves(piece) for piece in whole)))


def half_sums(mine, other):
    if four_dp():
        return mine, swap_cores(other)
    core = lax.axis_index("pipe")
    n = lax.axis_size("dp")
    full = jnp.concatenate([mine, other], -3)
    full = full.reshape(full.shape[:-3] + (n, 2, -1, full.shape[-1]))
    axis = full.ndim - 3
    kept = lax.dynamic_index_in_dim(full, core, axis, keepdims=False)
    return kept, swap_cores(lax.dynamic_index_in_dim(full, 1 - core, axis, keepdims=False))


def own_layer(first, second):
    core = lax.axis_index("pipe")
    mine = jnp.where(core == 0, first, second)
    other = swap_cores(jnp.where(core == 0, second, first))
    return join_halves(mine, other, 0).reshape(-1, first.shape[-1])


def norm_parts(stream):
    average = jnp.mean(stream, axis=-1, keepdims=True)
    centred = stream - average
    spread = jnp.mean(centred * centred, axis=-1, keepdims=True)
    scale = lax.rsqrt(spread + EPS)
    return centred * scale, scale


def norm_back(grad, unit, scale, gain):
    scaled = grad * gain
    mean_one = jnp.mean(scaled, axis=-1, keepdims=True)
    mean_two = jnp.mean(scaled * unit, axis=-1, keepdims=True)
    return scale * (scaled - mean_one - unit * mean_two)


def dot(left, right, dims):
    return lax.dot_general(left, right, (dims, ((), ())), preferred_element_type=F32)


NN = ((1,), (0,))
NT = ((1,), (1,))
TN = ((0,), (0,))


def cost(micros):
    return pl.CostEstimate(
        flops=int(micros * 1.15e9), bytes_accessed=int(micros * 3.6e6), transcendentals=0
    )


def slot_rows(place_ref, slot, half, rows):
    return pl.ds(pl.multiple_of((place_ref[2 + slot] * 2 + half) * rows, rows), rows)


def load_halves(place_ref, mine_ref, other_ref, whole_ref, low=0):
    core = place_ref[1]
    slots, rows = mine_ref.shape[0], mine_ref.shape[1]
    packed = mine_ref.shape[2] == 2 * whole_ref.shape[1]
    for slot in range(slots):
        for ref, half in ((mine_ref, core), (other_ref, 1 - core)):
            target = slot_rows(place_ref, low + slot, half, 2 * rows if packed else rows)
            whole_ref[target, :] = unpack(ref[slot]) if packed else ref[slot]


def store_halves(place_ref, whole_ref, mine_ref, other_ref, columns):
    core = place_ref[1]
    slots, rows = mine_ref.shape[0], mine_ref.shape[1]
    packed = mine_ref.shape[2] == 2 * whole_ref.shape[1]
    for slot in range(slots):
        for ref, half in ((mine_ref, core), (other_ref, 1 - core)):
            if packed:
                ref[slot] = pack(whole_ref[slot_rows(place_ref, slot, half, 2 * rows), :])
            else:
                ref[slot, :, columns] = whole_ref[slot_rows(place_ref, slot, half, rows), columns]


def load_pieces(place_ref, mine_refs, other_refs, whole_ref):
    for index, (mine_ref, other_ref) in enumerate(zip(mine_refs, other_refs)):
        low = mine_refs[3].shape[0] if index == 4 else 0
        load_halves(place_ref, mine_ref, other_ref, whole_ref.at[min(index, 3)], low)


def pack(block):
    half = block.shape[0] // 2
    return jnp.concatenate([block[:half], block[half:]], 1)


def unpack(block):
    half = block.shape[1] // 2
    return jnp.concatenate([block[:, :half], block[:, half:]], 0)


SCALARS = pl.BlockSpec(memory_space=pltpu.SMEM)
WHOLE = pl.BlockSpec(memory_space=pltpu.VMEM)


def window_start(block_id, rows, span):
    if span == rows:
        return 0
    start = jnp.clip(block_id * BLOCK - WINDOW // 2, 0, rows - span)
    return pl.multiple_of(start, WINDOW // 2)


def key_mask(start, span, first, last):
    keys = start + lax.broadcasted_iota(jnp.int32, (span, BLOCK), 0)
    return (keys >= first) & (keys < last)


def stack_kernel(split, block0_ref, block1_ref, block2_ref, block3_ref, upper_ref, lower_ref):
    for slot, ref in enumerate((block0_ref, block1_ref, block2_ref, block3_ref)):
        upper_ref[slot] = ref[:split]
        lower_ref[slot] = ref[split:]


def stack_blocks(blocks, split):
    rows, columns = blocks[0].shape
    return pl.pallas_call(
        functools.partial(stack_kernel, split),
        out_shape=(
            jax.ShapeDtypeStruct((4, split, columns), BF16),
            jax.ShapeDtypeStruct((4, rows - split, columns), BF16),
        ),
        in_specs=[WHOLE] * 4,
        compiler_params=pltpu.CompilerParams(vmem_limit_bytes=VMEM_BYTES),
        cost_estimate=cost(2),
        name="stack_blocks",
    )(*blocks)


def attend_kernel(
    span, place_ref, own_ref, one_ref, two_ref, head_ref, tail_ref, mine_ref, other_ref,
    cos_ref, sin_ref, first_ref, last_ref,
    mixed0_ref, mixed1_ref, mixed2_ref, mixed3_ref, queries_ref, keys_ref, values_ref, mass_ref,
    normed_ref, qkv_ref, outs_ref, key_rows, value_rows, proj, mixed_rows, bias, scores,
):
    width, rows = queries_ref.shape
    heads = width // HEAD_DIM
    half = HEAD_DIM // 2
    local = rows // 4
    me = place_ref[0]
    load_halves(place_ref, mine_ref, other_ref, qkv_ref)
    pieces = (
        (own_ref, 0, 0), (one_ref, 1, 0), (two_ref, 2, 0), (head_ref, 3, 0), (tail_ref, 3, local // 2)
    )
    for ref, bit, shift in pieces:
        low = pl.multiple_of((me ^ bit) * local + shift, local // 2)
        normed_ref[pl.ds(low, ref.shape[0]), :] = ref[...]
    proj[...] = dot(qkv_ref[...].T, normed_ref[...], NT)
    cosines, sines = cos_ref[...], sin_ref[...]
    for head in range(heads):
        low = head * HEAD_DIM
        for part, ref in ((0, queries_ref), (1, keys_ref)):
            upper = proj[part * width + low : part * width + low + half, :]
            lower = proj[part * width + low + half : part * width + low + HEAD_DIM, :]
            turned = jnp.concatenate(
                [upper * cosines - lower * sines, lower * cosines + upper * sines], 0
            )
            ref[low : low + HEAD_DIM, :] = turned.astype(BF16)
            if part == 1:
                key_rows[head] = turned.T.astype(BF16)
        value = proj[2 * width + low : 2 * width + low + HEAD_DIM, :]
        values_ref[low : low + HEAD_DIM, :] = value.astype(BF16)
        value_rows[head] = value.T.astype(BF16)
    mass_ref[...] = jnp.zeros_like(mass_ref)

    def block(block_id, carry):
        start = window_start(block_id, rows, span)
        columns = pl.ds(pl.multiple_of(block_id * BLOCK, BLOCK), BLOCK)
        mask = key_mask(start, span, first_ref[:, columns], last_ref[:, columns])
        bias[...] = jnp.where(mask, 0.0, -1e30)
        outs = []
        for head in range(heads):
            low = head * HEAD_DIM
            query = queries_ref[low : low + HEAD_DIM, columns] * BF16(HEAD_DIM**-0.5)
            top = jnp.full((1, BLOCK), -2e30, F32)
            for part in range(0, span, CHUNK):
                key = key_rows[head, pl.ds(start + part, CHUNK), :]
                score = dot(key, query, NN) + bias[part : part + CHUNK]
                scores[part : part + CHUNK] = score
                top = jnp.maximum(top, jnp.max(score, axis=0, keepdims=True))
            total = jnp.zeros((1, BLOCK), F32)
            out = jnp.zeros((HEAD_DIM, BLOCK), F32)
            for part in range(0, span, CHUNK):
                expos = jnp.exp(scores[part : part + CHUNK] - top)
                total += jnp.sum(expos, axis=0, keepdims=True)
                if span == rows:
                    value = values_ref[low : low + HEAD_DIM, part : part + CHUNK]
                else:
                    value = value_rows[head, pl.ds(start + part, CHUNK), :].T
                out += dot(value, expos.astype(BF16), NN)
            outs.append(out * (1.0 / total))
            mass_ref[head : head + 1, columns] = top + jnp.log(total)
        outs_ref[:, columns] = jnp.concatenate(outs, 0)
        mixed_rows[columns, :] = jnp.concatenate(outs, 0).T.astype(BF16)
        return carry

    lax.fori_loop(0, rows // BLOCK, block, 0)
    for bit, ref in enumerate((mixed0_ref, mixed1_ref, mixed2_ref, mixed3_ref)):
        low = pl.multiple_of((me ^ bit) * local, local)
        ref[...] = pack(mixed_rows[pl.ds(low, local), :])


def attend(place, pieces, mine, other, width, cosines, sines, first, last, is_local):
    local, model = pieces[0].shape
    rows = 4 * local
    heads = width // HEAD_DIM
    span = min(rows, BLOCK + WINDOW) if is_local else rows
    shape = jax.ShapeDtypeStruct((width, rows), BF16)
    mixed = jax.ShapeDtypeStruct((local // 2, 2 * width), BF16)
    return pl.pallas_call(
        functools.partial(attend_kernel, span),
        out_shape=(
            mixed, mixed, mixed, mixed, shape, shape, shape, jax.ShapeDtypeStruct((8, rows), F32),
            jax.ShapeDtypeStruct((rows, model), BF16),
            jax.ShapeDtypeStruct((model, 3 * width), BF16),
            jax.ShapeDtypeStruct((width, rows), F32),
        ),
        in_specs=[SCALARS] + [WHOLE] * 11,
        scratch_shapes=[
            pltpu.VMEM((heads, rows, HEAD_DIM), BF16),
            pltpu.VMEM((heads, rows, HEAD_DIM), BF16),
            pltpu.VMEM((3 * width, rows), F32),
            pltpu.VMEM((rows, width), BF16),
            pltpu.VMEM((span, BLOCK), F32),
            pltpu.VMEM((span, BLOCK), F32),
        ],
        compiler_params=pltpu.CompilerParams(vmem_limit_bytes=VMEM_BYTES),
        cost_estimate=cost(11 if is_local else 20),
        name="attend_local" if is_local else "attend_global",
    )(place, *pieces, mine, other, cosines, sines, first, last)


def attend_back_kernel(
    span, place_ref, queries_ref, keys_ref, values_ref, mass_ref,
    grad0_ref, grad1_ref, grad2_ref, grad3_ref,
    cos_ref, sin_ref, first_ref, last_ref, qkv_ref, outs_ref,
    own_ref, one0_ref, one1_ref, two0_ref, two1_ref, far0_ref, far1_ref, out_ref,
    query_rows, key_rows, value_rows, grad_cols, grad_all, grad_rows, sum_q, sum_k, sum_v, flat, bias,
    probs_low, scores_low,
):
    width, rows = queries_ref.shape
    heads = width // HEAD_DIM
    half = HEAD_DIM // 2
    local = rows // 4
    scale = HEAD_DIM**-0.5
    me = place_ref[0]
    for bit, ref in enumerate((grad0_ref, grad1_ref, grad2_ref, grad3_ref)):
        low = pl.multiple_of((me ^ bit) * local, local)
        grad_all[pl.ds(low, local), :] = unpack(ref[...])
    grad_cols[...] = grad_all[...].T
    for head in range(heads):
        cut = slice(head * HEAD_DIM, (head + 1) * HEAD_DIM)
        query_rows[head] = (queries_ref[cut, :] * BF16(scale)).T
        key_rows[head] = keys_ref[cut, :].T
        value_rows[head] = values_ref[cut, :].T
        grad_rows[head] = grad_all[:, cut]
    sum_k[...] = jnp.zeros_like(sum_k)
    sum_v[...] = jnp.zeros_like(sum_v)

    def block(block_id, carry):
        start = window_start(block_id, rows, span)
        columns = pl.ds(pl.multiple_of(block_id * BLOCK, BLOCK), BLOCK)
        mask = key_mask(start, span, first_ref[:, columns], last_ref[:, columns])
        bias[...] = jnp.where(mask, 0.0, -1e30)
        for head in range(heads):
            cut = slice(head * HEAD_DIM, (head + 1) * HEAD_DIM)
            query = queries_ref[cut, columns] * BF16(scale)
            grad = grad_cols[cut, columns]
            mass = mass_ref[head : head + 1, columns]
            inner = jnp.sum(grad.astype(F32) * outs_ref[cut, columns], axis=0, keepdims=True)
            for part in range(0, span, CHUNK):
                window = pl.ds(start + part, CHUNK)
                scores = dot(key_rows[head, window, :], query, NN)
                probs = jnp.exp(scores - mass + bias[part : part + CHUNK])
                grad_probs = dot(value_rows[head, window, :], grad, NN)
                probs_low[part : part + CHUNK] = probs.astype(BF16)
                scores_low[part : part + CHUNK] = (probs * (grad_probs - inner)).astype(BF16)
            window = pl.ds(start, span)
            key_cols = keys_ref[cut, :] if span == rows else key_rows[head, window, :].T
            sum_v[head, window, :] += dot(probs_low[...], grad_rows[head, columns, :], NN)
            sum_k[head, window, :] += dot(scores_low[...], query_rows[head, columns, :], NN)
            sum_q[cut, columns] = dot(key_cols, scores_low[...], NN)
        return carry

    lax.fori_loop(0, rows // BLOCK, block, 0)
    cosines, sines = cos_ref[...], sin_ref[...]
    for head in range(heads):
        low = head * HEAD_DIM
        turned_q = sum_q[low : low + HEAD_DIM, :] * scale
        for part, turned in ((0, turned_q), (1, sum_k[head].T)):
            upper, lower = turned[:half], turned[half:]
            raw = jnp.concatenate(
                [upper * cosines + lower * sines, lower * cosines - upper * sines], 0
            )
            flat[part * width + low : part * width + low + HEAD_DIM, :] = raw.astype(BF16)
        flat[2 * width + low : 2 * width + low + HEAD_DIM, :] = sum_v[head].T.astype(BF16)
    out_ref[...] = flat[...].T
    targets = ((own_ref,), (one0_ref, one1_ref), (two0_ref, two1_ref), (far0_ref, far1_ref))
    for bit, refs in enumerate(targets):
        low = pl.multiple_of((me ^ bit) * local, local)
        part = dot(out_ref[pl.ds(low, local), :], qkv_ref[...], NT).astype(BF16)
        size = local // len(refs)
        for index, ref in enumerate(refs):
            ref[...] = part[index * size : (index + 1) * size]


def attend_back(
    place, queries, keys, values, mass, grads, cosines, sines, first, last, qkv, outs, is_local
):
    width, rows = queries.shape
    model = qkv.shape[0]
    heads = width // HEAD_DIM
    span = min(rows, BLOCK + WINDOW) if is_local else rows
    low_rows = pltpu.VMEM((heads, rows, HEAD_DIM), BF16)
    sums = pltpu.VMEM((heads, rows, HEAD_DIM), F32)
    part = jax.ShapeDtypeStruct((rows // 4, model), BF16)
    half = jax.ShapeDtypeStruct((rows // 8, model), BF16)
    return pl.pallas_call(
        functools.partial(attend_back_kernel, span),
        out_shape=(part,) + (half,) * 6 + (jax.ShapeDtypeStruct((rows, 3 * width), BF16),),
        in_specs=[SCALARS] + [WHOLE] * 14,
        scratch_shapes=[
            low_rows, low_rows, low_rows, pltpu.VMEM((width, rows), BF16),
            pltpu.VMEM((rows, width), BF16), low_rows,
            pltpu.VMEM((width, rows), F32), sums, sums, pltpu.VMEM((3 * width, rows), BF16),
            pltpu.VMEM((span, BLOCK), F32), pltpu.VMEM((span, BLOCK), BF16),
            pltpu.VMEM((span, BLOCK), BF16),
        ],
        compiler_params=pltpu.CompilerParams(vmem_limit_bytes=VMEM_BYTES),
        cost_estimate=cost(11 if is_local else 21),
        name="attend_back_local" if is_local else "attend_back_global",
    )(place, queries, keys, values, mass, *grads, cosines, sines, first, last, qkv, outs)


def qkv_grad_kernel(place_ref, normed_ref, grad_ref, qkv_ref, mine_ref, other_ref, gain_ref, whole):
    grad = dot(normed_ref[...].T, grad_ref[...], NN)
    gain_ref[...] = jnp.sum(grad * qkv_ref[...].astype(F32), axis=1, keepdims=True)
    whole[...] = grad.astype(BF16)
    store_halves(place_ref, whole, mine_ref, other_ref, slice(None))


def qkv_grad(place, normed, grad, qkv, shape):
    part = jax.ShapeDtypeStruct(shape, BF16)
    return pl.pallas_call(
        qkv_grad_kernel,
        out_shape=(part, part, jax.ShapeDtypeStruct((qkv.shape[0], 1), F32)),
        in_specs=[SCALARS, WHOLE, WHOLE, WHOLE],
        scratch_shapes=[pltpu.VMEM((normed.shape[1], grad.shape[1]), BF16)],
        compiler_params=pltpu.CompilerParams(vmem_limit_bytes=VMEM_BYTES),
        cost_estimate=cost(4),
        name="qkv_grad",
    )(place, normed, grad, qkv)


def erf_parts(gate):
    cumulative = 0.5 * (1.0 + lax.erf(gate * 0.7071067811865476))
    density = 0.3989422804014327 * jnp.exp(-0.5 * gate * gate)
    return cumulative, density


def forward_step(pair, mixed_refs, in_ref, gain_ref, mid_ref, sums, mats):
    parts = mats.shape[0]
    width = mixed_refs[0].shape[1] // 2
    units = pair // 2
    mid = in_ref[...].astype(F32)
    for part, ref in enumerate(mixed_refs):
        mid += dot(unpack(ref[...]), mats[part, :, pair : pair + width], NT)
    mid_ref[...] = mid
    sums[...] = mid
    normed = (norm_parts(mid)[0] * gain_ref[...]).astype(BF16)

    def feed(part, carry):
        gate_up = dot(normed, mats[part, :, :pair], NN)
        gate = gate_up[:, :units]
        hidden = (gate * erf_parts(gate)[0] * gate_up[:, units:]).astype(BF16)
        sums[...] += dot(hidden, mats[part, :, pair + width : pair + width + units], NT)
        return carry

    lax.fori_loop(0, parts, feed, 0)


def token_kernel(pair, place_ref, mixed0_ref, mixed1_ref, mixed2_ref, mixed3_ref, in_ref, *refs):
    pieces = (len(refs) - 7) // 2
    mine_refs, other_refs = refs[:pieces], refs[pieces : 2 * pieces]
    gain_ref, next_ref, mid_ref, out_ref, normed_ref, sums, mats = refs[2 * pieces :]
    load_pieces(place_ref, mine_refs, other_refs, mats)
    mixed_refs = (mixed0_ref, mixed1_ref, mixed2_ref, mixed3_ref)
    forward_step(pair, mixed_refs, in_ref, gain_ref, mid_ref, sums, mats)
    low = sums[...].astype(BF16)
    out_ref[...] = low
    normed_ref[...] = (norm_parts(low.astype(F32))[0] * next_ref[...]).astype(BF16)


def token_forward(place, mixed, layer_in, mine, other, gain, next_gain, pair):
    shape = layer_in.shape
    return pl.pallas_call(
        functools.partial(token_kernel, pair),
        out_shape=(
            jax.ShapeDtypeStruct(shape, F32),
            jax.ShapeDtypeStruct(shape, BF16),
            jax.ShapeDtypeStruct(shape, BF16),
        ),
        in_specs=[SCALARS] + [WHOLE] * (7 + 2 * len(mine)),
        scratch_shapes=[
            pltpu.VMEM(shape, F32),
            pltpu.VMEM((4, shape[1], mine[0].shape[2]), BF16),
        ],
        compiler_params=pltpu.CompilerParams(vmem_limit_bytes=VMEM_BYTES),
        cost_estimate=cost(10),
        name="token_forward",
    )(place, *mixed, layer_in, *mine, *other, gain, next_gain)


def token_back_kernel(
    pair, place_ref, grad_ref, mid_ref, mixed0_ref, mixed1_ref, mixed2_ref, mixed3_ref, *refs
):
    pieces = (len(refs) - 12) // 2
    mats = refs[-2]
    load_pieces(place_ref, refs[:pieces], refs[pieces : 2 * pieces], mats)
    mixed_refs = (mixed0_ref, mixed1_ref, mixed2_ref, mixed3_ref)
    back_step(pair, place_ref, grad_ref, mid_ref, mixed_refs, *refs[2 * pieces :])


def token_last_kernel(
    pair, place_ref, grad_ref, in_ref, mixed0_ref, mixed1_ref, mixed2_ref, mixed3_ref, *refs
):
    pieces = (len(refs) - 14) // 2
    mats, sums = refs[-3], refs[-4]
    load_pieces(place_ref, refs[:pieces], refs[pieces : 2 * pieces], mats)
    mixed_refs = (mixed0_ref, mixed1_ref, mixed2_ref, mixed3_ref)
    rest = refs[2 * pieces :]
    gain_ref, out_ref, mid = rest[0], rest[9], rest[13]
    forward_step(pair, mixed_refs, in_ref, gain_ref, mid, sums, mats)
    out_ref[...] = sums[...].astype(BF16)
    back_step(pair, place_ref, grad_ref, mid, mixed_refs, *rest[:9], *rest[10:13])


def back_step(
    pair, place_ref, grad_ref, mid_ref, mixed_refs, gain_ref, mine_grad_ref, other_grad_ref,
    mixed_grad0_ref, mixed_grad1_ref, mixed_grad2_ref, mixed_grad3_ref, grad_mid_ref,
    gain_grad_ref, sums, mats, grads,
):
    parts = mats.shape[0]
    width = mixed_refs[0].shape[1] // 2
    units = pair // 2
    grad = grad_ref[...].astype(F32)
    grad_low = grad.astype(BF16)
    grad_flip = grad.T.astype(BF16)
    unit, scale = norm_parts(mid_ref[...])
    gained = unit * gain_ref[...]
    normed = gained.astype(BF16)
    normed_flip = gained.T.astype(BF16)
    sums[...] = jnp.zeros_like(sums)
    used = pair + width + units
    grads[:, used:] = jnp.zeros((grads.shape[0], grads.shape[1] - used), BF16)

    def feed(part, carry):
        gate_up = dot(normed, mats[part, :, :pair], NN)
        gate, up = gate_up[:, :units], gate_up[:, units:]
        cumulative, density = erf_parts(gate)
        gelu = gate * cumulative
        hidden = (gelu * up).astype(BF16)
        grad_hidden = dot(grad_low, mats[part, :, pair + width : pair + width + units], NN)
        grad_gate = grad_hidden * up * (cumulative + gate * density)
        grad_up = grad_hidden * gelu
        grad_pair = jnp.concatenate([grad_gate, grad_up], 1).astype(BF16)
        grads[:, pair + width : used] = dot(grad_flip, hidden, NN).astype(BF16)
        grads[:, :pair] = dot(normed_flip, grad_pair, NN).astype(BF16)
        for columns in (slice(0, pair), slice(pair + width, None)):
            store_halves(
                place_ref, grads, mine_grad_ref.at[part], other_grad_ref.at[part], columns
            )
        sums[...] += dot(grad_pair, mats[part, :, :pair], NT)
        return carry

    lax.fori_loop(0, parts, feed, 0)
    grad_normed = sums[...]
    gain_grad_ref[...] = jnp.sum(grad_normed * unit, axis=0, keepdims=True)
    grad_mid = grad + norm_back(grad_normed, unit, scale, gain_ref[...])
    grad_mid_ref[...] = grad_mid
    mid_low = grad_mid.astype(BF16)
    mid_flip = grad_mid.T.astype(BF16)
    mixed_grad_refs = (mixed_grad0_ref, mixed_grad1_ref, mixed_grad2_ref, mixed_grad3_ref)
    for part in range(parts):
        weight = mats[part, :, pair : pair + width]
        mixed_grad_refs[part][...] = pack(dot(mid_low, weight, NN).astype(BF16))
        grads[:, pair : pair + width] = dot(mid_flip, unpack(mixed_refs[part][...]), NN).astype(BF16)
        store_halves(
            place_ref, grads, mine_grad_ref.at[part], other_grad_ref.at[part],
            slice(pair, pair + width),
        )


def token_back(place, grad, mid, mixed, mine, other, gain, pair):
    shape = mine[0].shape
    half = jax.ShapeDtypeStruct((4,) + shape, BF16)
    mixed_grad = jax.ShapeDtypeStruct(mixed[0].shape, BF16)
    return pl.pallas_call(
        functools.partial(token_back_kernel, pair),
        out_shape=(
            half, half, mixed_grad, mixed_grad, mixed_grad, mixed_grad,
            jax.ShapeDtypeStruct(mid.shape, F32),
            jax.ShapeDtypeStruct((1, mid.shape[1]), F32),
        ),
        in_specs=[SCALARS] + [WHOLE] * (7 + 2 * len(mine)),
        scratch_shapes=[
            pltpu.VMEM(mid.shape, F32),
            pltpu.VMEM((4, mid.shape[1], shape[2]), BF16),
            pltpu.VMEM((mid.shape[1], shape[2]), BF16),
        ],
        compiler_params=pltpu.CompilerParams(vmem_limit_bytes=VMEM_BYTES),
        cost_estimate=cost(20),
        name="token_back",
    )(place, grad, mid, *mixed, *mine, *other, gain)


def token_last(place, grad, layer_in, mixed, mine, other, gain, pair):
    shape, rows = mine[0].shape, layer_in.shape
    half = jax.ShapeDtypeStruct((4,) + shape, BF16)
    mixed_grad = jax.ShapeDtypeStruct(mixed[0].shape, BF16)
    return pl.pallas_call(
        functools.partial(token_last_kernel, pair),
        out_shape=(
            half, half, mixed_grad, mixed_grad, mixed_grad, mixed_grad,
            jax.ShapeDtypeStruct(rows, F32),
            jax.ShapeDtypeStruct((1, rows[1]), F32),
            jax.ShapeDtypeStruct(rows, BF16),
        ),
        in_specs=[SCALARS] + [WHOLE] * (7 + 2 * len(mine)),
        scratch_shapes=[
            pltpu.VMEM(rows, F32),
            pltpu.VMEM((4, rows[1], shape[2]), BF16),
            pltpu.VMEM((rows[1], shape[2]), BF16),
            pltpu.VMEM(rows, F32),
        ],
        compiler_params=pltpu.CompilerParams(vmem_limit_bytes=VMEM_BYTES),
        cost_estimate=cost(20),
        name="token_last",
    )(place, grad, layer_in, *mixed, *mine, *other, gain)


def frequencies(theta_base, half_dim):
    return theta_base ** (-(jnp.arange(half_dim, dtype=F32) * 2.0) / (2.0 * half_dim))


def sequences(seq_lengths, rows):
    seq_ends = jnp.cumsum(seq_lengths)
    positions = jnp.arange(rows, dtype=jnp.int32)
    seq_of = jnp.sum((positions[:, None] >= seq_ends[None, :]).astype(jnp.int32), axis=1)
    matches = jnp.arange(seq_lengths.shape[0], dtype=jnp.int32)[None, :] == seq_of[:, None]
    last = jnp.sum(jnp.where(matches, seq_ends[None, :], 0), axis=1)
    first = jnp.sum(jnp.where(matches, (seq_ends - seq_lengths)[None, :], 0), axis=1)
    return first[None], last[None], positions[None]


def body(
    tokens, lengths, qkv_weight, out_weight, gate_up_weight, down_weight, gains, out_cotangent
):
    core = lax.axis_index("pipe")
    model = tokens.shape[-1]
    local_rows = tokens.shape[2]
    rows = 4 * local_rows
    shard_rows = qkv_weight.shape[1]
    width = qkv_weight.shape[3]
    pair = 2 * gate_up_weight.shape[3]

    stream = take(tokens[0], core)
    cotangent = take(out_cotangent[0], core)
    first, last, positions = sequences(take(lengths[0], core), rows)
    bounds = (
        (jnp.maximum(first, positions - WINDOW // 2), jnp.minimum(last, positions + WINDOW // 2 + 1)),
        (first, last),
    )
    tables = []
    for base in (10000.0, 160000.0):
        turns = frequencies(base, HEAD_DIM // 2)[:, None] * (positions - first).astype(F32)
        tables.append((jnp.cos(turns), jnp.sin(turns)))

    other_gains = swap_cores(gains[0])
    gain_rows = (
        jnp.where(core == 0, gains[0], other_gains)[None],
        jnp.where(core == 0, other_gains, gains[0])[None],
    )
    place = placement()

    normed = (norm_parts(stream.astype(F32))[0] * gain_rows[0][:, :model]).astype(BF16)
    mats = jnp.concatenate(
        [gate_up_weight[0].reshape(shard_rows, pair), out_weight[0].T, down_weight[0].T], 1
    )
    spare = 6 * width - mats.shape[1]
    mats = jnp.pad(mats, ((0, 0), (0, spare))).reshape(2, shard_rows // 2, 6 * width)
    qkv = qkv_weight[0].reshape(2, 2, shard_rows // 4, 3 * width)
    qkv = jnp.concatenate([qkv[:, 0], qkv[:, 1]], -1)
    first_half, second_half = layer_halves(
        jnp.concatenate([mats, qkv], 1).reshape(-1, 6 * width)
    )
    split = shard_rows // 2
    total = first_half.shape[0]
    qkv_shape = (4, split // 2, 6 * width) if four_dp() else (1, model // 2, 3 * width)

    def split_blocks(blocks):
        if four_dp():
            upper, lower = stack_blocks(blocks, split)
            return upper, halves(lower)
        upper, lower = blocks[0][:, :split], blocks[0][:, split:]
        lower = jnp.concatenate([lower[..., : 3 * width], lower[..., 3 * width :]], 1)
        return upper, halves(lower)

    normed, first_half, second_half = after((normed, first_half, second_half))
    near, blocks = to_neighbours(normed), gather_dp(first_half)
    far = to_far(*after(near))
    far, blocks = after((far, blocks))
    mats_first, qkv_first = split_blocks(blocks)
    mats_first, second_half = after((mats_first, second_half), qkv_first)
    pieces = (normed,) + near + far
    saved_attend = [None, None]
    saved_token = [None, None]

    mats_near = to_neighbours(mats_first)
    second_blocks = gather_dp(second_half)
    second_blocks, second_late = second_blocks[:3], second_blocks[3:]
    *mixed, queries, keys, values, mass, normed_full, qkv, outs = attend(
        place, pieces, *qkv_first, width, *tables[0], *bounds[0], True
    )
    saved_attend[0] = (queries, keys, values, mass, normed_full, qkv, outs)
    mixed, mats_first, mats_near, second_blocks = after(
        (mixed, mats_first, mats_near, second_blocks)
    )
    mixed, mats_far = after((swap_tensor(mixed), to_far(*mats_near)))
    mats = piece_halves((mats_first,) + mats_near + mats_far)
    mid, first_out, normed = token_forward(
        place, mixed, stream, *mats, gain_rows[0][:, model:], gain_rows[1][:, :model], pair
    )
    saved_token[0] = (mid, mixed) + mats

    near, second_late = after((to_neighbours(normed), second_late))
    blocks = second_blocks + second_late
    mats_second, qkv_second = split_blocks(blocks)
    far, qkv_second = after((to_far(*near), qkv_second))
    pieces = (normed,) + near + far
    mats_second = after(mats_second, far)
    second_near = to_neighbours(mats_second)
    *mixed, queries, keys, values, mass, normed_full, qkv, outs = attend(
        place, pieces, *qkv_second, width, *tables[1], *bounds[1], False
    )
    saved_attend[1] = (queries, keys, values, mass, normed_full, qkv, outs)
    mixed, second_near = after((mixed, second_near))
    mixed, second_far = after((swap_tensor(mixed), to_far(*second_near)))
    mats = piece_halves((mats_second,) + second_near + second_far)
    def token_step(layer, grad):
        mid, mixed, mine, other = saved_token[layer]
        return token_back(
            place, grad, mid, mixed, mine, other, gain_rows[layer][:, model:], pair
        )

    def attend_step(layer, mixed_grad):
        queries, keys, values, mass, _, qkv, outs = saved_attend[layer]
        return attend_back(
            place, queries, keys, values, mass, mixed_grad, *tables[layer], *bounds[layer],
            qkv, outs, layer == 0,
        )

    def weight_step(layer, grad_projected):
        normed_full, qkv = saved_attend[layer][4:6]
        mine, other, gain_sum = qkv_grad(
            place, normed_full, grad_projected, qkv, qkv_shape
        )
        return half_sums(mine, other) + (gain_sum.reshape(1, model) / gain_rows[layer][:, :model],)

    def norm_step(layer, grad_normed, grad_mid):
        unit, scale = norm_parts((stream, first_out)[layer].astype(F32))
        return grad_mid + norm_back(grad_normed, unit, scale, gain_rows[layer][:, :model])

    def qkv_blocks(kept, came):
        return [add_low(kept[slot], came[slot]) for slot in range(kept.shape[0])]

    mine_grad, other_grad, *mixed_grad, grad_mid, gain_mlp, second_out = token_last(
        place, cotangent, first_out, mixed, *mats, gain_rows[1][:, model:], pair
    )
    mixed_grad = swap_tensor(mixed_grad)
    kept, came = half_sums(mine_grad, other_grad)
    mixed_grad, kept, came = after((mixed_grad, kept, came))
    far = far_terms(add_low(kept[3], came[3]))
    *parts, grad_projected = attend_step(1, mixed_grad)
    parts, grad_projected, far = after((parts, grad_projected, far))
    early = rows_early(parts)
    pair_terms = near_terms(add_low(kept[1], came[1]), add_low(kept[2], came[2]), *far)
    qkv_kept, qkv_came, gain_attn = weight_step(1, grad_projected)
    second_gain = jnp.concatenate([gain_attn, gain_mlp], 1)
    late = rows_late(parts, early)
    late, pair_terms, qkv_kept, qkv_came = after((late, pair_terms, qkv_kept, qkv_came), early)
    near = to_near(pair_terms)
    grad = norm_step(1, rows_sum(parts, early, late), grad_mid).astype(BF16)
    second_grad = grad.astype(F32)

    second_kept, second_came, second_qkv = kept, came, qkv_blocks(qkv_kept, qkv_came)
    mine_grad, other_grad, *mixed_grad, grad_mid, gain_mlp = token_step(0, grad)
    mixed_grad, other_grad, near = after((mixed_grad, other_grad, near))
    mixed_grad = swap_tensor(mixed_grad)
    kept, came = half_sums(mine_grad, other_grad)
    second = slot_sums(second_kept, second_came, near)
    if four_dp():
        second = [jnp.concatenate(block, 0) for block in zip(second, second_qkv)]
    mixed_grad, kept, came, second = after((mixed_grad, kept, came, second))
    far = far_terms(add_low(kept[3], came[3]))
    came_early = scatter_dp(second, (1, 2))
    *parts, grad_projected = attend_step(0, mixed_grad)
    parts, grad_projected, far, kept, came, came_early, second = after(
        (parts, grad_projected, far, kept, came, came_early, second)
    )

    pair_terms = near_terms(add_low(kept[1], came[1]), add_low(kept[2], came[2]), *far)
    pair_terms, grad_projected = after((pair_terms, grad_projected))
    near, came_late = to_near(pair_terms), scatter_dp(second, (3,))
    qkv_kept, qkv_came, gain_attn = weight_step(0, grad_projected)
    first_gain = jnp.concatenate([gain_attn, gain_mlp], 1)
    gain_sum = jnp.where(core == 0, first_gain, second_gain)
    gain_sum += swap_cores(jnp.where(core == 0, second_gain, first_gain))
    first_qkv = qkv_blocks(qkv_kept, qkv_came)
    near, came_late, parts, gain_sum, first_qkv = after(
        (near, came_late, parts, gain_sum, first_qkv)
    )
    second_came = came_early + came_late
    first = slot_sums(kept, came, near)
    if four_dp():
        first = [jnp.concatenate(block, 0) for block in zip(first, first_qkv)]
    first_came = scatter_dp(first)
    gain_sum += to_mate(gain_sum, 1)
    rows_far = (to_mate(parts[5], 1), to_mate(parts[6], 2))
    rows_far, parts, gain_sum = after((rows_far, parts, gain_sum))
    rows_near = to_near(
        (
            jnp.concatenate([parts[1], add_low(parts[2], rows_far[1])], 0),
            jnp.concatenate([add_low(parts[3], rows_far[0]), parts[4]], 0),
        )
    )
    gain_sum += to_mate(gain_sum, 2)
    gain_sum, first_came = after((gain_sum, first_came))
    chunk = model * 2 // (4 * lax.axis_size("dp"))
    me = lax.axis_index("dp") * 4 + lax.axis_index("tensor")
    if four_dp():
        rank = lax.axis_index("dp")
        chunks = take(jnp.swapaxes(gain_sum.reshape(4, 4, chunk), 0, 1), lax.axis_index("tensor"))
        gain_part = take(chunks, rank)
        for bit in (1, 2, 3):
            gain_part += to_peer(take(chunks, rank ^ bit), bit)
    else:
        gain_sum = lax.psum(gain_sum, "dp")
        gain_part = lax.dynamic_slice_in_dim(gain_sum[0], me * chunk, chunk, 0)
    first_grad = norm_step(0, add_up(parts[0], *rows_near), grad_mid)
    input_grads = (first_grad, second_grad)

    if four_dp():
        total_grad = own_layer(scatter_sum(first, first_came), scatter_sum(second, second_came))
        total_grad = total_grad.reshape(2, total, 6 * width)
        mats_total = total_grad[:, :split].reshape(shard_rows, 6 * width)
        qkv_total = total_grad[:, split:].reshape(-1, 6 * width)
    else:
        mats_total = own_layer(scatter_sum(first, ()), scatter_sum(second, ()))
        qkv_total = own_layer(scatter_sum(first_qkv, ()), scatter_sum(second_qkv, ()))
    if four_dp():
        qkv_total = qkv_total.reshape(2, shard_rows // 4, 2, 3 * width)
        qkv_total = jnp.moveaxis(qkv_total, 2, 1).reshape(shard_rows, 3 * width)

    activations = join_halves(
        jnp.where(core == 0, first_out, second_out),
        swap_cores(jnp.where(core == 0, second_out, first_out)),
        0,
    )
    grads_in = join_halves(
        jnp.where(core == 0, input_grads[0], input_grads[1]),
        swap_cores(jnp.where(core == 0, input_grads[1], input_grads[0]).astype(BF16)).astype(F32),
        0,
    )
    return (
        activations[None, None],
        grads_in[None, None],
        qkv_total.reshape(qkv_weight.shape),
        mats_total[:, pair : pair + width].T[None],
        mats_total[:, :pair].reshape(gate_up_weight.shape),
        mats_total[:, pair + width : pair + width + pair // 2].T[None],
        gain_part[None],
    )


def solution(mesh):
    return jax.shard_map(
        body,
        mesh=mesh,
        in_specs=(
            P("dp", None, "tensor", None),
            P("dp", None, None),
            P("pipe", "dp", None, "tensor"),
            P("pipe", "tensor", "dp"),
            P("pipe", "dp", None, "tensor"),
            P("pipe", "tensor", "dp"),
            P("pipe", None),
            P("dp", None, "tensor", None),
        ),
        out_specs=(
            P("pipe", "dp", None, "tensor", None),
            P("pipe", "dp", None, "tensor", None),
            P("pipe", "dp", None, "tensor"),
            P("pipe", "tensor", "dp"),
            P("pipe", "dp", None, "tensor"),
            P("pipe", "tensor", "dp"),
            P("pipe", ("dp", "tensor")),
        ),
        check_vma=False,
    )
```
